256 devices in a mesh: ta: 4 (over y_hi, core), ha: 8 (over z), wa: 8 (over y_lo, x).
Axes of the slice: x: 4, y: 4 (y_hi: 2, y_lo: 2; y = y_hi * 2 + y_lo), z: 8, core: 2. Of those that a mesh axis runs over, the one named last changes fastest.
Arguments:
- coarse: bfloat16 [8, 128, 64, 256], P('ta', 'ha', 'wa'), may hold values from -20 to 20
- cache_coarse: bfloat16 [2, 128, 64, 256], P(None, 'ha', 'wa'), may hold values from -6 to 6
- cache_middle: bfloat16 [2, 128, 64, 256], P(None, 'ha', 'wa'), may hold values from -6 to 6
- cache_fine: bfloat16 [2, 256, 128, 256], P(None, 'ha', 'wa'), may hold values from -6 to 6
- coarse_gain: float32 [256], replicated, may hold values from 0.25 to 1.75
- coarse_shift: float32 [256], replicated, may hold values from -2 to 2
- fine_gain: float32 [256], replicated, may hold values from 0.25 to 1.75
- fine_shift: float32 [256], replicated, may hold values from -2 to 2
- coarse_kernel: bfloat16 [3, 3, 3, 256, 256], replicated, may hold values from -0.078125 to 0.078125
- lift_kernel: bfloat16 [3, 3, 3, 256, 256], replicated, may hold values from -0.078125 to 0.078125
- fine_kernel: bfloat16 [3, 3, 3, 256, 128], replicated, may hold values from -0.078125 to 0.078125
- skip_kernel: bfloat16 [256, 128], replicated, may hold values from -0.375 to 0.375
Outputs:
- decoded: bfloat16 [8, 256, 128, 128], P('ta', 'ha', 'wa')
The draws below stay inside these ranges and needn't reach their ends.
All inputs are finite; a program needn't handle non-finite values.
Results may differ from the reference program's by a relative error of at most 0.008.
Values may be sent and summed in bfloat16 or wider, within the bound.
A program may use at most 128 MiB of HBM per device.

```python
import jax
import jax.numpy as jnp
from jax import lax

C2 = 256
C1 = 128
GROUPS = 32
FT = 2
CH = 16
CW = 8
FRAMES = 8
HC = 128
WC = 64
HF = 256
WF = 128


def block_levels(key, count, repeat, low, high):
    levels = jnp.exp(jax.random.uniform(key, (count,), jnp.float32, low, high))
    return jnp.repeat(levels, repeat)


def draw_coarse(key, part):
    key = jax.random.fold_in(key, 11)
    keys = jax.random.split(key, 9)
    frame_pos = jnp.arange(FRAMES, dtype=jnp.float32) / (FRAMES - 1)
    row_pos = jnp.arange(HC, dtype=jnp.float32) / (HC - 1)
    col_pos = jnp.arange(WC, dtype=jnp.float32) / (WC - 1)
    ramp = frame_pos[:, None, None, None] + row_pos[None, :, None, None] + col_pos[None, None, :, None]
    level_frames = block_levels(keys[2], FRAMES // FT, FT, -1.0, 0.0)
    level_rows = block_levels(keys[3], HC // CH, CH, -1.0, 0.0)
    level_cols = block_levels(keys[4], WC // CW, CW, -1.0, 0.0)
    level = level_frames[:, None, None, None] * level_rows[None, :, None, None] * level_cols[None, None, :, None]
    scale = 0.5 * jnp.power(3.0, ramp) / 3.0 * level
    factor_frames = block_levels(keys[5], FRAMES // FT, FT, -0.7, 0.7)
    factor_rows = block_levels(keys[6], HC // CH, CH, -0.7, 0.7)
    factor_cols = block_levels(keys[7], WC // CW, CW, -0.7, 0.7)
    factor = factor_frames[:, None, None, None] * factor_rows[None, :, None, None] * factor_cols[None, None, :, None]
    channel_offset = 0.3 * jax.random.normal(keys[8], (C2,), jnp.float32)
    block_offset = channel_offset * factor
    values = jax.random.truncated_normal(keys[0], -4.0, 4.0, (FRAMES, HC, WC, C2), jnp.float32) * scale + block_offset
    values = jnp.clip(values, -20.0, 20.0)
    return values.astype(jnp.bfloat16)


def steps_of(rng, extent, shards, smallest, largest):
    level, own = 1.0, jax.random.fold_in(rng, 6)
    for dim, blocks in shards:
        draws = jnp.exp(jax.random.uniform(jax.random.fold_in(own, dim), (blocks,), jnp.float32, smallest / len(shards), largest / len(shards)))
        level = level * jnp.repeat(draws, extent[dim] // blocks).reshape([-1 if axis == dim else 1 for axis in range(len(extent))])
    return level


def scatter_about(key, extent, deviation, bound, pieces=(), kind=jnp.bfloat16):
    loudness = steps_of(key, extent, pieces, -0.22, 0.18) if pieces else 1.0
    array = jax.random.normal(key, extent, jnp.float32) * deviation * loudness
    return jnp.minimum(jnp.maximum(array, -bound), bound).astype(kind)


def setup_inputs(seed: int = 0) -> dict:
    splits = jax.random.split(jax.random.key(seed), 13)
    return {
        "coarse": draw_coarse(jax.random.fold_in(splits[12], 71), 0),
        "cache_coarse": scatter_about(splits[1], (2, HC, WC, C2), 1.0, 6.0, ((1, 8), (2, 8))),
        "cache_middle": scatter_about(splits[2], (2, HC, WC, C2), 1.0, 6.0, ((1, 8), (2, 8))),
        "cache_fine": scatter_about(splits[3], (2, HF, WF, C2), 1.0, 6.0, ((1, 8), (2, 8))),
        "coarse_gain": jnp.clip(1.0 + 0.15 * jax.random.normal(splits[4], (C2,), jnp.float32), 0.25, 1.75),
        "coarse_shift": scatter_about(splits[5], (C2,), 0.5, 2.0, (), jnp.float32),
        "fine_gain": jnp.clip(1.0 + 0.15 * jax.random.normal(splits[6], (C2,), jnp.float32), 0.25, 1.75),
        "fine_shift": scatter_about(splits[7], (C2,), 0.5, 2.0, (), jnp.float32),
        "coarse_kernel": scatter_about(splits[8], (3, 3, 3, C2, C2), (27 * C2) ** -0.5, 0.078125),
        "lift_kernel": scatter_about(splits[9], (3, 3, 3, C2, C2), (27 * C2) ** -0.5, 0.078125),
        "fine_kernel": scatter_about(splits[10], (3, 3, 3, C2, C1), (27 * C2) ** -0.5, 0.078125),
        "skip_kernel": scatter_about(splits[11], (C2, C1), C2 ** -0.5, 0.375),
    }


def norm_silu(values, gain, shift):
    floats = values.astype(jnp.float32)
    channels = floats.shape[-1]
    group_size = channels // GROUPS
    entries = floats.shape[0] * floats.shape[1] * floats.shape[2] * group_size
    sums = lax.optimization_barrier(jnp.sum(floats, axis=(0, 1, 2)))
    average = jnp.repeat(lax.optimization_barrier(jnp.sum(sums.reshape(GROUPS, group_size), axis=1)) / entries, group_size)
    centered = floats - average
    squares = lax.optimization_barrier(jnp.sum(centered * centered, axis=(0, 1, 2)))
    spread = jnp.repeat(lax.optimization_barrier(jnp.sum(squares.reshape(GROUPS, group_size), axis=1)) / entries, group_size)
    normed = centered * lax.rsqrt(spread + 1e-06) * gain + shift
    return jax.nn.silu(normed).astype(jnp.bfloat16)

def causal_conv(inputs, cache, kernel):
    joined = jnp.concatenate([cache, inputs], axis=0).astype(jnp.float32)
    result = lax.conv_general_dilated(joined[None], kernel.astype(jnp.float32), (1, 1, 1), ((0, 0), (1, 1), (1, 1)), dimension_numbers=('NDHWC', 'DHWIO', 'NDHWC'), precision=lax.Precision.HIGHEST)
    return result[0]

def enlarge(values):
    return jnp.repeat(jnp.repeat(values, 2, axis=1), 2, axis=2)

def reference(coarse, cache_coarse, cache_middle, cache_fine, coarse_gain, coarse_shift, fine_gain, fine_shift, coarse_kernel, lift_kernel, fine_kernel, skip_kernel):
    activated = norm_silu(coarse, coarse_gain, coarse_shift)
    middle = (coarse.astype(jnp.float32) + causal_conv(activated, cache_coarse, coarse_kernel)).astype(jnp.bfloat16)
    lifted = causal_conv(enlarge(middle), enlarge(cache_middle), lift_kernel).astype(jnp.bfloat16)
    fine_act = norm_silu(lifted, fine_gain, fine_shift)
    shape = lifted.shape
    skipped = jnp.dot(lifted.reshape(-1, shape[3]), skip_kernel, preferred_element_type=jnp.float32)
    skipped = skipped.reshape(shape[0], shape[1], shape[2], skip_kernel.shape[1])
    decoded = skipped + causal_conv(fine_act, cache_fine, fine_kernel)
    return decoded.astype(jnp.bfloat16)
```

```python
import functools

import jax
import jax.numpy as jnp
from jax import lax
from jax.experimental import pallas as pl
from jax.experimental.pallas import tpu as pltpu
from jax.sharding import PartitionSpec as P

GROUPS = 32
EPS = 1e-06
MESH = pl.DeviceIdType.MESH
F32 = jnp.float32
BF16 = jnp.bfloat16


def rolled(value, shift):
    size = value.shape[0]
    shift = shift % size
    return value if shift == 0 else pltpu.roll(value, shift, 0)


def put(ref, start, value):
    width = ref.shape[-1]
    for part in range(value.shape[1] // width):
        ref[part, pl.ds(start, value.shape[0]), :] = value[:, part * width : (part + 1) * width]


def take(ref, start, stride=1, parts=None):
    at = pl.ds(start, 16) if stride == 1 else pl.ds(start, 16, stride=stride)
    return jnp.concatenate([ref[part, at, :] for part in range(parts or ref.shape[0])], axis=1)


def body(
    sizes,
    coarse_hbm, cache_coarse_hbm, cache_middle_hbm, cache_fine_hbm,
    coarse_gain, coarse_shift, fine_gain, fine_shift,
    coarse_kernel, lift_kernel, fine_kernel, skip_kernel,
    out_ref, affine,
    cb, ccb, cmb, cfb, xf, cff, xt, ts, xtf, ss, sr, saf, act_a, acc1, w1, lk, w2, w3, skw,
    cm, cs, cfs, mt, mid_g, gf, acc2, lt, lf, acc3, back, ar_src, ar_recv,
    local_sem, ar_send, ar_got, send_sem, recv_sem,
):
    nt, nh, nw, C, C1 = sizes
    half = gf.shape[0] // 2
    ta, ha, wa = lax.axis_index("ta"), lax.axis_index("ha"), lax.axis_index("wa")
    row16 = lax.broadcasted_iota(jnp.int32, (16, C), 0)
    row16w = lax.broadcasted_iota(jnp.int32, (16, 2 * C), 0)
    first_w, last_w, first_h, last_h = wa == 0, wa == nw - 1, ha == 0, ha == nh - 1

    def near(t=0, h=0, w=0):
        where = {}
        if t:
            where["ta"] = lax.rem(ta + (t + nt), nt)
        if h:
            where["ha"] = lax.rem(ha + (h + nh), nh)
        if w:
            where["wa"] = lax.rem(wa + (w + nw), nw)
        return where

    loads = []

    def load(src, dst):
        copy = pltpu.make_async_copy(src, dst, local_sem.at[len(loads)])
        copy.start()
        loads.append(copy)
        return copy

    get_coarse = load(coarse_hbm, cb)
    barrier = pltpu.get_barrier_semaphore()
    friends = [near(w=d) for d in range(1, nw)] + [near(h=d) for d in range(1, nh)] + [near(t=d) for d in range(1, nt)]
    friends += [near(t=-1, w=1), near(t=-1, w=-1)]
    for friend in friends:
        pl.semaphore_signal(barrier, inc=1, device_id=friend, device_id_type=MESH)
    get_cc = load(cache_coarse_hbm, ccb)
    get_cm = load(cache_middle_hbm, cmb)
    get_cf = load(cache_fine_hbm, cfb)
    get_lk = load(lift_kernel, lk)
    get_w1 = [
        load(coarse_kernel.at[dt, dh, dw], w1.at[dt, (3 * dw + dh) * C : (3 * dw + dh + 1) * C])
        for dt in range(3) for dh in range(3) for dw in range(3)
    ]
    get_w3 = [
        load(fine_kernel.at[dt, dh], w3.at[3 * dt : 3 * dt + 3, (a + dh) * C : (a + dh + 1) * C, a * C1 : (a + 1) * C1])
        for dt in range(3) for dh in range(3) for a in range(2)
    ]
    get_affine = [load(ref, affine.at[i]) for i, ref in enumerate((coarse_gain, coarse_shift, fine_gain, fine_shift))]
    get_skip = [load(skip_kernel, skw.at[a * C : (a + 1) * C, a * C1 : (a + 1) * C1]) for a in range(2)]

    get_coarse.wait()
    flat = cb[...].astype(F32)
    put(xf, 0, flat)
    count = flat.shape[0]
    mean = jnp.sum(flat, axis=0, keepdims=True) / count
    centred = flat - mean
    ar_src[0, 0] = jnp.zeros((8, C), F32)
    ar_src[0, 0, 0:1, :] = mean
    ar_src[0, 0, 1:2, :] = jnp.sum(centred * centred, axis=0, keepdims=True) / count
    get_cc.wait()
    pl.semaphore_wait(barrier, len(friends))

    def message(index, src, dst, where):
        return pltpu.make_async_remote_copy(
            src_ref=src, dst_ref=dst, send_sem=send_sem.at[index], recv_sem=recv_sem.at[index],
            device_id=where, device_id_type=MESH,
        )

    stages = ((("w", nw), 0), (("h", nh), nw - 1), (("t", nt), nw - 1 + nh - 1))

    def ar_copies(which, stage):
        (axis, n), base = stages[stage]
        return [
            pltpu.make_async_remote_copy(
                src_ref=ar_src.at[which, stage], dst_ref=ar_recv.at[which, base + d - 1],
                send_sem=ar_send.at[which, base + d - 1], recv_sem=ar_got.at[which, base + d - 1],
                device_id=near(**{axis: d}), device_id_type=MESH,
            )
            for d in range(1, n)
        ]

    def ar_start(which, stage):
        for copy in ar_copies(which, stage):
            copy.start()

    def ar_finish(which, stage):
        (_, n), base = stages[stage]
        for copy in ar_copies(which, stage):
            copy.wait_recv()
        tiles = [ar_src[which, stage]] + [ar_recv[which, base + d - 1] for d in range(1, n)]
        average = functools.reduce(jnp.add, tiles) / n
        spread = functools.reduce(jnp.add, [(tile - average) * (tile - average) for tile in tiles]) / n
        rows = lax.broadcasted_iota(jnp.int32, (8, C), 0)
        return average + jnp.where(rows == 1, pltpu.roll(spread, 1, 0), 0.0)

    def ar_next(which, stage):
        ar_src[which, stage + 1] = ar_finish(which, stage)
        ar_start(which, stage + 1)

    size = C // GROUPS
    width = xf.shape[-1]

    def group_mean(value):
        lane_of = lax.broadcasted_iota(jnp.int32, (8, width), 1)
        parts = []
        for part in range(C // width):
            x = jnp.broadcast_to(value[:, part * width : (part + 1) * width], (8, width))
            step = 1
            while step < size:
                x = x + jnp.where((lane_of & step) == 0, pltpu.roll(x, width - step, 1), pltpu.roll(x, step, 1))
                step *= 2
            parts.append(x[0:1])
        return jnp.concatenate(parts, axis=1) / size

    def normaliser(which, gain, shift):
        tile = ar_finish(which, 2)
        mean, variance = tile[0:1], tile[1:2]
        grouped = group_mean(mean)
        away = mean - grouped
        mean, variance = grouped, group_mean(variance + away * away)
        half_scale = 0.5 * (gain * lax.rsqrt(variance + EPS))
        half_shift = 0.5 * shift

        def act(x, mean=mean, half_scale=half_scale, half_shift=half_shift):
            half = (x - mean) * half_scale + half_shift
            return half + half * jnp.tanh(half)

        return act, mean, half_scale, half_shift

    ar_start(0, 0)
    for f in range(2):
        for c in range(8):
            xt[2 + f, 2 + c] = take(xf, f * 128 + c, 8).astype(BF16)

    @pl.when(ta == nt - 1)
    def _():
        put(xf, 0, ccb[...].astype(F32))
        for f in range(2):
            for c in range(8):
                ts[f, c] = take(xf, f * 128 + c, 8).astype(BF16)

    @pl.when(ta != nt - 1)
    def _():
        ts[...] = xt[2:4, 2:10]

    first = [
        message(0, ts, xt.at[0:2, 2:10], near(t=1)),
        message(1, xt.at[2:4, 8:10], xt.at[2:4, 0:2], near(w=1)),
        message(2, xt.at[2:4, 2:4], xt.at[2:4, 10:12], near(w=-1)),
        message(3, ts.at[:, 6:8], xt.at[0:2, 0:2], near(t=1, w=1)),
        message(4, ts.at[:, 0:2], xt.at[0:2, 10:12], near(t=1, w=-1)),
    ]
    for copy in first:
        copy.start()

    cm_first = [
        message(5, cm.at[:, 8:9], cm.at[:, 0:1], near(w=1)),
        message(6, cm.at[:, 1:2], cm.at[:, 9:10], near(w=-1)),
    ]
    cf_first = [
        message(7, lt.at[:, 0:2, 8:9, :, 0:C], lt.at[:, 0:2, 0:1, :, 0:C], near(w=1)),
        message(8, lt.at[:, 0:2, 0:1, :, C : 2 * C], lt.at[:, 0:2, 8:9, :, C : 2 * C], near(w=-1)),
    ]
    cm_second = [
        message(11, cs.at[:, 0:1], cm.at[:, 11:12], near(h=-1)),
        message(12, cs.at[:, 1:2], cm.at[:, 10:11], near(h=1)),
    ]
    cf_second = [
        message(13, cfs.at[0], lt.at[0, 0:2, 9:10], near(h=-1)),
        message(14, cfs.at[1], lt.at[1, 0:2, 9:10], near(h=1)),
    ]

    get_cm.wait()

    @pl.when(ta < 2)
    def _():
        put(xf, 0, cmb[...].astype(F32))
        for f in range(2):
            for c in range(8):
                cm[f, 1 + c] = take(xf, f * 128 + c, 8).astype(BF16)
        for copy in cm_first:
            copy.start()

    for dt in range(3):
        for dw in range(3):
            w3[3 * dt + dw, 3 * C : 4 * C, 0:C1] = jnp.zeros((C, C1), BF16)
            w3[3 * dt + dw, 0:C, C1 : 2 * C1] = jnp.zeros((C, C1), BF16)
    skw[0:C, C1 : 2 * C1] = jnp.zeros((C, C1), BF16)
    skw[C : 2 * C, 0:C1] = jnp.zeros((C, C1), BF16)
    def fold(i, carry):
        dt, r = i // (C // 16), pl.multiple_of(lax.rem(i, C // 16) * 16, 16)
        taps = [[lk[dt, dh, dw, pl.ds(r, 16), :].astype(F32) for dw in range(3)] for dh in range(3)]
        for a in range(2):
            for k in range(2):
                if a == 0:
                    line = taps[0] if k == 0 else [taps[1][d] + taps[2][d] for d in range(3)]
                else:
                    line = [taps[0][d] + taps[1][d] for d in range(3)] if k == 0 else taps[2]
                wide = ((line[0] + line[1], line[2]), (line[0], line[1] + line[2]))
                for b in range(2):
                    for j in range(2):
                        w2[a, dt, pl.ds((2 * j + k) * C + r, 16), b * C : (b + 1) * C] = wide[b][j].astype(BF16)
        return carry

    get_lk.wait()
    ar_next(0, 0)
    lax.fori_loop(0, 3 * (C // 32), fold, 0)
    ar_next(0, 1)

    for copy in first:
        copy.wait_recv()

    def widen(i, carry):
        f, c = i // 12, i % 12
        put(xtf, pl.multiple_of(i * 16, 16), xt[f, c].astype(F32))
        return carry

    lax.fori_loop(0, 48, widen, 0, unroll=8)
    for f in range(4):
        for side, rows in enumerate(((0, 1), (14, 15))):
            for k, row in enumerate(rows):
                ss[side, f, k] = take(xtf, f * 192 + row, 16).astype(BF16)
    second = [
        message(9, ss.at[0], sr.at[1], near(h=-1)),
        message(10, ss.at[1], sr.at[0], near(h=1)),
    ]
    for copy in second:
        copy.start()

    @pl.when(ta < 2)
    def _():
        for copy in cm_first:
            copy.wait_recv()
        for f in range(2):
            for c in range(10):
                put(gf, 16 * c, cm[f, c].astype(F32))
            cs[f, 0] = take(gf, 0, 16, half).astype(BF16)
            cs[f, 1] = take(gf, 15, 16, half).astype(BF16)
        for copy in cm_second:
            copy.start()

    lax.fori_loop(3 * (C // 32), 3 * (C // 16), fold, 0)
    for copy in get_w1 + get_w3 + get_skip + get_affine:
        copy.wait()

    for copy in second:
        copy.wait_recv()
    act, *_ = normaliser(0, affine[0], affine[1])

    cols = lax.broadcasted_iota(jnp.int32, (16, C), 0)

    def strips_of(f):
        raw = jnp.logical_and(ta == 0, f < 2)
        for side in range(2):
            outside = first_h if side == 0 else last_h
            for k in range(2):
                x = sr[side, f, k].astype(F32)
                y = jnp.where(raw, x, act(x)) if f < 2 else act(x)
                gone = jnp.logical_or(jnp.logical_and(first_w, cols < 2), jnp.logical_and(last_w, cols >= 10))
                saf[f, side, k] = jnp.where(jnp.logical_or(outside, gone), 0.0, y)

    def act_coarse(f):
        strips_of(f)
        for c in range(12):
            at = f * 192 + c * 16
            x = take(xtf, at)
            x = jnp.where(ta == 0, x, act(x)) if f < 2 else act(x)
            if c < 2:
                x = jnp.where(first_w, 0.0, x)
            if c >= 10:
                x = jnp.where(last_w, 0.0, x)
            put(xtf, at, x)
            above = jnp.where(row16 == 0, saf[f, 0, 1, c : c + 1, :], rolled(x, 1))
            below = jnp.where(row16 == 15, saf[f, 1, 0, c : c + 1, :], rolled(x, -1))
            act_a[f, c, :, 0:C] = above.astype(BF16)
            act_a[f, c, :, C : 2 * C] = x.astype(BF16)
            act_a[f, c, :, 2 * C : 3 * C] = below.astype(BF16)
        top = take(xtf, f * 192, 16)
        bottom = take(xtf, f * 192 + 15, 16)
        for side, lines in enumerate(((saf[f, 0, 0], saf[f, 0, 1], top), (bottom, saf[f, 1, 0], saf[f, 1, 1]))):
            for dw in range(3):
                for dh in range(3):
                    act_a[f, 12 + 2 * dw + side, :, dh * C : (dh + 1) * C] = rolled(lines[dh], -dw).astype(BF16)

    def conv_coarse(g):
        lhs = jnp.concatenate(
            [
                jnp.concatenate([act_a[g, dw : dw + 10], act_a[g, 12 + 2 * dw : 14 + 2 * dw]], axis=0)
                for dw in range(3)
            ],
            axis=-1,
        ).reshape(12 * 16, 9 * C)
        for f in range(2):
            if 0 <= g - f <= 2:
                part = jnp.dot(lhs, w1[g - f], preferred_element_type=F32).reshape(12, 16, C)
                acc1[f] = part if g == f else acc1[f] + part

    def finish_middle(f):
        for c in range(10):
            y = xt[2 + f, 1 + c].astype(F32) + acc1[f, c]
            if c == 0:
                y = jnp.where(first_w, 0.0, y)
            if c == 9:
                y = jnp.where(last_w, 0.0, y)
            mt[4 + f, c] = y.astype(BF16)
        gone = (cols > 9) | (first_w & (cols == 0)) | (last_w & (cols == 9))
        for side in range(2):
            y = rolled(sr[side, 2 + f, 1 - side].astype(F32), -1) + acc1[f, 10 + side]
            y = jnp.where(jnp.logical_or(gone, first_h if side == 0 else last_h), 0.0, y)
            mt[4 + f, 10 + side] = y.astype(BF16)

    to_next = [message(15 + f, mt.at[4 + f : 5 + f], mt.at[2 + f : 3 + f], near(t=1)) for f in range(2)]

    def send_middle(f):
        finish_middle(f)

        @pl.when(ta < nt - 1)
        def _():
            to_next[f].start()

    act_coarse(0)
    for g in range(4):
        if g < 3:
            act_coarse(g + 1)
        conv_coarse(g)
        if g >= 2:
            send_middle(g - 2)

    to_second = message(17, mt.at[4:6], mt.at[0:2], near(t=2))
    by_second = message(17, mt.at[2:4], mt.at[0:2], near(t=1))

    def prepare(g):
        top = mt[g, 10].astype(F32)
        bottom = mt[g, 11].astype(F32)
        for c in range(10):
            x = mt[g, c].astype(F32)
            put(gf, 16 * c, x)
            mid_g[g, c, :, 0:C] = jnp.where(row16 == 0, top[c : c + 1], rolled(x, 1)).astype(BF16)
            mid_g[g, c, :, C : 2 * C] = mt[g, c]
            mid_g[g, c, :, 2 * C : 3 * C] = jnp.where(row16 == 15, bottom[c : c + 1], rolled(x, -1)).astype(BF16)
        row_top = take(gf, 0, 16, half)
        row_bottom = take(gf, 15, 16, half)
        for j in range(2):
            mid_g[g, 10 + j, :, 0:C] = rolled(row_bottom, -j).astype(BF16)
            mid_g[g, 10 + j, :, C : 2 * C] = rolled(bottom, -j).astype(BF16)
            mid_g[g, 12 + j, :, C : 2 * C] = rolled(top, -j).astype(BF16)
            mid_g[g, 12 + j, :, 2 * C : 3 * C] = rolled(row_top, -j).astype(BF16)

    def lift_part(a, dt, g, frames):
        lanes = slice(a * C, (a + 2) * C)
        lhs = jnp.concatenate(
            [
                jnp.concatenate(
                    [mid_g[g : g + frames, j : j + 9, :, lanes], mid_g[g : g + frames, 10 + 2 * a + j : 11 + 2 * a + j, :, lanes]],
                    axis=1,
                )
                for j in range(2)
            ],
            axis=-1,
        ).reshape(frames * 10 * 16, 4 * C)
        part = jnp.dot(lhs, w2[a, dt], preferred_element_type=F32)
        return part.reshape(frames, 10, 16, 2 * C)

    def cached_middle(at):
        gone = (cols > 9) | (first_w & (cols == 0)) | (last_w & (cols == 9))
        for f in range(2):
            mt[at + f, 1:9] = cm[f, 1:9]
            mt[at + f, 0] = jnp.where(first_w, 0.0, cm[f, 0].astype(F32)).astype(BF16)
            mt[at + f, 9] = jnp.where(last_w, 0.0, cm[f, 9].astype(F32)).astype(BF16)
            for side in range(2):
                outside = jnp.logical_or(gone, first_h if side == 0 else last_h)
                mt[at + f, 10 + side] = jnp.where(outside, 0.0, cm[f, 10 + side].astype(F32)).astype(BF16)

    prepare(4)
    prepare(5)
    for a in range(2):
        acc2[a] = lift_part(a, 2, 4, 2)
        acc2[a, 1:2] += lift_part(a, 1, 4, 1)

    @pl.when(ta == 0)
    def _():
        for copy in cm_second:
            copy.wait_recv()
        cached_middle(2)

    @pl.when(ta > 0)
    def _():
        for copy in to_next:
            copy.wait_recv()

    @pl.when(ta == 2)
    def _():
        by_second.start()

    prepare(2)
    prepare(3)
    for a in range(2):
        acc2[a] += lift_part(a, 0, 2, 2)
        acc2[a, 0:1] += lift_part(a, 1, 3, 1)
        lt[a, 2:4] = acc2[a].astype(BF16)

    @pl.when(ta == 0)
    def _():
        to_second.start()

    def own_sums(fn):
        total = jnp.zeros((16, C), F32)
        for a in range(2):
            for f in range(2):
                for p in range(9):
                    for b in range(2):
                        if (p, b) in ((0, 0), (8, 1)):
                            continue
                        total = total + fn(lt[a, 2 + f, p, :, b * C : (b + 1) * C].astype(F32))
        return jnp.sum(total, axis=0, keepdims=True) / (2 * 2 * 16 * 16)

    mean = own_sums(lambda x: x)
    ar_src[1, 0] = jnp.zeros((8, C), F32)
    ar_src[1, 0, 0:1, :] = mean
    ar_src[1, 0, 1:2, :] = own_sums(lambda x: (x - mean) * (x - mean))
    ar_start(1, 0)

    def lift_before_new(a):
        acc2[a] = lift_part(a, 2, 2, 2)
        acc2[a, 1:2] += lift_part(a, 1, 2, 1)

    def lift_before_old(a):
        acc2[a] += lift_part(a, 0, 0, 2)
        lt[a, 0:1] = (acc2[a, 0:1] + lift_part(a, 1, 1, 1)).astype(BF16)
        lt[a, 1:2] = acc2[a, 1:2].astype(BF16)

    @pl.when(ta > 0)
    def _():
        lift_before_new(0)
        lift_before_new(1)

    get_cf.wait()

    @pl.when(ta == 0)
    def _():
        put(cff, 0, cfb[...].astype(F32))
        for f in range(2):
            for c in range(16):
                p, b = (c + 1) // 2, (c + 1) % 2
                for a in range(2):
                    lt[a, f, p, :, b * C : (b + 1) * C] = take(cff, f * 512 + a * 16 + c, 32).astype(BF16)
        for copy in cf_first:
            copy.start()

    ar_next(1, 0)

    @pl.when(ta == 0)
    def _():
        for copy in cf_first:
            copy.wait_recv()
        for f in range(2):
            for a, row in ((0, 0), (1, 15)):
                for p in range(9):
                    put(gf, 16 * p, lt[a, f, p].astype(F32))
                cfs[a, f, 0] = take(gf, row, 16).astype(BF16)
        for copy in cf_second:
            copy.start()

    for b in range(2):
        lhs = jnp.concatenate([lt[a, 2:4, 1 - b : 9 - b, :, b * C : (b + 1) * C] for a in range(2)], axis=-1)
        part = jnp.dot(lhs.reshape(2 * 8 * 16, 2 * C), skw[...], preferred_element_type=F32)
        acc3[:, :, 1 - b] = part.reshape(2, 8, 16, 2 * C1)

    ar_next(1, 1)

    @pl.when(ta == 1)
    def _():
        for copy in cm_second:
            copy.wait_recv()
        cached_middle(0)

    @pl.when(ta > 1)
    def _():
        to_second.wait_recv()

    @pl.when(ta > 0)
    def _():
        prepare(0)
        prepare(1)
        lift_before_old(0)
        lift_before_old(1)


    lane = lax.broadcasted_iota(jnp.int32, (16, 2 * C), 1)

    def spread_fine(f, fn):
        top = jnp.where(first_h, 0.0, fn(lt[1, f, 9].astype(F32)))
        bottom = jnp.where(last_h, 0.0, fn(lt[0, f, 9].astype(F32)))
        for p in range(9):
            even = fn(lt[0, f, p].astype(F32))
            odd = fn(lt[1, f, p].astype(F32))
            before = jnp.where(row16w == 0, top[p : p + 1], rolled(odd, 1))
            after = jnp.where(row16w == 15, bottom[p : p + 1], rolled(even, -1))
            for k, part in enumerate((before, even, odd, after)):
                if p == 0:
                    part = jnp.where(first_w & (lane < C), 0.0, part)
                if p == 8:
                    part = jnp.where(last_w & (lane >= C), 0.0, part)
                part = part.astype(BF16)
                for b in range(2):
                    lf[f, 2 * p + b, :, k * C : (k + 1) * C] = part[:, b * C : (b + 1) * C]

    @pl.when(ta == 0)
    def _():
        for copy in cf_second:
            copy.wait_recv()

    _, mean, half_scale, half_shift = normaliser(1, affine[2], affine[3])
    mean2 = jnp.concatenate([mean, mean], axis=1)
    scale2 = jnp.concatenate([half_scale, half_scale], axis=1)
    shift2 = jnp.concatenate([half_shift, half_shift], axis=1)

    def fine_act(x):
        half = (x - mean2) * scale2 + shift2
        return half + half * jnp.tanh(half)

    def fine_act_or_cached(x):
        return jnp.where(ta == 0, x, fine_act(x))

    def conv_fine(g):
        lhs = jnp.concatenate([lf[g, dw : dw + 16] for dw in range(3)], axis=-1).reshape(16 * 16, 12 * C)
        for f in range(2):
            dt = g - f
            if 0 <= dt <= 2:
                weights = w3[3 * dt : 3 * dt + 3].reshape(12 * C, 2 * C1)
                acc3[f] += jnp.dot(lhs, weights, preferred_element_type=F32).reshape(8, 2, 16, 2 * C1)

    def finish_fine(f):
        for c in range(16):
            for a in range(2):
                back[pl.ds(f * 512 + a * 16 + c, 16, stride=32), :] = acc3[f, c // 2, c % 2, :, a * C1 : (a + 1) * C1]
        out_ref[f * 512 : (f + 1) * 512] = back[f * 512 : (f + 1) * 512].astype(BF16)

    spread_fine(0, fine_act_or_cached)
    for g in range(4):
        if g < 3:
            spread_fine(g + 1, fine_act_or_cached if g + 1 < 2 else fine_act)
        conv_fine(g)
        if g >= 2:
            finish_fine(g - 2)

    for which in range(2):
        for stage in range(3):
            for copy in ar_copies(which, stage):
                copy.wait_send()
    for copy in first + second:
        copy.wait_send()

    @pl.when(ta < 2)
    def _():
        for copy in cm_first + cm_second:
            copy.wait_send()

    @pl.when(ta == 0)
    def _():
        for copy in cf_first + cf_second:
            copy.wait_send()

    @pl.when(ta < nt - 1)
    def _():
        for copy in to_next:
            copy.wait_send()

    @pl.when(jnp.logical_or(ta == 0, ta == 2))
    def _():
        to_second.wait_send()


def local(
    sizes, coarse, cache_coarse, cache_middle, cache_fine, coarse_gain, coarse_shift, fine_gain, fine_shift,
    coarse_kernel, lift_kernel, fine_kernel, skip_kernel,
):
    nt, nh, nw, C, C1 = sizes
    frames, rows, cols, _ = coarse.shape
    assert (frames, rows, cols) == (2, 16, 8)
    peers = nw + nh + nt - 3
    hbm = pl.BlockSpec(memory_space=pltpu.HBM)
    vmem = pl.BlockSpec(memory_space=pltpu.VMEM)
    V = pltpu.VMEM
    W = min(128, C)
    L = C // W
    scratch = [
        V((4, 1, C), F32),
        V((256, C), BF16), V((256, C), BF16), V((256, C), BF16), V((1024, C), BF16),
        V((L, 256, W), F32), V((L, 1024, W), F32),
        V((4, 12, 16, C), BF16), V((2, 8, 16, C), BF16), V((L, 4 * 12 * 16 + 64, W), F32),
        V((2, 4, 2, 16, C), BF16), V((2, 4, 2, 16, C), BF16), V((4, 2, 2, 16, C), F32),
        V((4, 18, 16, 3 * C), BF16), V((2, 12, 16, C), F32),
        V((3, 9 * C, C), BF16), V((3, 3, 3, C, C), BF16), V((2, 3, 4 * C, 2 * C), BF16),
        V((9, 4 * C, 2 * C1), BF16), V((2 * C, 2 * C1), BF16),
        V((2, 12, 16, C), BF16), V((2, 2, 16, C), BF16), V((2, 2, 1, 16, 2 * C), BF16),
        V((6, 12, 16, C), BF16), V((6, 14, 16, 3 * C), BF16), V((2 * L, 256, W), F32),
        V((2, 2, 10, 16, 2 * C), F32), V((2, 4, 10, 16, 2 * C), BF16),
        V((4, 18, 16, 4 * C), BF16), V((2, 8, 2, 16, 2 * C1), F32), V((1024, C1), F32),
        V((2, 3, 8, C), F32), V((2, peers, 8, C), F32),
        pltpu.SemaphoreType.DMA((60,)),
        pltpu.SemaphoreType.DMA((2, peers)), pltpu.SemaphoreType.DMA((2, peers)),
        pltpu.SemaphoreType.DMA((18,)), pltpu.SemaphoreType.DMA((18,)),
    ]
    decoded = pl.pallas_call(
        functools.partial(body, sizes),
        out_shape=jax.ShapeDtypeStruct((1024, C1), BF16),
        in_specs=[hbm] * 12,
        out_specs=vmem,
        scratch_shapes=scratch,
        compiler_params=pltpu.CompilerParams(
            collective_id=0, has_side_effects=True, vmem_limit_bytes=63 * 1024 * 1024
        ),
    )(
        coarse.reshape(256, C), cache_coarse.reshape(256, C), cache_middle.reshape(256, C), cache_fine.reshape(1024, C),
        coarse_gain.reshape(1, C), coarse_shift.reshape(1, C), fine_gain.reshape(1, C), fine_shift.reshape(1, C),
        coarse_kernel, lift_kernel, fine_kernel, skip_kernel,
    )
    return decoded.reshape(2, 32, 16, C1)


def solution(mesh):
    def run(*args):
        channels, outer = args[-1].shape
        sizes = (mesh.shape["ta"], mesh.shape["ha"], mesh.shape["wa"], channels, outer)
        return jax.shard_map(
            functools.partial(local, sizes),
            mesh=mesh,
            in_specs=(P("ta", "ha", "wa", None),) + (P(None, "ha", "wa", None),) * 3 + (P(),) * 8,
            out_specs=P("ta", "ha", "wa", None),
            check_vma=False,
        )(*args)

    return run
```

```python
import functools

import jax
import jax.numpy as jnp
from jax import lax
from jax.experimental import pallas as pl
from jax.experimental.pallas import tpu as pltpu
from jax.sharding import PartitionSpec as P

GROUPS = 32
EPS = 1e-06
MESH = pl.DeviceIdType.MESH
F32 = jnp.float32
BF16 = jnp.bfloat16


def rolled(value, shift):
    size = value.shape[0]
    shift = shift % size
    return value if shift == 0 else pltpu.roll(value, shift, 0)


def put(ref, start, value):
    width = ref.shape[-1]
    for part in range(value.shape[1] // width):
        ref[part, pl.ds(start, value.shape[0]), :] = value[:, part * width : (part + 1) * width]


def take(ref, start, stride=1, parts=None):
    at = pl.ds(start, 16) if stride == 1 else pl.ds(start, 16, stride=stride)
    return jnp.concatenate([ref[part, at, :] for part in range(parts or ref.shape[0])], axis=1)


def body(
    sizes,
    coarse_hbm, cache_coarse_hbm, cache_middle_hbm, cache_fine_hbm,
    coarse_gain, coarse_shift, fine_gain, fine_shift,
    coarse_kernel, lift_kernel, fine_kernel, skip_kernel,
    out_ref, affine,
    cb, cbp, cmb, cfb, xf, cff, xt, xtf, ss, sr, saf, act_a, acc1, w1, lk, w2, w3, skw,
    cm, cs, cfs, mt, mid_g, gf, acc2, lt, lf, acc3, back, outb, ar_src, ar_recv,
    local_sem, ar_send, ar_got, send_sem, recv_sem,
):
    nt, nh, nw, C, C1 = sizes
    half = gf.shape[0] // 2
    ta, ha, wa = lax.axis_index("ta"), lax.axis_index("ha"), lax.axis_index("wa")
    row16 = lax.broadcasted_iota(jnp.int32, (16, C), 0)
    row16w = lax.broadcasted_iota(jnp.int32, (16, 2 * C), 0)
    first_w, last_w, first_h, last_h = wa == 0, wa == nw - 1, ha == 0, ha == nh - 1

    def near(t=0, h=0, w=0):
        where = {}
        if t:
            where["ta"] = lax.rem(ta + (t + nt), nt)
        if h:
            where["ha"] = lax.rem(ha + (h + nh), nh)
        if w:
            where["wa"] = lax.rem(wa + (w + nw), nw)
        return where

    loads = []

    def load(src, dst):
        copy = pltpu.make_async_copy(src, dst, local_sem.at[len(loads)])
        copy.start()
        loads.append(copy)
        return copy

    get_coarse = load(coarse_hbm, cb)
    barrier = pltpu.get_barrier_semaphore()
    y_hi, core = ta // 2, lax.rem(ta, 2)
    by_z = [
        {"ta": 2 * y_hi + lax.rem(core + dc, 2), "ha": lax.rem(ha + dh, nh)}
        for dc in range(2) for dh in range(nh) if dc or dh
    ]
    by_xy = [
        {"ta": 2 * lax.rem(y_hi + dy, 2) + core, "wa": lax.rem(wa + dw, nw)}
        for dy in range(2) for dw in range(nw) if dy or dw
    ]
    stages = ((by_z, 0), (by_xy, len(by_z)))
    friends = by_z + by_xy + [near(t=-1), near(t=-1, w=1), near(t=-1, w=-1), near(t=-1, h=1), near(t=-1, h=-1)]
    for friend in friends:
        pl.semaphore_signal(barrier, inc=1, device_id=friend, device_id_type=MESH)
    get_cc = pltpu.make_async_copy(cache_coarse_hbm, cbp, local_sem.at[59])

    @pl.when(ta == 0)
    def _():
        get_cc.start()

    get_cm = load(cache_middle_hbm, cmb)
    get_cf = load(cache_fine_hbm, cfb)
    get_lk = load(lift_kernel, lk)
    get_w1 = [
        load(coarse_kernel.at[dt, dh, dw], w1.at[dt, (3 * dw + dh) * C : (3 * dw + dh + 1) * C])
        for dt in range(3) for dh in range(3) for dw in range(3)
    ]
    get_w3 = [
        load(fine_kernel.at[dt, dh], w3.at[3 * dt : 3 * dt + 3, (a + dh) * C : (a + dh + 1) * C, a * C1 : (a + 1) * C1])
        for dt in range(3) for dh in range(3) for a in range(2)
    ]
    get_affine = [load(ref, affine.at[i]) for i, ref in enumerate((coarse_gain, coarse_shift, fine_gain, fine_shift))]
    get_skip = [load(skip_kernel, skw.at[a * C : (a + 1) * C, a * C1 : (a + 1) * C1]) for a in range(2)]

    def message(index, src, dst, where, leaves=None):
        return pltpu.make_async_remote_copy(
            src_ref=src, dst_ref=dst, send_sem=send_sem.at[index if leaves is None else leaves], recv_sem=recv_sem.at[index],
            device_id=where, device_id_type=MESH,
        )

    center = message(0, coarse_hbm, cbp, near(t=1))
    cols_own = [
        message(1, xt.at[2:4, 8:10], xt.at[2:4, 0:2], near(w=1)),
        message(2, xt.at[2:4, 2:4], xt.at[2:4, 10:12], near(w=-1)),
    ]
    cols_next = [
        message(3, xt.at[2:4, 8:10], xt.at[0:2, 0:2], near(t=1, w=1)),
        message(4, xt.at[2:4, 2:4], xt.at[0:2, 10:12], near(t=1, w=-1)),
    ]
    cols_cached = [
        message(3, xt.at[0:2, 8:10], xt.at[0:2, 0:2], near(w=1), 18),
        message(4, xt.at[0:2, 2:4], xt.at[0:2, 10:12], near(w=-1), 19),
    ]
    rows_own = [
        message(9, ss.at[0, 2:4], sr.at[1, 2:4], near(h=-1)),
        message(10, ss.at[1, 2:4], sr.at[0, 2:4], near(h=1)),
    ]
    rows_next = [
        message(20, ss.at[0, 2:4], sr.at[1, 0:2], near(t=1, h=-1)),
        message(21, ss.at[1, 2:4], sr.at[0, 0:2], near(t=1, h=1)),
    ]
    rows_cached = [
        message(20, ss.at[0, 0:2], sr.at[1, 0:2], near(h=-1), 22),
        message(21, ss.at[1, 0:2], sr.at[0, 0:2], near(h=1), 23),
    ]

    pl.semaphore_wait(barrier, len(friends))

    @pl.when(ta < nt - 1)
    def _():
        center.start()

    def transpose_into(first_frame):
        for f in range(2):
            for c in range(8):
                cells = take(xf, f * 128 + c, 8)
                put(xtf, (first_frame + f) * 192 + (2 + c) * 16, cells)
                xt[first_frame + f, 2 + c] = cells.astype(BF16)

    get_coarse.wait()
    flat = cb[...].astype(F32)
    put(xf, 0, flat)
    transpose_into(2)
    for copy in cols_own:
        copy.start()

    @pl.when(ta < nt - 1)
    def _():
        for copy in cols_next:
            copy.start()

    count = flat.shape[0]
    mean = jnp.sum(flat, axis=0, keepdims=True) / count
    centred = flat - mean
    ar_src[0, 0] = jnp.zeros((8, C), F32)
    ar_src[0, 0, 0:1, :] = mean
    ar_src[0, 0, 1:2, :] = jnp.sum(centred * centred, axis=0, keepdims=True) / count

    def ar_copies(which, stage):
        peers, base = stages[stage]
        return [
            pltpu.make_async_remote_copy(
                src_ref=ar_src.at[which, stage], dst_ref=ar_recv.at[which, base + i],
                send_sem=ar_send.at[which, base + i], recv_sem=ar_got.at[which, base + i],
                device_id=peer, device_id_type=MESH,
            )
            for i, peer in enumerate(peers)
        ]

    def ar_start(which, stage):
        for copy in ar_copies(which, stage):
            copy.start()

    def ar_finish(which, stage):
        peers, base = stages[stage]
        n = len(peers) + 1
        for copy in ar_copies(which, stage):
            copy.wait_recv()
        tiles = [ar_src[which, stage]] + [ar_recv[which, base + i] for i in range(n - 1)]
        average = functools.reduce(jnp.add, tiles) / n
        spread = functools.reduce(jnp.add, [(tile - average) * (tile - average) for tile in tiles]) / n
        rows = lax.broadcasted_iota(jnp.int32, (8, C), 0)
        return average + jnp.where(rows == 1, pltpu.roll(spread, 1, 0), 0.0)

    def ar_next(which, stage):
        ar_src[which, stage + 1] = ar_finish(which, stage)
        ar_start(which, stage + 1)

    size = C // GROUPS
    width = xf.shape[-1]

    def group_mean(value):
        lane_of = lax.broadcasted_iota(jnp.int32, (8, width), 1)
        parts = []
        for part in range(C // width):
            x = jnp.broadcast_to(value[:, part * width : (part + 1) * width], (8, width))
            step = 1
            while step < size:
                x = x + jnp.where((lane_of & step) == 0, pltpu.roll(x, width - step, 1), pltpu.roll(x, step, 1))
                step *= 2
            parts.append(x[0:1])
        return jnp.concatenate(parts, axis=1) / size

    def normaliser(which, gain, shift):
        tile = ar_finish(which, 1)
        mean, variance = tile[0:1], tile[1:2]
        grouped = group_mean(mean)
        away = mean - grouped
        mean, variance = grouped, group_mean(variance + away * away)
        half_scale = 0.5 * (gain * lax.rsqrt(variance + EPS))
        half_shift = 0.5 * shift

        def act(x, mean=mean, half_scale=half_scale, half_shift=half_shift):
            half = (x - mean) * half_scale + half_shift
            return half + half * jnp.tanh(half)

        return act, mean, half_scale, half_shift

    ar_start(0, 0)

    @pl.when(ta == 0)
    def _():
        get_cc.wait()
        put(xf, 0, cbp[...].astype(F32))
        transpose_into(0)
        for copy in cols_cached:
            copy.start()

    cm_first = [
        message(5, cm.at[:, 8:9], cm.at[:, 0:1], near(w=1)),
        message(6, cm.at[:, 1:2], cm.at[:, 9:10], near(w=-1)),
    ]
    cf_first = [
        message(7, lt.at[:, 0:2, 8:9, :, 0:C], lt.at[:, 0:2, 0:1, :, 0:C], near(w=1)),
        message(8, lt.at[:, 0:2, 0:1, :, C : 2 * C], lt.at[:, 0:2, 8:9, :, C : 2 * C], near(w=-1)),
    ]
    cm_second = [
        message(11, cs.at[:, 0:1], cm.at[:, 11:12], near(h=-1)),
        message(12, cs.at[:, 1:2], cm.at[:, 10:11], near(h=1)),
    ]
    cf_second = [
        message(13, cfs.at[0], lt.at[0, 0:2, 9:10], near(h=-1)),
        message(14, cfs.at[1], lt.at[1, 0:2, 9:10], near(h=1)),
    ]

    get_cm.wait()

    @pl.when(ta < 2)
    def _():
        put(xf, 0, cmb[...].astype(F32))
        for f in range(2):
            for c in range(8):
                cm[f, 1 + c] = take(xf, f * 128 + c, 8).astype(BF16)
        for copy in cm_first:
            copy.start()

    for dt in range(3):
        for dw in range(3):
            w3[3 * dt + dw, 3 * C : 4 * C, 0:C1] = jnp.zeros((C, C1), BF16)
            w3[3 * dt + dw, 0:C, C1 : 2 * C1] = jnp.zeros((C, C1), BF16)
    skw[0:C, C1 : 2 * C1] = jnp.zeros((C, C1), BF16)
    skw[C : 2 * C, 0:C1] = jnp.zeros((C, C1), BF16)
    def widen(f, slots):
        for c in slots:
            put(xtf, f * 192 + c * 16, xt[f, c].astype(F32))

    def pick_rows(f):
        for side, rows in enumerate(((0, 1), (14, 15))):
            for k, row in enumerate(rows):
                ss[side, f, k] = take(xtf, f * 192 + row, 16).astype(BF16)

    for copy in cols_own:
        copy.wait_recv()
    for f in (2, 3):
        widen(f, (0, 1, 10, 11))
        pick_rows(f)
    for copy in rows_own:
        copy.start()

    @pl.when(ta < nt - 1)
    def _():
        for copy in rows_next:
            copy.start()

    @pl.when(ta == 0)
    def _():
        for copy in cols_cached:
            copy.wait_recv()
        for f in (0, 1):
            widen(f, (0, 1, 10, 11))
            pick_rows(f)
        for copy in rows_cached:
            copy.start()

    def fold(i, carry):
        dt, r = i // (C // 16), pl.multiple_of(lax.rem(i, C // 16) * 16, 16)
        taps = [[lk[dt, dh, dw, pl.ds(r, 16), :].astype(F32) for dw in range(3)] for dh in range(3)]
        for a in range(2):
            for k in range(2):
                if a == 0:
                    line = taps[0] if k == 0 else [taps[1][d] + taps[2][d] for d in range(3)]
                else:
                    line = [taps[0][d] + taps[1][d] for d in range(3)] if k == 0 else taps[2]
                wide = ((line[0] + line[1], line[2]), (line[0], line[1] + line[2]))
                for b in range(2):
                    for j in range(2):
                        w2[a, dt, pl.ds((2 * j + k) * C + r, 16), b * C : (b + 1) * C] = wide[b][j].astype(BF16)
        return carry

    get_lk.wait()
    ar_next(0, 0)
    lax.fori_loop(0, 3 * (C // 32), fold, 0)
    @pl.when(ta < 2)
    def _():
        for copy in cm_first:
            copy.wait_recv()
        for f in range(2):
            for c in range(10):
                put(gf, 16 * c, cm[f, c].astype(F32))
            cs[f, 0] = take(gf, 0, 16, half).astype(BF16)
            cs[f, 1] = take(gf, 15, 16, half).astype(BF16)
        for copy in cm_second:
            copy.start()

    @pl.when(ta > 0)
    def _():
        center.wait_recv()
        put(xf, 0, cbp[...].astype(F32))
        for f in range(2):
            for c in range(8):
                put(xtf, f * 192 + (2 + c) * 16, take(xf, f * 128 + c, 8))
        for copy in cols_next:
            copy.wait_recv()
        for f in (0, 1):
            widen(f, (0, 1, 10, 11))

    lax.fori_loop(3 * (C // 32), 3 * (C // 16), fold, 0)
    for copy in get_w1 + get_w3 + get_skip + get_affine:
        copy.wait()

    for copy in rows_own + rows_next:
        copy.wait_recv()
    act, *_ = normaliser(0, affine[0], affine[1])

    cols = lax.broadcasted_iota(jnp.int32, (16, C), 0)

    def strips_of(f):
        raw = jnp.logical_and(ta == 0, f < 2)
        for side in range(2):
            outside = first_h if side == 0 else last_h
            for k in range(2):
                x = sr[side, f, k].astype(F32)
                y = jnp.where(raw, x, act(x)) if f < 2 else act(x)
                gone = jnp.logical_or(jnp.logical_and(first_w, cols < 2), jnp.logical_and(last_w, cols >= 10))
                saf[f, side, k] = jnp.where(jnp.logical_or(outside, gone), 0.0, y)

    def act_coarse(f):
        strips_of(f)
        for c in range(12):
            at = f * 192 + c * 16
            x = take(xtf, at)
            x = jnp.where(ta == 0, x, act(x)) if f < 2 else act(x)
            if c < 2:
                x = jnp.where(first_w, 0.0, x)
            if c >= 10:
                x = jnp.where(last_w, 0.0, x)
            put(xtf, at, x)
            above = jnp.where(row16 == 0, saf[f, 0, 1, c : c + 1, :], rolled(x, 1))
            below = jnp.where(row16 == 15, saf[f, 1, 0, c : c + 1, :], rolled(x, -1))
            act_a[f, c, :, 0:C] = above.astype(BF16)
            act_a[f, c, :, C : 2 * C] = x.astype(BF16)
            act_a[f, c, :, 2 * C : 3 * C] = below.astype(BF16)
        top = take(xtf, f * 192, 16)
        bottom = take(xtf, f * 192 + 15, 16)
        for side, lines in enumerate(((saf[f, 0, 0], saf[f, 0, 1], top), (bottom, saf[f, 1, 0], saf[f, 1, 1]))):
            for dw in range(3):
                for dh in range(3):
                    act_a[f, 12 + 2 * dw + side, :, dh * C : (dh + 1) * C] = rolled(lines[dh], -dw).astype(BF16)

    def conv_coarse(f, g):
        lhs = jnp.concatenate(
            [
                jnp.concatenate([act_a[g, dw : dw + 10], act_a[g, 12 + 2 * dw : 14 + 2 * dw]], axis=0)
                for dw in range(3)
            ],
            axis=-1,
        ).reshape(12 * 16, 9 * C)
        part = jnp.dot(lhs, w1[g - f], preferred_element_type=F32).reshape(12, 16, C)
        acc1[f] = part if g == f else acc1[f] + part

    def finish_middle(f):
        for c in range(10):
            y = xt[2 + f, 1 + c].astype(F32) + acc1[f, c]
            if c == 0:
                y = jnp.where(first_w, 0.0, y)
            if c == 9:
                y = jnp.where(last_w, 0.0, y)
            mt[4 + f, c] = y.astype(BF16)
        gone = (cols > 9) | (first_w & (cols == 0)) | (last_w & (cols == 9))
        for side in range(2):
            y = rolled(sr[side, 2 + f, 1 - side].astype(F32), -1) + acc1[f, 10 + side]
            y = jnp.where(jnp.logical_or(gone, first_h if side == 0 else last_h), 0.0, y)
            mt[4 + f, 10 + side] = y.astype(BF16)

    to_next = [message(15 + f, mt.at[4 + f : 5 + f], mt.at[2 + f : 3 + f], near(t=1)) for f in range(2)]

    def send_middle(f):
        finish_middle(f)

        @pl.when(ta < nt - 1)
        def _():
            to_next[f].start()

    act_coarse(0)
    act_coarse(1)
    conv_coarse(0, 0)
    act_coarse(2)
    conv_coarse(0, 1)
    conv_coarse(0, 2)
    send_middle(0)
    act_coarse(3)
    for g in (1, 2, 3):
        conv_coarse(1, g)
    send_middle(1)

    to_second = message(17, mt.at[4:6], mt.at[0:2], near(t=2))
    by_second = message(17, mt.at[2:4], mt.at[0:2], near(t=1))

    def prepare(g):
        top = mt[g, 10].astype(F32)
        bottom = mt[g, 11].astype(F32)
        for c in range(10):
            x = mt[g, c].astype(F32)
            put(gf, 16 * c, x)
            mid_g[g, c, :, 0:C] = jnp.where(row16 == 0, top[c : c + 1], rolled(x, 1)).astype(BF16)
            mid_g[g, c, :, C : 2 * C] = mt[g, c]
            mid_g[g, c, :, 2 * C : 3 * C] = jnp.where(row16 == 15, bottom[c : c + 1], rolled(x, -1)).astype(BF16)
        row_top = take(gf, 0, 16, half)
        row_bottom = take(gf, 15, 16, half)
        for j in range(2):
            mid_g[g, 10 + j, :, 0:C] = rolled(row_bottom, -j).astype(BF16)
            mid_g[g, 10 + j, :, C : 2 * C] = rolled(bottom, -j).astype(BF16)
            mid_g[g, 12 + j, :, C : 2 * C] = rolled(top, -j).astype(BF16)
            mid_g[g, 12 + j, :, 2 * C : 3 * C] = rolled(row_top, -j).astype(BF16)

    def lift_part(a, dt, g, frames):
        lanes = slice(a * C, (a + 2) * C)
        lhs = jnp.concatenate(
            [
                jnp.concatenate(
                    [mid_g[g : g + frames, j : j + 9, :, lanes], mid_g[g : g + frames, 10 + 2 * a + j : 11 + 2 * a + j, :, lanes]],
                    axis=1,
                )
                for j in range(2)
            ],
            axis=-1,
        ).reshape(frames * 10 * 16, 4 * C)
        part = jnp.dot(lhs, w2[a, dt], preferred_element_type=F32)
        return part.reshape(frames, 10, 16, 2 * C)

    def cached_middle(at):
        gone = (cols > 9) | (first_w & (cols == 0)) | (last_w & (cols == 9))
        for f in range(2):
            mt[at + f, 1:9] = cm[f, 1:9]
            mt[at + f, 0] = jnp.where(first_w, 0.0, cm[f, 0].astype(F32)).astype(BF16)
            mt[at + f, 9] = jnp.where(last_w, 0.0, cm[f, 9].astype(F32)).astype(BF16)
            for side in range(2):
                outside = jnp.logical_or(gone, first_h if side == 0 else last_h)
                mt[at + f, 10 + side] = jnp.where(outside, 0.0, cm[f, 10 + side].astype(F32)).astype(BF16)

    prepare(4)
    prepare(5)
    for a in range(2):
        acc2[a] = lift_part(a, 2, 4, 2)
        acc2[a, 1:2] += lift_part(a, 1, 4, 1)

    @pl.when(ta == 0)
    def _():
        for copy in cm_second:
            copy.wait_recv()
        cached_middle(2)

    @pl.when(ta > 0)
    def _():
        for copy in to_next:
            copy.wait_recv()

    @pl.when(ta == 2)
    def _():
        by_second.start()

    prepare(2)
    prepare(3)
    for a in range(2):
        acc2[a] += lift_part(a, 0, 2, 2)
        acc2[a, 0:1] += lift_part(a, 1, 3, 1)
        lt[a, 2:4] = acc2[a].astype(BF16)

    @pl.when(ta == 0)
    def _():
        to_second.start()

    pivot = jnp.sum(lt[0, 2, 1, :, 0:C].astype(F32), axis=0, keepdims=True) / 16
    sums = jnp.zeros((16, C), F32)
    squares = jnp.zeros((16, C), F32)
    for a in range(2):
        for f in range(2):
            for p in range(9):
                for b in range(2):
                    if (p, b) not in ((0, 0), (8, 1)):
                        x = lt[a, 2 + f, p, :, b * C : (b + 1) * C].astype(F32) - pivot
                        sums = sums + x
                        squares = squares + x * x
    count = 2 * 2 * 16 * 16
    off = jnp.sum(sums, axis=0, keepdims=True) / count
    ar_src[1, 0] = jnp.zeros((8, C), F32)
    ar_src[1, 0, 0:1, :] = pivot + off
    ar_src[1, 0, 1:2, :] = jnp.maximum(jnp.sum(squares, axis=0, keepdims=True) / count - off * off, 0.0)
    ar_start(1, 0)

    def lift_before_new(a):
        acc2[a] = lift_part(a, 2, 2, 2)
        acc2[a, 1:2] += lift_part(a, 1, 2, 1)

    def lift_before_old(a):
        acc2[a] += lift_part(a, 0, 0, 2)
        lt[a, 0:1] = (acc2[a, 0:1] + lift_part(a, 1, 1, 1)).astype(BF16)
        lt[a, 1:2] = acc2[a, 1:2].astype(BF16)

    @pl.when(ta > 0)
    def _():
        lift_before_new(0)
        lift_before_new(1)

    get_cf.wait()

    @pl.when(ta == 0)
    def _():
        put(cff, 0, cfb[...].astype(F32))
        for f in range(2):
            for c in range(16):
                p, b = (c + 1) // 2, (c + 1) % 2
                for a in range(2):
                    lt[a, f, p, :, b * C : (b + 1) * C] = take(cff, f * 512 + a * 16 + c, 32).astype(BF16)
        for copy in cf_first:
            copy.start()

    ar_next(1, 0)

    @pl.when(ta == 0)
    def _():
        for copy in cf_first:
            copy.wait_recv()
        for f in range(2):
            for a, row in ((0, 0), (1, 15)):
                for p in range(9):
                    put(gf, 16 * p, lt[a, f, p].astype(F32))
                cfs[a, f, 0] = take(gf, row, 16).astype(BF16)
        for copy in cf_second:
            copy.start()

    for b in range(2):
        lhs = jnp.concatenate([lt[a, 2:4, 1 - b : 9 - b, :, b * C : (b + 1) * C] for a in range(2)], axis=-1)
        part = jnp.dot(lhs.reshape(2 * 8 * 16, 2 * C), skw[...], preferred_element_type=F32)
        acc3[:, :, 1 - b] = part.reshape(2, 8, 16, 2 * C1)

    @pl.when(ta == 1)
    def _():
        for copy in cm_second:
            copy.wait_recv()
        cached_middle(0)

    @pl.when(ta > 1)
    def _():
        to_second.wait_recv()

    @pl.when(ta > 0)
    def _():
        prepare(0)
        prepare(1)
        lift_before_old(0)
        lift_before_old(1)


    lane = lax.broadcasted_iota(jnp.int32, (16, 2 * C), 1)

    def spread_fine(f, fn):
        top = jnp.where(first_h, 0.0, fn(lt[1, f, 9].astype(F32)))
        bottom = jnp.where(last_h, 0.0, fn(lt[0, f, 9].astype(F32)))
        for p in range(9):
            even = fn(lt[0, f, p].astype(F32))
            odd = fn(lt[1, f, p].astype(F32))
            before = jnp.where(row16w == 0, top[p : p + 1], rolled(odd, 1))
            after = jnp.where(row16w == 15, bottom[p : p + 1], rolled(even, -1))
            for k, part in enumerate((before, even, odd, after)):
                if p == 0:
                    part = jnp.where(first_w & (lane < C), 0.0, part)
                if p == 8:
                    part = jnp.where(last_w & (lane >= C), 0.0, part)
                part = part.astype(BF16)
                for b in range(2):
                    lf[f, 2 * p + b, :, k * C : (k + 1) * C] = part[:, b * C : (b + 1) * C]

    @pl.when(ta == 0)
    def _():
        for copy in cf_second:
            copy.wait_recv()

    _, mean, half_scale, half_shift = normaliser(1, affine[2], affine[3])
    mean2 = jnp.concatenate([mean, mean], axis=1)
    scale2 = jnp.concatenate([half_scale, half_scale], axis=1)
    shift2 = jnp.concatenate([half_shift, half_shift], axis=1)

    def fine_act(x):
        half = (x - mean2) * scale2 + shift2
        return half + half * jnp.tanh(half)

    def fine_act_or_cached(x):
        return jnp.where(ta == 0, x, fine_act(x))

    def conv_fine(g):
        lhs = jnp.concatenate([lf[g, dw : dw + 16] for dw in range(3)], axis=-1).reshape(16 * 16, 12 * C)
        for f in range(2):
            dt = g - f
            if 0 <= dt <= 2:
                weights = w3[3 * dt : 3 * dt + 3].reshape(12 * C, 2 * C1)
                acc3[f] += jnp.dot(lhs, weights, preferred_element_type=F32).reshape(8, 2, 16, 2 * C1)

    def finish_fine(f):
        for c in range(16):
            for a in range(2):
                back[pl.ds(f * 512 + a * 16 + c, 16, stride=32), :] = acc3[f, c // 2, c % 2, :, a * C1 : (a + 1) * C1]
        outb[f * 512 : (f + 1) * 512] = back[f * 512 : (f + 1) * 512].astype(BF16)
        leave[f].start()

    leave = [
        pltpu.make_async_copy(outb.at[f * 512 : (f + 1) * 512], out_ref.at[f * 512 : (f + 1) * 512], local_sem.at[57 + f])
        for f in range(2)
    ]

    spread_fine(0, fine_act_or_cached)
    for g in range(4):
        if g < 3:
            spread_fine(g + 1, fine_act_or_cached if g + 1 < 2 else fine_act)
        conv_fine(g)
        if g >= 2:
            finish_fine(g - 2)

    for copy in leave:
        copy.wait()
    for which in range(2):
        for stage in range(2):
            for copy in ar_copies(which, stage):
                copy.wait_send()
    for copy in cols_own + rows_own:
        copy.wait_send()

    @pl.when(ta < 2)
    def _():
        for copy in cm_first + cm_second:
            copy.wait_send()

    @pl.when(ta == 0)
    def _():
        for copy in cols_cached + rows_cached + cf_first + cf_second:
            copy.wait_send()

    @pl.when(ta < nt - 1)
    def _():
        for copy in [center] + cols_next + rows_next + to_next:
            copy.wait_send()

    @pl.when(jnp.logical_or(ta == 0, ta == 2))
    def _():
        to_second.wait_send()


def local(
    sizes, coarse, cache_coarse, cache_middle, cache_fine, coarse_gain, coarse_shift, fine_gain, fine_shift,
    coarse_kernel, lift_kernel, fine_kernel, skip_kernel,
):
    nt, nh, nw, C, C1 = sizes
    frames, rows, cols, _ = coarse.shape
    assert (frames, rows, cols) == (2, 16, 8)
    peers = 2 * nh + 2 * nw - 2
    hbm = pl.BlockSpec(memory_space=pltpu.HBM)
    V = pltpu.VMEM
    W = min(128, C)
    L = C // W
    scratch = [
        V((4, 1, C), F32),
        V((256, C), BF16), V((256, C), BF16), V((256, C), BF16), V((1024, C), BF16),
        V((L, 256, W), F32), V((L, 1024, W), F32),
        V((4, 12, 16, C), BF16), V((L, 4 * 12 * 16 + 64, W), F32),
        V((2, 4, 2, 16, C), BF16), V((2, 4, 2, 16, C), BF16), V((4, 2, 2, 16, C), F32),
        V((4, 18, 16, 3 * C), BF16), V((2, 12, 16, C), F32),
        V((3, 9 * C, C), BF16), V((3, 3, 3, C, C), BF16), V((2, 3, 4 * C, 2 * C), BF16),
        V((9, 4 * C, 2 * C1), BF16), V((2 * C, 2 * C1), BF16),
        V((2, 12, 16, C), BF16), V((2, 2, 16, C), BF16), V((2, 2, 1, 16, 2 * C), BF16),
        V((6, 12, 16, C), BF16), V((6, 14, 16, 3 * C), BF16), V((2 * L, 256, W), F32),
        V((2, 2, 10, 16, 2 * C), F32), V((2, 4, 10, 16, 2 * C), BF16),
        V((4, 18, 16, 4 * C), BF16), V((2, 8, 2, 16, 2 * C1), F32), V((1024, C1), F32), V((1024, C1), BF16),
        V((2, 2, 8, C), F32), V((2, peers, 8, C), F32),
        pltpu.SemaphoreType.DMA((60,)),
        pltpu.SemaphoreType.DMA((2, peers)), pltpu.SemaphoreType.DMA((2, peers)),
        pltpu.SemaphoreType.DMA((24,)), pltpu.SemaphoreType.DMA((24,)),
    ]
    decoded = pl.pallas_call(
        functools.partial(body, sizes),
        out_shape=jax.ShapeDtypeStruct((1024, C1), BF16),
        in_specs=[hbm] * 12,
        out_specs=hbm,
        scratch_shapes=scratch,
        compiler_params=pltpu.CompilerParams(
            collective_id=0, has_side_effects=True, vmem_limit_bytes=63 * 1024 * 1024
        ),
    )(
        coarse.reshape(256, C), cache_coarse.reshape(256, C), cache_middle.reshape(256, C), cache_fine.reshape(1024, C),
        coarse_gain.reshape(1, C), coarse_shift.reshape(1, C), fine_gain.reshape(1, C), fine_shift.reshape(1, C),
        coarse_kernel, lift_kernel, fine_kernel, skip_kernel,
    )
    return decoded.reshape(2, 32, 16, C1)


def solution(mesh):
    def run(*args):
        channels, outer = args[-1].shape
        sizes = (mesh.shape["ta"], mesh.shape["ha"], mesh.shape["wa"], channels, outer)
        return jax.shard_map(
            functools.partial(local, sizes),
            mesh=mesh,
            in_specs=(P("ta", "ha", "wa", None),) + (P(None, "ha", "wa", None),) * 3 + (P(),) * 8,
            out_specs=P("ta", "ha", "wa", None),
            check_vma=False,
        )(*args)

    return run
```

```python
import functools

import jax
import jax.numpy as jnp
from jax import lax
from jax.experimental import pallas as pl
from jax.experimental.pallas import tpu as pltpu
from jax.sharding import PartitionSpec as P

GROUPS = 32
EPS = 1e-06
MESH = pl.DeviceIdType.MESH
F32 = jnp.float32
BF16 = jnp.bfloat16


def rolled(value, shift):
    size = value.shape[0]
    shift = shift % size
    return value if shift == 0 else pltpu.roll(value, shift, 0)


def put(ref, start, value):
    width = ref.shape[-1]
    for part in range(value.shape[1] // width):
        ref[part, pl.ds(start, value.shape[0]), :] = value[:, part * width : (part + 1) * width]


def take(ref, start, stride=1, parts=None):
    at = pl.ds(start, 16) if stride == 1 else pl.ds(start, 16, stride=stride)
    return jnp.concatenate([ref[part, at, :] for part in range(parts or ref.shape[0])], axis=1)


def body(
    sizes,
    coarse_hbm, cache_coarse_hbm, cache_middle_hbm, cache_fine_hbm,
    coarse_gain, coarse_shift, fine_gain, fine_shift,
    coarse_kernel, lift_kernel, fine_kernel, skip_kernel,
    out_ref, affine,
    cb, cbp, cmb, cfb, xf, cff, xt, xtf, ss, sr, saf, act_a, acc1, w1, lk, w2, w3, skw,
    cm, cs, cfs, mt, mid_g, gf, acc2, lt, lf, acc3, back, outb, ar_src, ar_recv,
    local_sem, ar_send, ar_got, send_sem, recv_sem,
):
    nt, nh, nw, C, C1 = sizes
    half = gf.shape[0] // 2
    ta, ha, wa = lax.axis_index("ta"), lax.axis_index("ha"), lax.axis_index("wa")
    row16 = lax.broadcasted_iota(jnp.int32, (16, C), 0)
    row16w = lax.broadcasted_iota(jnp.int32, (16, 2 * C), 0)
    first_w, last_w, first_h, last_h = wa == 0, wa == nw - 1, ha == 0, ha == nh - 1

    def near(t=0, h=0, w=0):
        where = {}
        if t:
            where["ta"] = lax.rem(ta + (t + nt), nt)
        if h:
            where["ha"] = lax.rem(ha + (h + nh), nh)
        if w:
            where["wa"] = lax.rem(wa + (w + nw), nw)
        return where

    loads = []

    def load(src, dst):
        copy = pltpu.make_async_copy(src, dst, local_sem.at[len(loads)])
        copy.start()
        loads.append(copy)
        return copy

    get_coarse = load(coarse_hbm, cb)
    barrier = pltpu.get_barrier_semaphore()
    y_hi, core = ta // 2, lax.rem(ta, 2)
    by_z = [
        {"ta": 2 * y_hi + lax.rem(core + dc, 2), "ha": lax.rem(ha + dh, nh)}
        for dc in range(2) for dh in range(nh) if dc or dh
    ]
    by_xy = [
        {"ta": 2 * lax.rem(y_hi + dy, 2) + core, "wa": lax.rem(wa + dw, nw)}
        for dy in range(2) for dw in range(nw) if dy or dw
    ]
    stages = ((by_z, 0), (by_xy, len(by_z)))
    friends = by_z + by_xy + [near(t=-1), near(t=-1, w=1), near(t=-1, w=-1), near(t=-1, h=1), near(t=-1, h=-1)]
    for friend in friends:
        pl.semaphore_signal(barrier, inc=1, device_id=friend, device_id_type=MESH)
    get_cc = pltpu.make_async_copy(cache_coarse_hbm, cbp, local_sem.at[59])

    @pl.when(ta == 0)
    def _():
        get_cc.start()

    get_lk = load(lift_kernel, lk)

    def message(index, src, dst, where, leaves=None):
        return pltpu.make_async_remote_copy(
            src_ref=src, dst_ref=dst, send_sem=send_sem.at[index if leaves is None else leaves], recv_sem=recv_sem.at[index],
            device_id=where, device_id_type=MESH,
        )

    center = message(0, coarse_hbm, cbp, near(t=1))
    cols_own = [
        message(1, xt.at[2:4, 8:10], xt.at[2:4, 0:2], near(w=1)),
        message(2, xt.at[2:4, 2:4], xt.at[2:4, 10:12], near(w=-1)),
    ]
    cols_next = [
        message(3, xt.at[2:4, 8:10], xt.at[0:2, 0:2], near(t=1, w=1)),
        message(4, xt.at[2:4, 2:4], xt.at[0:2, 10:12], near(t=1, w=-1)),
    ]
    cols_cached = [
        message(3, xt.at[0:2, 8:10], xt.at[0:2, 0:2], near(w=1), 18),
        message(4, xt.at[0:2, 2:4], xt.at[0:2, 10:12], near(w=-1), 19),
    ]
    rows_own = [
        message(9, ss.at[0, 2:4], sr.at[1, 2:4], near(h=-1)),
        message(10, ss.at[1, 2:4], sr.at[0, 2:4], near(h=1)),
    ]
    rows_next = [
        message(20, ss.at[0, 2:4], sr.at[1, 0:2], near(t=1, h=-1)),
        message(21, ss.at[1, 2:4], sr.at[0, 0:2], near(t=1, h=1)),
    ]
    rows_cached = [
        message(20, ss.at[0, 0:2], sr.at[1, 0:2], near(h=-1), 22),
        message(21, ss.at[1, 0:2], sr.at[0, 0:2], near(h=1), 23),
    ]

    pl.semaphore_wait(barrier, len(friends))

    @pl.when(ta < nt - 1)
    def _():
        center.start()

    def transpose_into(first_frame):
        for f in range(2):
            for c in range(8):
                cells = take(xf, f * 128 + c, 8)
                put(xtf, (first_frame + f) * 192 + (2 + c) * 16, cells)
                xt[first_frame + f, 2 + c] = cells.astype(BF16)

    get_coarse.wait()
    flat = cb[...].astype(F32)
    put(xf, 0, flat)
    transpose_into(2)
    for copy in cols_own:
        copy.start()

    @pl.when(ta < nt - 1)
    def _():
        for copy in cols_next:
            copy.start()

    count = flat.shape[0]
    mean = jnp.sum(flat, axis=0, keepdims=True) / count
    centred = flat - mean
    ar_src[0, 0] = jnp.zeros((8, C), F32)
    ar_src[0, 0, 0:1, :] = mean
    ar_src[0, 0, 1:2, :] = jnp.sum(centred * centred, axis=0, keepdims=True) / count

    def ar_copies(which, stage):
        peers, base = stages[stage]
        return [
            pltpu.make_async_remote_copy(
                src_ref=ar_src.at[which, stage], dst_ref=ar_recv.at[which, base + i],
                send_sem=ar_send.at[which, base + i], recv_sem=ar_got.at[which, base + i],
                device_id=peer, device_id_type=MESH,
            )
            for i, peer in enumerate(peers)
        ]

    def ar_start(which, stage):
        for copy in ar_copies(which, stage):
            copy.start()

    def ar_finish(which, stage):
        peers, base = stages[stage]
        n = len(peers) + 1
        for copy in ar_copies(which, stage):
            copy.wait_recv()
        tiles = [ar_src[which, stage]] + [ar_recv[which, base + i] for i in range(n - 1)]
        average = functools.reduce(jnp.add, tiles) / n
        spread = functools.reduce(jnp.add, [(tile - average) * (tile - average) for tile in tiles]) / n
        rows = lax.broadcasted_iota(jnp.int32, (8, C), 0)
        return average + jnp.where(rows == 1, pltpu.roll(spread, 1, 0), 0.0)

    def ar_next(which, stage):
        ar_src[which, stage + 1] = ar_finish(which, stage)
        ar_start(which, stage + 1)

    size = C // GROUPS
    width = xf.shape[-1]

    def group_mean(value):
        lane_of = lax.broadcasted_iota(jnp.int32, (8, width), 1)
        parts = []
        for part in range(C // width):
            x = jnp.broadcast_to(value[:, part * width : (part + 1) * width], (8, width))
            step = 1
            while step < size:
                x = x + jnp.where((lane_of & step) == 0, pltpu.roll(x, width - step, 1), pltpu.roll(x, step, 1))
                step *= 2
            parts.append(x[0:1])
        return jnp.concatenate(parts, axis=1) / size

    def normaliser(which, gain, shift):
        tile = ar_finish(which, 1)
        mean, variance = tile[0:1], tile[1:2]
        grouped = group_mean(mean)
        away = mean - grouped
        mean, variance = grouped, group_mean(variance + away * away)
        half_scale = 0.5 * (gain * lax.rsqrt(variance + EPS))
        half_shift = 0.5 * shift

        def act(x, mean=mean, half_scale=half_scale, half_shift=half_shift):
            half = (x - mean) * half_scale + half_shift
            return half + half * jnp.tanh(half)

        return act, mean, half_scale, half_shift

    ar_start(0, 0)
    get_cm = load(cache_middle_hbm, cmb)
    get_w1 = load(coarse_kernel, w1)
    get_affine = [load(ref, affine.at[i]) for i, ref in enumerate((coarse_gain, coarse_shift, fine_gain, fine_shift))]
    get_w3 = [load(fine_kernel, w3.at[:, a : a + 3, :, :, a * C1 : (a + 1) * C1]) for a in range(2)]
    get_skip = [load(skip_kernel, skw.at[a * C : (a + 1) * C, a * C1 : (a + 1) * C1]) for a in range(2)]
    get_cf = load(cache_fine_hbm, cfb)

    @pl.when(ta == 0)
    def _():
        get_cc.wait()
        put(xf, 0, cbp[...].astype(F32))
        transpose_into(0)
        for copy in cols_cached:
            copy.start()

    cm_first = [
        message(5, cm.at[:, 8:9], cm.at[:, 0:1], near(w=1)),
        message(6, cm.at[:, 1:2], cm.at[:, 9:10], near(w=-1)),
    ]
    cf_first = [
        message(7, lt.at[:, 0:2, 8:9, :, 0:C], lt.at[:, 0:2, 0:1, :, 0:C], near(w=1)),
        message(8, lt.at[:, 0:2, 0:1, :, C : 2 * C], lt.at[:, 0:2, 8:9, :, C : 2 * C], near(w=-1)),
    ]
    cm_second = [
        message(11, cs.at[:, 0:1], cm.at[:, 11:12], near(h=-1)),
        message(12, cs.at[:, 1:2], cm.at[:, 10:11], near(h=1)),
    ]
    cf_second = [
        message(13, cfs.at[0], lt.at[0, 0:2, 9:10], near(h=-1)),
        message(14, cfs.at[1], lt.at[1, 0:2, 9:10], near(h=1)),
    ]

    get_cm.wait()

    @pl.when(ta < 2)
    def _():
        put(xf, 0, cmb[...].astype(F32))
        for f in range(2):
            for c in range(8):
                cm[f, 1 + c] = take(xf, f * 128 + c, 8).astype(BF16)
        for copy in cm_first:
            copy.start()

    for dt in range(3):
        for dw in range(3):
            w3[dt, 3, dw, :, 0:C1] = jnp.zeros((C, C1), BF16)
            w3[dt, 0, dw, :, C1 : 2 * C1] = jnp.zeros((C, C1), BF16)
    skw[0:C, C1 : 2 * C1] = jnp.zeros((C, C1), BF16)
    skw[C : 2 * C, 0:C1] = jnp.zeros((C, C1), BF16)
    def widen(f, slots):
        for c in slots:
            put(xtf, f * 192 + c * 16, xt[f, c].astype(F32))

    def pick_rows(f):
        for side, rows in enumerate(((0, 1), (14, 15))):
            for k, row in enumerate(rows):
                ss[side, f, k] = take(xtf, f * 192 + row, 16).astype(BF16)

    for copy in cols_own:
        copy.wait_recv()
    for f in (2, 3):
        widen(f, (0, 1, 10, 11))
        pick_rows(f)
    for copy in rows_own:
        copy.start()

    @pl.when(ta < nt - 1)
    def _():
        for copy in rows_next:
            copy.start()

    @pl.when(ta == 0)
    def _():
        for copy in cols_cached:
            copy.wait_recv()
        for f in (0, 1):
            widen(f, (0, 1, 10, 11))
            pick_rows(f)
        for copy in rows_cached:
            copy.start()

    def fold(i, carry):
        dt, r = i // (C // 16), pl.multiple_of(lax.rem(i, C // 16) * 16, 16)
        taps = [[lk[dt, dh, dw, pl.ds(r, 16), :].astype(F32) for dw in range(3)] for dh in range(3)]
        for a in range(2):
            for k in range(2):
                if a == 0:
                    line = taps[0] if k == 0 else [taps[1][d] + taps[2][d] for d in range(3)]
                else:
                    line = [taps[0][d] + taps[1][d] for d in range(3)] if k == 0 else taps[2]
                wide = ((line[0] + line[1], line[2]), (line[0], line[1] + line[2]))
                for b in range(2):
                    for j in range(2):
                        w2[a, dt, pl.ds((2 * j + k) * C + r, 16), b * C : (b + 1) * C] = wide[b][j].astype(BF16)
        return carry

    get_lk.wait()
    ar_next(0, 0)
    lax.fori_loop(0, 3 * (C // 32), fold, 0)
    @pl.when(ta < 2)
    def _():
        for copy in cm_first:
            copy.wait_recv()
        for f in range(2):
            for c in range(10):
                put(gf, 16 * c, cm[f, c].astype(F32))
            cs[f, 0] = take(gf, 0, 16, half).astype(BF16)
            cs[f, 1] = take(gf, 15, 16, half).astype(BF16)
        for copy in cm_second:
            copy.start()

    @pl.when(ta > 0)
    def _():
        center.wait_recv()
        put(xf, 0, cbp[...].astype(F32))
        for f in range(2):
            for c in range(8):
                put(xtf, f * 192 + (2 + c) * 16, take(xf, f * 128 + c, 8))
        for copy in cols_next:
            copy.wait_recv()
        for f in (0, 1):
            widen(f, (0, 1, 10, 11))

    lax.fori_loop(3 * (C // 32), 3 * (C // 16), fold, 0)
    for copy in [get_w1] + get_affine:
        copy.wait()

    for copy in rows_own + rows_next:
        copy.wait_recv()
    act, *_ = normaliser(0, affine[0], affine[1])

    cols = lax.broadcasted_iota(jnp.int32, (16, C), 0)

    def strips_of(f):
        raw = jnp.logical_and(ta == 0, f < 2)
        for side in range(2):
            outside = first_h if side == 0 else last_h
            for k in range(2):
                x = sr[side, f, k].astype(F32)
                y = jnp.where(raw, x, act(x)) if f < 2 else act(x)
                gone = jnp.logical_or(jnp.logical_and(first_w, cols < 2), jnp.logical_and(last_w, cols >= 10))
                saf[f, side, k] = jnp.where(jnp.logical_or(outside, gone), 0.0, y)

    def act_coarse(f):
        strips_of(f)
        for c in range(12):
            at = f * 192 + c * 16
            x = take(xtf, at)
            x = jnp.where(ta == 0, x, act(x)) if f < 2 else act(x)
            if c < 2:
                x = jnp.where(first_w, 0.0, x)
            if c >= 10:
                x = jnp.where(last_w, 0.0, x)
            put(xtf, at, x)
            above = jnp.where(row16 == 0, saf[f, 0, 1, c : c + 1, :], rolled(x, 1))
            below = jnp.where(row16 == 15, saf[f, 1, 0, c : c + 1, :], rolled(x, -1))
            act_a[f, c, :, 0:C] = above.astype(BF16)
            act_a[f, c, :, C : 2 * C] = x.astype(BF16)
            act_a[f, c, :, 2 * C : 3 * C] = below.astype(BF16)
        top = take(xtf, f * 192, 16)
        bottom = take(xtf, f * 192 + 15, 16)
        for side, lines in enumerate(((saf[f, 0, 0], saf[f, 0, 1], top), (bottom, saf[f, 1, 0], saf[f, 1, 1]))):
            for dw in range(3):
                for dh in range(3):
                    act_a[f, 12 + 2 * dw + side, :, dh * C : (dh + 1) * C] = rolled(lines[dh], -dw).astype(BF16)

    def conv_coarse(f, g):
        lhs = jnp.concatenate(
            [
                jnp.concatenate([act_a[g, dw : dw + 10, :, lanes], act_a[g, 12 + 2 * dw : 14 + 2 * dw, :, lanes]], axis=0)
                for lanes in (slice(0, C), slice(C, 2 * C), slice(2 * C, 3 * C))
                for dw in range(3)
            ],
            axis=-1,
        ).reshape(12 * 16, 9 * C)
        part = jnp.dot(lhs, w1[g - f].reshape(9 * C, C), preferred_element_type=F32).reshape(12, 16, C)
        acc1[f] = part if g == f else acc1[f] + part

    def finish_middle(f):
        for c in range(10):
            y = xt[2 + f, 1 + c].astype(F32) + acc1[f, c]
            if c == 0:
                y = jnp.where(first_w, 0.0, y)
            if c == 9:
                y = jnp.where(last_w, 0.0, y)
            mt[4 + f, c] = y.astype(BF16)
        gone = (cols > 9) | (first_w & (cols == 0)) | (last_w & (cols == 9))
        for side in range(2):
            y = rolled(sr[side, 2 + f, 1 - side].astype(F32), -1) + acc1[f, 10 + side]
            y = jnp.where(jnp.logical_or(gone, first_h if side == 0 else last_h), 0.0, y)
            mt[4 + f, 10 + side] = y.astype(BF16)

    to_next = [message(15 + f, mt.at[4 + f : 5 + f], mt.at[2 + f : 3 + f], near(t=1)) for f in range(2)]

    def send_middle(f):
        finish_middle(f)

        @pl.when(ta < nt - 1)
        def _():
            to_next[f].start()

    act_coarse(0)
    act_coarse(1)
    conv_coarse(0, 0)
    act_coarse(2)
    conv_coarse(0, 1)
    conv_coarse(0, 2)
    send_middle(0)
    act_coarse(3)
    for g in (1, 2, 3):
        conv_coarse(1, g)
    send_middle(1)

    to_second = message(17, mt.at[4:6], mt.at[0:2], near(t=2))
    by_second = message(17, mt.at[2:4], mt.at[0:2], near(t=1))

    def prepare(g):
        top = mt[g, 10].astype(F32)
        bottom = mt[g, 11].astype(F32)
        for c in range(10):
            x = mt[g, c].astype(F32)
            put(gf, 16 * c, x)
            mid_g[g, c, :, 0:C] = jnp.where(row16 == 0, top[c : c + 1], rolled(x, 1)).astype(BF16)
            mid_g[g, c, :, C : 2 * C] = mt[g, c]
            mid_g[g, c, :, 2 * C : 3 * C] = jnp.where(row16 == 15, bottom[c : c + 1], rolled(x, -1)).astype(BF16)
        row_top = take(gf, 0, 16, half)
        row_bottom = take(gf, 15, 16, half)
        for j in range(2):
            mid_g[g, 10 + j, :, 0:C] = rolled(row_bottom, -j).astype(BF16)
            mid_g[g, 10 + j, :, C : 2 * C] = rolled(bottom, -j).astype(BF16)
            mid_g[g, 12 + j, :, C : 2 * C] = rolled(top, -j).astype(BF16)
            mid_g[g, 12 + j, :, 2 * C : 3 * C] = rolled(row_top, -j).astype(BF16)

    def lift_part(a, dt, g, frames):
        lanes = slice(a * C, (a + 2) * C)
        lhs = jnp.concatenate(
            [
                jnp.concatenate(
                    [mid_g[g : g + frames, j : j + 9, :, lanes], mid_g[g : g + frames, 10 + 2 * a + j : 11 + 2 * a + j, :, lanes]],
                    axis=1,
                )
                for j in range(2)
            ],
            axis=-1,
        ).reshape(frames * 10 * 16, 4 * C)
        part = jnp.dot(lhs, w2[a, dt], preferred_element_type=F32)
        return part.reshape(frames, 10, 16, 2 * C)

    def cached_middle(at):
        gone = (cols > 9) | (first_w & (cols == 0)) | (last_w & (cols == 9))
        for f in range(2):
            mt[at + f, 1:9] = cm[f, 1:9]
            mt[at + f, 0] = jnp.where(first_w, 0.0, cm[f, 0].astype(F32)).astype(BF16)
            mt[at + f, 9] = jnp.where(last_w, 0.0, cm[f, 9].astype(F32)).astype(BF16)
            for side in range(2):
                outside = jnp.logical_or(gone, first_h if side == 0 else last_h)
                mt[at + f, 10 + side] = jnp.where(outside, 0.0, cm[f, 10 + side].astype(F32)).astype(BF16)

    for copy in get_w3 + get_skip + [get_cf]:
        copy.wait()
    prepare(4)
    prepare(5)
    for a in range(2):
        acc2[a] = lift_part(a, 2, 4, 2)
        acc2[a, 1:2] += lift_part(a, 1, 4, 1)

    @pl.when(ta == 0)
    def _():
        for copy in cm_second:
            copy.wait_recv()
        cached_middle(2)
        put(cff, 0, cfb[...].astype(F32))
        for f in range(2):
            for c in range(16):
                p, b = (c + 1) // 2, (c + 1) % 2
                for a in range(2):
                    lt[a, f, p, :, b * C : (b + 1) * C] = take(cff, f * 512 + a * 16 + c, 32).astype(BF16)
        for copy in cf_first:
            copy.start()

    @pl.when(ta > 0)
    def _():
        for copy in to_next:
            copy.wait_recv()

    @pl.when(ta == 2)
    def _():
        by_second.start()

    prepare(2)
    prepare(3)
    for a in range(2):
        acc2[a] += lift_part(a, 0, 2, 2)
        acc2[a, 0:1] += lift_part(a, 1, 3, 1)
        lt[a, 2:4] = acc2[a].astype(BF16)

    @pl.when(ta == 0)
    def _():
        to_second.start()

    pivot = jnp.sum(lt[0, 2, 1, :, 0:C].astype(F32), axis=0, keepdims=True) / 16
    sums = jnp.zeros((16, C), F32)
    squares = jnp.zeros((16, C), F32)
    for a in range(2):
        for f in range(2):
            for p in range(9):
                for b in range(2):
                    if (p, b) not in ((0, 0), (8, 1)):
                        x = lt[a, 2 + f, p, :, b * C : (b + 1) * C].astype(F32) - pivot
                        sums = sums + x
                        squares = squares + x * x
    count = 2 * 2 * 16 * 16
    off = jnp.sum(sums, axis=0, keepdims=True) / count
    ar_src[1, 0] = jnp.zeros((8, C), F32)
    ar_src[1, 0, 0:1, :] = pivot + off
    ar_src[1, 0, 1:2, :] = jnp.maximum(jnp.sum(squares, axis=0, keepdims=True) / count - off * off, 0.0)
    ar_start(1, 0)

    def lift_before_new(a):
        acc2[a] = lift_part(a, 2, 2, 2)

    def lift_before_old(a):
        acc2[a] += lift_part(a, 0, 0, 2)
        lt[a, 0:2] = (acc2[a] + lift_part(a, 1, 1, 2)).astype(BF16)

    @pl.when(ta > 0)
    def _():
        lift_before_new(0)
        lift_before_new(1)

    @pl.when(ta == 0)
    def _():
        for copy in cf_first:
            copy.wait_recv()
        for f in range(2):
            for a, row in ((0, 0), (1, 15)):
                for p in range(9):
                    put(gf, 16 * p, lt[a, f, p].astype(F32))
                cfs[a, f, 0] = take(gf, row, 16).astype(BF16)
        for copy in cf_second:
            copy.start()

    ar_next(1, 0)

    for b in range(2):
        lhs = jnp.concatenate([lt[a, 2:4, 1 - b : 9 - b, :, b * C : (b + 1) * C] for a in range(2)], axis=-1)
        part = jnp.dot(lhs.reshape(2 * 8 * 16, 2 * C), skw[...], preferred_element_type=F32)
        acc3[:, :, 1 - b] = part.reshape(2, 8, 16, 2 * C1)

    @pl.when(ta == 1)
    def _():
        for copy in cm_second:
            copy.wait_recv()
        cached_middle(0)

    @pl.when(ta > 1)
    def _():
        to_second.wait_recv()

    @pl.when(ta > 0)
    def _():
        prepare(0)
        prepare(1)
        lift_before_old(0)
        lift_before_old(1)


    lane = lax.broadcasted_iota(jnp.int32, (16, 2 * C), 1)

    def spread_fine(f, fn):
        top = jnp.where(first_h, 0.0, fn(lt[1, f, 9].astype(F32)))
        bottom = jnp.where(last_h, 0.0, fn(lt[0, f, 9].astype(F32)))
        for p in range(9):
            even = fn(lt[0, f, p].astype(F32))
            odd = fn(lt[1, f, p].astype(F32))
            before = jnp.where(row16w == 0, top[p : p + 1], rolled(odd, 1))
            after = jnp.where(row16w == 15, bottom[p : p + 1], rolled(even, -1))
            for k, part in enumerate((before, even, odd, after)):
                if p == 0:
                    part = jnp.where(first_w & (lane < C), 0.0, part)
                if p == 8:
                    part = jnp.where(last_w & (lane >= C), 0.0, part)
                part = part.astype(BF16)
                for b in range(2):
                    lf[f, 2 * p + b, :, k * C : (k + 1) * C] = part[:, b * C : (b + 1) * C]

    @pl.when(ta == 0)
    def _():
        for copy in cf_second:
            copy.wait_recv()

    _, mean, half_scale, half_shift = normaliser(1, affine[2], affine[3])
    mean2 = jnp.concatenate([mean, mean], axis=1)
    scale2 = jnp.concatenate([half_scale, half_scale], axis=1)
    shift2 = jnp.concatenate([half_shift, half_shift], axis=1)

    def fine_act(x):
        half = (x - mean2) * scale2 + shift2
        return half + half * jnp.tanh(half)

    def fine_act_or_cached(x):
        return jnp.where(ta == 0, x, fine_act(x))

    def conv_fine(dt):
        lhs = jnp.concatenate(
            [lf[dt : dt + 2, dw : dw + 16, :, k * C : (k + 1) * C] for k in range(4) for dw in range(3)], axis=-1
        ).reshape(2 * 16 * 16, 12 * C)
        part = jnp.dot(lhs, w3[dt].reshape(12 * C, 2 * C1), preferred_element_type=F32)
        acc3[...] += part.reshape(2, 8, 2, 16, 2 * C1)

    def finish_fine(f):
        for c in range(16):
            for a in range(2):
                back[pl.ds(f * 512 + a * 16 + c, 16, stride=32), :] = acc3[f, c // 2, c % 2, :, a * C1 : (a + 1) * C1]
        outb[f * 512 : (f + 1) * 512] = back[f * 512 : (f + 1) * 512].astype(BF16)
        leave[f].start()

    leave = [
        pltpu.make_async_copy(outb.at[f * 512 : (f + 1) * 512], out_ref.at[f * 512 : (f + 1) * 512], local_sem.at[57 + f])
        for f in range(2)
    ]

    spread_fine(0, fine_act_or_cached)
    spread_fine(1, fine_act_or_cached)
    spread_fine(2, fine_act)
    conv_fine(0)
    spread_fine(3, fine_act)
    conv_fine(1)
    conv_fine(2)
    finish_fine(0)
    finish_fine(1)

    for copy in leave:
        copy.wait()
    for which in range(2):
        for stage in range(2):
            for copy in ar_copies(which, stage):
                copy.wait_send()
    for copy in cols_own + rows_own:
        copy.wait_send()

    @pl.when(ta < 2)
    def _():
        for copy in cm_first + cm_second:
            copy.wait_send()

    @pl.when(ta == 0)
    def _():
        for copy in cols_cached + rows_cached + cf_first + cf_second:
            copy.wait_send()

    @pl.when(ta < nt - 1)
    def _():
        for copy in [center] + cols_next + rows_next + to_next:
            copy.wait_send()

    @pl.when(jnp.logical_or(ta == 0, ta == 2))
    def _():
        to_second.wait_send()


def local(
    sizes, coarse, cache_coarse, cache_middle, cache_fine, coarse_gain, coarse_shift, fine_gain, fine_shift,
    coarse_kernel, lift_kernel, fine_kernel, skip_kernel,
):
    nt, nh, nw, C, C1 = sizes
    frames, rows, cols, _ = coarse.shape
    assert (frames, rows, cols) == (2, 16, 8)
    peers = 2 * nh + 2 * nw - 2
    hbm = pl.BlockSpec(memory_space=pltpu.HBM)
    V = pltpu.VMEM
    W = min(128, C)
    L = C // W
    scratch = [
        V((4, 1, C), F32),
        V((256, C), BF16), V((256, C), BF16), V((256, C), BF16), V((1024, C), BF16),
        V((L, 256, W), F32), V((L, 1024, W), F32),
        V((4, 12, 16, C), BF16), V((L, 4 * 12 * 16 + 64, W), F32),
        V((2, 4, 2, 16, C), BF16), V((2, 4, 2, 16, C), BF16), V((4, 2, 2, 16, C), F32),
        V((4, 18, 16, 3 * C), BF16), V((2, 12, 16, C), F32),
        V((3, 3, 3, C, C), BF16), V((3, 3, 3, C, C), BF16), V((2, 3, 4 * C, 2 * C), BF16),
        V((3, 4, 3, C, 2 * C1), BF16), V((2 * C, 2 * C1), BF16),
        V((2, 12, 16, C), BF16), V((2, 2, 16, C), BF16), V((2, 2, 1, 16, 2 * C), BF16),
        V((6, 12, 16, C), BF16), V((6, 14, 16, 3 * C), BF16), V((2 * L, 256, W), F32),
        V((2, 2, 10, 16, 2 * C), F32), V((2, 4, 10, 16, 2 * C), BF16),
        V((4, 18, 16, 4 * C), BF16), V((2, 8, 2, 16, 2 * C1), F32), V((1024, C1), F32), V((1024, C1), BF16),
        V((2, 2, 8, C), F32), V((2, peers, 8, C), F32),
        pltpu.SemaphoreType.DMA((60,)),
        pltpu.SemaphoreType.DMA((2, peers)), pltpu.SemaphoreType.DMA((2, peers)),
        pltpu.SemaphoreType.DMA((24,)), pltpu.SemaphoreType.DMA((24,)),
    ]
    decoded = pl.pallas_call(
        functools.partial(body, sizes),
        out_shape=jax.ShapeDtypeStruct((1024, C1), BF16),
        in_specs=[hbm] * 12,
        out_specs=hbm,
        scratch_shapes=scratch,
        compiler_params=pltpu.CompilerParams(
            collective_id=0, has_side_effects=True, vmem_limit_bytes=63 * 1024 * 1024
        ),
    )(
        coarse.reshape(256, C), cache_coarse.reshape(256, C), cache_middle.reshape(256, C), cache_fine.reshape(1024, C),
        coarse_gain.reshape(1, C), coarse_shift.reshape(1, C), fine_gain.reshape(1, C), fine_shift.reshape(1, C),
        coarse_kernel, lift_kernel, fine_kernel, skip_kernel,
    )
    return decoded.reshape(2, 32, 16, C1)


def solution(mesh):
    def run(*args):
        channels, outer = args[-1].shape
        sizes = (mesh.shape["ta"], mesh.shape["ha"], mesh.shape["wa"], channels, outer)
        return jax.shard_map(
            functools.partial(local, sizes),
            mesh=mesh,
            in_specs=(P("ta", "ha", "wa", None),) + (P(None, "ha", "wa", None),) * 3 + (P(),) * 8,
            out_specs=P("ta", "ha", "wa", None),
            check_vma=False,
        )(*args)

    return run
```

```python
import functools

import jax
import jax.numpy as jnp
from jax import lax
from jax.experimental import pallas as pl
from jax.experimental.pallas import tpu as pltpu
from jax.sharding import PartitionSpec as P

GROUPS = 32
EPS = 1e-06
MESH = pl.DeviceIdType.MESH
F32 = jnp.float32
BF16 = jnp.bfloat16


def rolled(value, shift):
    size = value.shape[0]
    shift = shift % size
    return value if shift == 0 else pltpu.roll(value, shift, 0)


def put(ref, start, value):
    width = ref.shape[-1]
    for part in range(value.shape[1] // width):
        ref[part, pl.ds(start, value.shape[0]), :] = value[:, part * width : (part + 1) * width]


def take(ref, start, stride=1, parts=None):
    at = pl.ds(start, 16) if stride == 1 else pl.ds(start, 16, stride=stride)
    return jnp.concatenate([ref[part, at, :] for part in range(parts or ref.shape[0])], axis=1)


def body(
    sizes,
    coarse_hbm, cache_coarse_hbm, cache_middle_hbm, cache_fine_hbm,
    coarse_gain, coarse_shift, fine_gain, fine_shift,
    coarse_kernel, lift_kernel, fine_kernel, skip_kernel,
    out_ref, affine,
    cb, cbp, cmb, cfb, xf, cff, xt, xtf, ss, sr, saf, act_a, acc1, w1, lk, w2, w3, wp, skw,
    cm, cs, cfs, mt, mid_g, gf, acc2, lt, lf, acc3, back, outb, ar_src, ar_recv,
    local_sem, ar_send, ar_got, send_sem, recv_sem,
):
    nt, nh, nw, C, C1 = sizes
    half = gf.shape[0] // 2
    ta, ha, wa = lax.axis_index("ta"), lax.axis_index("ha"), lax.axis_index("wa")
    row16 = lax.broadcasted_iota(jnp.int32, (16, C), 0)
    row16w = lax.broadcasted_iota(jnp.int32, (16, 2 * C), 0)
    first_w, last_w, first_h, last_h = wa == 0, wa == nw - 1, ha == 0, ha == nh - 1

    def near(t=0, h=0, w=0):
        where = {}
        if t:
            where["ta"] = lax.rem(ta + (t + nt), nt)
        if h:
            where["ha"] = lax.rem(ha + (h + nh), nh)
        if w:
            where["wa"] = lax.rem(wa + (w + nw), nw)
        return where

    loads = []

    def load(src, dst):
        copy = pltpu.make_async_copy(src, dst, local_sem.at[len(loads)])
        copy.start()
        loads.append(copy)
        return copy

    get_coarse = load(coarse_hbm, cb)
    barrier = pltpu.get_barrier_semaphore()
    y_hi, core = ta // 2, lax.rem(ta, 2)
    by_z = [
        {"ta": 2 * y_hi + lax.rem(core + dc, 2), "ha": lax.rem(ha + dh, nh)}
        for dc in range(2) for dh in range(nh) if dc or dh
    ]
    by_xy = [
        {"ta": 2 * lax.rem(y_hi + dy, 2) + core, "wa": lax.rem(wa + dw, nw)}
        for dy in range(2) for dw in range(nw) if dy or dw
    ]
    stages = ((by_z, 0), (by_xy, len(by_z)))
    friends = by_z + by_xy + [near(t=-1), near(t=-1, w=1), near(t=-1, w=-1), near(t=-1, h=1), near(t=-1, h=-1)]
    for friend in friends:
        pl.semaphore_signal(barrier, inc=1, device_id=friend, device_id_type=MESH)
    get_cc = pltpu.make_async_copy(cache_coarse_hbm, cbp, local_sem.at[59])

    @pl.when(ta == 0)
    def _():
        get_cc.start()

    get_lk = load(lift_kernel, lk)

    def message(index, src, dst, where, leaves=None):
        return pltpu.make_async_remote_copy(
            src_ref=src, dst_ref=dst, send_sem=send_sem.at[index if leaves is None else leaves], recv_sem=recv_sem.at[index],
            device_id=where, device_id_type=MESH,
        )

    center = message(0, coarse_hbm, cbp, near(t=1))
    cols_own = [
        message(1, xt.at[2:4, 8:10], xt.at[2:4, 0:2], near(w=1)),
        message(2, xt.at[2:4, 2:4], xt.at[2:4, 10:12], near(w=-1)),
    ]
    cols_next = [
        message(3, xt.at[2:4, 8:10], xt.at[0:2, 0:2], near(t=1, w=1)),
        message(4, xt.at[2:4, 2:4], xt.at[0:2, 10:12], near(t=1, w=-1)),
    ]
    cols_cached = [
        message(3, xt.at[0:2, 8:10], xt.at[0:2, 0:2], near(w=1), 18),
        message(4, xt.at[0:2, 2:4], xt.at[0:2, 10:12], near(w=-1), 19),
    ]
    rows_own = [
        message(9, ss.at[0, 2:4], sr.at[1, 2:4], near(h=-1)),
        message(10, ss.at[1, 2:4], sr.at[0, 2:4], near(h=1)),
    ]
    rows_next = [
        message(20, ss.at[0, 2:4], sr.at[1, 0:2], near(t=1, h=-1)),
        message(21, ss.at[1, 2:4], sr.at[0, 0:2], near(t=1, h=1)),
    ]
    rows_cached = [
        message(20, ss.at[0, 0:2], sr.at[1, 0:2], near(h=-1), 22),
        message(21, ss.at[1, 0:2], sr.at[0, 0:2], near(h=1), 23),
    ]

    pl.semaphore_wait(barrier, len(friends))

    @pl.when(ta < nt - 1)
    def _():
        center.start()

    def transpose_into(first_frame):
        for f in range(2):
            for c in range(8):
                cells = take(xf, f * 128 + c, 8)
                put(xtf, (first_frame + f) * 192 + (2 + c) * 16, cells)
                xt[first_frame + f, 2 + c] = cells.astype(BF16)

    get_coarse.wait()
    flat = cb[...].astype(F32)
    put(xf, 0, flat)
    transpose_into(2)
    for copy in cols_own:
        copy.start()

    @pl.when(ta < nt - 1)
    def _():
        for copy in cols_next:
            copy.start()

    count = flat.shape[0]
    mean = jnp.sum(flat, axis=0, keepdims=True) / count
    centred = flat - mean
    ar_src[0, 0] = jnp.zeros((8, C), F32)
    ar_src[0, 0, 0:1, :] = mean
    ar_src[0, 0, 1:2, :] = jnp.sum(centred * centred, axis=0, keepdims=True) / count

    def ar_copies(which, stage):
        peers, base = stages[stage]
        return [
            pltpu.make_async_remote_copy(
                src_ref=ar_src.at[which, stage], dst_ref=ar_recv.at[which, base + i],
                send_sem=ar_send.at[which, base + i], recv_sem=ar_got.at[which, base + i],
                device_id=peer, device_id_type=MESH,
            )
            for i, peer in enumerate(peers)
        ]

    def ar_start(which, stage):
        for copy in ar_copies(which, stage):
            copy.start()

    def ar_finish(which, stage):
        peers, base = stages[stage]
        n = len(peers) + 1
        for copy in ar_copies(which, stage):
            copy.wait_recv()
        tiles = [ar_src[which, stage]] + [ar_recv[which, base + i] for i in range(n - 1)]
        average = functools.reduce(jnp.add, tiles) / n
        spread = functools.reduce(jnp.add, [(tile - average) * (tile - average) for tile in tiles]) / n
        rows = lax.broadcasted_iota(jnp.int32, (8, C), 0)
        return average + jnp.where(rows == 1, pltpu.roll(spread, 1, 0), 0.0)

    def ar_next(which, stage):
        ar_src[which, stage + 1] = ar_finish(which, stage)
        ar_start(which, stage + 1)

    size = C // GROUPS
    width = xf.shape[-1]

    def group_mean(value):
        lane_of = lax.broadcasted_iota(jnp.int32, (8, width), 1)
        parts = []
        for part in range(C // width):
            x = jnp.broadcast_to(value[:, part * width : (part + 1) * width], (8, width))
            step = 1
            while step < size:
                x = x + jnp.where((lane_of & step) == 0, pltpu.roll(x, width - step, 1), pltpu.roll(x, step, 1))
                step *= 2
            parts.append(x[0:1])
        return jnp.concatenate(parts, axis=1) / size

    def normaliser(which, gain, shift):
        tile = ar_finish(which, 1)
        mean, variance = tile[0:1], tile[1:2]
        grouped = group_mean(mean)
        away = mean - grouped
        mean, variance = grouped, group_mean(variance + away * away)
        half_scale = 0.5 * (gain * lax.rsqrt(variance + EPS))
        half_shift = 0.5 * shift

        def act(x, mean=mean, half_scale=half_scale, half_shift=half_shift):
            half = (x - mean) * half_scale + half_shift
            return half + half * jnp.tanh(half)

        return act, mean, half_scale, half_shift

    ar_start(0, 0)
    get_cm = load(cache_middle_hbm, cmb)
    get_w1 = load(coarse_kernel, w1)
    get_affine = [load(ref, affine.at[i]) for i, ref in enumerate((coarse_gain, coarse_shift, fine_gain, fine_shift))]
    get_w3 = [
        load(fine_kernel.at[2 * i], w3.at[i, a : a + 3, :, :, a * C1 : (a + 1) * C1]) for i in range(2) for a in range(2)
    ] + [
        load(fine_kernel.at[1 + i - f], wp.at[i, :, :, :, f * C1 : (f + 1) * C1]) for i in range(2) for f in range(2)
    ]
    get_skip = [load(skip_kernel, skw.at[a * C : (a + 1) * C, a * C1 : (a + 1) * C1]) for a in range(2)]
    get_cf = load(cache_fine_hbm, cfb)

    @pl.when(ta == 0)
    def _():
        get_cc.wait()
        put(xf, 0, cbp[...].astype(F32))
        transpose_into(0)
        for copy in cols_cached:
            copy.start()

    cm_first = [
        message(5, cm.at[:, 8:9], cm.at[:, 0:1], near(w=1)),
        message(6, cm.at[:, 1:2], cm.at[:, 9:10], near(w=-1)),
    ]
    cf_first = [
        message(7, lt.at[:, 0:2, 8:9, :, 0:C], lt.at[:, 0:2, 0:1, :, 0:C], near(w=1)),
        message(8, lt.at[:, 0:2, 0:1, :, C : 2 * C], lt.at[:, 0:2, 8:9, :, C : 2 * C], near(w=-1)),
    ]
    cm_second = [
        message(11, cs.at[:, 0:1], cm.at[:, 11:12], near(h=-1)),
        message(12, cs.at[:, 1:2], cm.at[:, 10:11], near(h=1)),
    ]
    cf_second = [
        message(13, cfs.at[0], lt.at[0, 0:2, 9:10], near(h=-1)),
        message(14, cfs.at[1], lt.at[1, 0:2, 9:10], near(h=1)),
    ]

    get_cm.wait()

    @pl.when(ta < 2)
    def _():
        put(xf, 0, cmb[...].astype(F32))
        for f in range(2):
            for c in range(8):
                cm[f, 1 + c] = take(xf, f * 128 + c, 8).astype(BF16)
        for copy in cm_first:
            copy.start()

    def widen(f, slots):
        for c in slots:
            put(xtf, f * 192 + c * 16, xt[f, c].astype(F32))

    def pick_rows(f):
        for side, rows in enumerate(((0, 1), (14, 15))):
            for k, row in enumerate(rows):
                ss[side, f, k] = take(xtf, f * 192 + row, 16).astype(BF16)

    for copy in cols_own:
        copy.wait_recv()
    for f in (2, 3):
        widen(f, (0, 1, 10, 11))
        pick_rows(f)
    for copy in rows_own:
        copy.start()

    @pl.when(ta < nt - 1)
    def _():
        for copy in rows_next:
            copy.start()

    @pl.when(ta == 0)
    def _():
        for copy in cols_cached:
            copy.wait_recv()
        for f in (0, 1):
            widen(f, (0, 1, 10, 11))
            pick_rows(f)
        for copy in rows_cached:
            copy.start()

    def fold(i, carry):
        dt, r = i // (C // 16), pl.multiple_of(lax.rem(i, C // 16) * 16, 16)
        taps = [[lk[dt, dh, dw, pl.ds(r, 16), :].astype(F32) for dw in range(3)] for dh in range(3)]
        for a in range(2):
            for k in range(2):
                if a == 0:
                    line = taps[0] if k == 0 else [taps[1][d] + taps[2][d] for d in range(3)]
                else:
                    line = [taps[0][d] + taps[1][d] for d in range(3)] if k == 0 else taps[2]
                wide = ((line[0] + line[1], line[2]), (line[0], line[1] + line[2]))
                for b in range(2):
                    for j in range(2):
                        w2[a, dt, pl.ds((2 * j + k) * C + r, 16), b * C : (b + 1) * C] = wide[b][j].astype(BF16)
        return carry

    get_lk.wait()
    ar_next(0, 0)
    lax.fori_loop(2 * (C // 16), 3 * (C // 16), fold, 0)

    @pl.when(ta < 2)
    def _():
        for copy in cm_first:
            copy.wait_recv()
        for f in range(2):
            for c in range(10):
                put(gf, 16 * c, cm[f, c].astype(F32))
            cs[f, 0] = take(gf, 0, 16, half).astype(BF16)
            cs[f, 1] = take(gf, 15, 16, half).astype(BF16)
        for copy in cm_second:
            copy.start()

    @pl.when(ta > 0)
    def _():
        center.wait_recv()
        put(xf, 0, cbp[...].astype(F32))
        for f in range(2):
            for c in range(8):
                put(xtf, f * 192 + (2 + c) * 16, take(xf, f * 128 + c, 8))
        for copy in cols_next:
            copy.wait_recv()
        for f in (0, 1):
            widen(f, (0, 1, 10, 11))

    lax.fori_loop(C // 16, 2 * (C // 16), fold, 0)
    for copy in [get_w1] + get_affine:
        copy.wait()

    for copy in rows_own + rows_next:
        copy.wait_recv()
    act, *_ = normaliser(0, affine[0], affine[1])

    cols = lax.broadcasted_iota(jnp.int32, (16, C), 0)

    def strips_of(f):
        raw = jnp.logical_and(ta == 0, f < 2)
        for side in range(2):
            outside = first_h if side == 0 else last_h
            for k in range(2):
                x = sr[side, f, k].astype(F32)
                y = jnp.where(raw, x, act(x)) if f < 2 else act(x)
                gone = jnp.logical_or(jnp.logical_and(first_w, cols < 2), jnp.logical_and(last_w, cols >= 10))
                saf[f, side, k] = jnp.where(jnp.logical_or(outside, gone), 0.0, y)

    def act_coarse(f):
        strips_of(f)
        for c in range(12):
            at = f * 192 + c * 16
            x = take(xtf, at)
            x = jnp.where(ta == 0, x, act(x)) if f < 2 else act(x)
            if c < 2:
                x = jnp.where(first_w, 0.0, x)
            if c >= 10:
                x = jnp.where(last_w, 0.0, x)
            put(xtf, at, x)
            above = jnp.where(row16 == 0, saf[f, 0, 1, c : c + 1, :], rolled(x, 1))
            below = jnp.where(row16 == 15, saf[f, 1, 0, c : c + 1, :], rolled(x, -1))
            act_a[f, c, :, 0:C] = above.astype(BF16)
            act_a[f, c, :, C : 2 * C] = x.astype(BF16)
            act_a[f, c, :, 2 * C : 3 * C] = below.astype(BF16)
        top = take(xtf, f * 192, 16)
        bottom = take(xtf, f * 192 + 15, 16)
        for side, lines in enumerate(((saf[f, 0, 0], saf[f, 0, 1], top), (bottom, saf[f, 1, 0], saf[f, 1, 1]))):
            for dw in range(3):
                for dh in range(3):
                    act_a[f, 12 + 2 * dw + side, :, dh * C : (dh + 1) * C] = rolled(lines[dh], -dw).astype(BF16)

    def conv_coarse(f, g):
        lhs = jnp.concatenate(
            [
                jnp.concatenate([act_a[g, dw : dw + 10, :, lanes], act_a[g, 12 + 2 * dw : 14 + 2 * dw, :, lanes]], axis=0)
                for lanes in (slice(0, C), slice(C, 2 * C), slice(2 * C, 3 * C))
                for dw in range(3)
            ],
            axis=-1,
        ).reshape(12 * 16, 9 * C)
        part = jnp.dot(lhs, w1[g - f].reshape(9 * C, C), preferred_element_type=F32).reshape(12, 16, C)
        acc1[f] = part if g == f else acc1[f] + part

    def finish_middle(f):
        for c in range(10):
            y = xt[2 + f, 1 + c].astype(F32) + acc1[f, c]
            if c == 0:
                y = jnp.where(first_w, 0.0, y)
            if c == 9:
                y = jnp.where(last_w, 0.0, y)
            mt[4 + f, c] = y.astype(BF16)
        gone = (cols > 9) | (first_w & (cols == 0)) | (last_w & (cols == 9))
        for side in range(2):
            y = rolled(sr[side, 2 + f, 1 - side].astype(F32), -1) + acc1[f, 10 + side]
            y = jnp.where(jnp.logical_or(gone, first_h if side == 0 else last_h), 0.0, y)
            mt[4 + f, 10 + side] = y.astype(BF16)

    to_next = [message(15 + f, mt.at[4 + f : 5 + f], mt.at[2 + f : 3 + f], near(t=1)) for f in range(2)]

    def send_middle(f):
        finish_middle(f)

        @pl.when(ta < nt - 1)
        def _():
            to_next[f].start()

    act_coarse(1)
    act_coarse(2)
    conv_coarse(1, 1)
    act_coarse(3)
    conv_coarse(1, 2)
    conv_coarse(1, 3)
    send_middle(1)
    act_coarse(0)
    for g in range(3):
        conv_coarse(0, g)
    send_middle(0)

    to_second = message(17, mt.at[4:6], mt.at[0:2], near(t=2))
    by_second = message(17, mt.at[2:4], mt.at[0:2], near(t=1))

    def prepare(g):
        top = mt[g, 10].astype(F32)
        bottom = mt[g, 11].astype(F32)
        for c in range(10):
            x = mt[g, c].astype(F32)
            put(gf, 16 * c, x)
            mid_g[g, c, :, 0:C] = jnp.where(row16 == 0, top[c : c + 1], rolled(x, 1)).astype(BF16)
            mid_g[g, c, :, C : 2 * C] = mt[g, c]
            mid_g[g, c, :, 2 * C : 3 * C] = jnp.where(row16 == 15, bottom[c : c + 1], rolled(x, -1)).astype(BF16)
        row_top = take(gf, 0, 16, half)
        row_bottom = take(gf, 15, 16, half)
        for j in range(2):
            mid_g[g, 10 + j, :, 0:C] = rolled(row_bottom, -j).astype(BF16)
            mid_g[g, 10 + j, :, C : 2 * C] = rolled(bottom, -j).astype(BF16)
            mid_g[g, 12 + j, :, C : 2 * C] = rolled(top, -j).astype(BF16)
            mid_g[g, 12 + j, :, 2 * C : 3 * C] = rolled(row_top, -j).astype(BF16)

    def lift_part(a, dt, g, frames):
        lanes = slice(a * C, (a + 2) * C)
        lhs = jnp.concatenate(
            [
                jnp.concatenate(
                    [mid_g[g : g + frames, j : j + 9, :, lanes], mid_g[g : g + frames, 10 + 2 * a + j : 11 + 2 * a + j, :, lanes]],
                    axis=1,
                )
                for j in range(2)
            ],
            axis=-1,
        ).reshape(frames * 10 * 16, 4 * C)
        part = jnp.dot(lhs, w2[a, dt], preferred_element_type=F32)
        return part.reshape(frames, 10, 16, 2 * C)

    def cached_middle(at):
        gone = (cols > 9) | (first_w & (cols == 0)) | (last_w & (cols == 9))
        for f in range(2):
            mt[at + f, 1:9] = cm[f, 1:9]
            mt[at + f, 0] = jnp.where(first_w, 0.0, cm[f, 0].astype(F32)).astype(BF16)
            mt[at + f, 9] = jnp.where(last_w, 0.0, cm[f, 9].astype(F32)).astype(BF16)
            for side in range(2):
                outside = jnp.logical_or(gone, first_h if side == 0 else last_h)
                mt[at + f, 10 + side] = jnp.where(outside, 0.0, cm[f, 10 + side].astype(F32)).astype(BF16)

    for copy in get_w3 + get_skip + [get_cf]:
        copy.wait()
    prepare(4)
    prepare(5)
    for a in range(2):
        acc2[a] = lift_part(a, 2, 4, 2)
        acc2[a, 1:2] += lift_part(a, 1, 4, 1)

    lax.fori_loop(0, C // 16, fold, 0)
    for i in range(2):
        for dw in range(3):
            w3[i, 3, dw, :, 0:C1] = jnp.zeros((C, C1), BF16)
            w3[i, 0, dw, :, C1 : 2 * C1] = jnp.zeros((C, C1), BF16)
    skw[0:C, C1 : 2 * C1] = jnp.zeros((C, C1), BF16)
    skw[C : 2 * C, 0:C1] = jnp.zeros((C, C1), BF16)

    @pl.when(ta == 0)
    def _():
        for copy in cm_second:
            copy.wait_recv()
        cached_middle(2)

    @pl.when(ta > 0)
    def _():
        to_next[1].wait_recv()

    prepare(3)
    for a in range(2):
        acc2[a, 0:1] += lift_part(a, 1, 3, 1)
        acc2[a, 1:2] += lift_part(a, 0, 3, 1)

    @pl.when(ta > 0)
    def _():
        to_next[0].wait_recv()

    @pl.when(ta == 2)
    def _():
        by_second.start()

    prepare(2)
    for a in range(2):
        acc2[a, 0:1] += lift_part(a, 0, 2, 1)
        lt[a, 2:4] = acc2[a].astype(BF16)

    @pl.when(ta == 0)
    def _():
        to_second.start()
        put(cff, 0, cfb[...].astype(F32))
        for f in range(2):
            for c in range(16):
                p, b = (c + 1) // 2, (c + 1) % 2
                for a in range(2):
                    lt[a, f, p, :, b * C : (b + 1) * C] = take(cff, f * 512 + a * 16 + c, 32).astype(BF16)
        for copy in cf_first:
            copy.start()

    pivot = jnp.sum(lt[0, 2, 1, :, 0:C].astype(F32), axis=0, keepdims=True) / 16
    sums = jnp.zeros((16, C), F32)
    squares = jnp.zeros((16, C), F32)
    for a in range(2):
        for f in range(2):
            for p in range(9):
                for b in range(2):
                    if (p, b) not in ((0, 0), (8, 1)):
                        x = lt[a, 2 + f, p, :, b * C : (b + 1) * C].astype(F32) - pivot
                        sums = sums + x
                        squares = squares + x * x
    count = 2 * 2 * 16 * 16
    off = jnp.sum(sums, axis=0, keepdims=True) / count
    ar_src[1, 0] = jnp.zeros((8, C), F32)
    ar_src[1, 0, 0:1, :] = pivot + off
    ar_src[1, 0, 1:2, :] = jnp.maximum(jnp.sum(squares, axis=0, keepdims=True) / count - off * off, 0.0)
    ar_start(1, 0)

    def lift_before_new(a):
        acc2[a] = lift_part(a, 2, 2, 2)

    def lift_before_old(a):
        acc2[a] += lift_part(a, 0, 0, 2)
        lt[a, 0:2] = (acc2[a] + lift_part(a, 1, 1, 2)).astype(BF16)

    @pl.when(ta > 0)
    def _():
        lift_before_new(0)
        lift_before_new(1)

    @pl.when(ta == 0)
    def _():
        for copy in cf_first:
            copy.wait_recv()
        for f in range(2):
            for a, row in ((0, 0), (1, 15)):
                for p in range(9):
                    put(gf, 16 * p, lt[a, f, p].astype(F32))
                cfs[a, f, 0] = take(gf, row, 16).astype(BF16)
        for copy in cf_second:
            copy.start()

    ar_next(1, 0)

    for b in range(2):
        lhs = jnp.concatenate([lt[a, 2:4, 1 - b : 9 - b, :, b * C : (b + 1) * C] for a in range(2)], axis=-1)
        part = jnp.dot(lhs.reshape(2 * 8 * 16, 2 * C), skw[...], preferred_element_type=F32)
        acc3[:, :, 1 - b] = part.reshape(2, 8, 16, 2 * C1)

    @pl.when(ta == 1)
    def _():
        for copy in cm_second:
            copy.wait_recv()
        cached_middle(0)

    @pl.when(ta > 1)
    def _():
        to_second.wait_recv()

    @pl.when(ta > 0)
    def _():
        prepare(0)
        prepare(1)
        lift_before_old(0)
        lift_before_old(1)


    lane = lax.broadcasted_iota(jnp.int32, (16, 2 * C), 1)

    def spread_fine(f, fn):
        top = jnp.where(first_h, 0.0, fn(lt[1, f, 9].astype(F32)))
        bottom = jnp.where(last_h, 0.0, fn(lt[0, f, 9].astype(F32)))
        for p in range(9):
            even = fn(lt[0, f, p].astype(F32))
            odd = fn(lt[1, f, p].astype(F32))
            before = jnp.where(row16w == 0, top[p : p + 1], rolled(odd, 1))
            after = jnp.where(row16w == 15, bottom[p : p + 1], rolled(even, -1))
            for k, part in enumerate((before, even, odd, after)):
                if p == 0:
                    part = jnp.where(first_w & (lane < C), 0.0, part)
                if p == 8:
                    part = jnp.where(last_w & (lane >= C), 0.0, part)
                part = part.astype(BF16)
                for b in range(2):
                    lf[f, 2 * p + b, :, k * C : (k + 1) * C] = part[:, b * C : (b + 1) * C]

    @pl.when(ta == 0)
    def _():
        for copy in cf_second:
            copy.wait_recv()

    _, mean, half_scale, half_shift = normaliser(1, affine[2], affine[3])
    mean2 = jnp.concatenate([mean, mean], axis=1)
    scale2 = jnp.concatenate([half_scale, half_scale], axis=1)
    shift2 = jnp.concatenate([half_shift, half_shift], axis=1)

    def fine_act(x):
        half = (x - mean2) * scale2 + shift2
        return half + half * jnp.tanh(half)

    def fine_act_or_cached(x):
        return jnp.where(ta == 0, x, fine_act(x))

    def conv_fine(g):
        if g in (0, 3):
            f = 0 if g == 0 else 1
            lhs = jnp.concatenate(
                [lf[g, dw : dw + 16, :, k * C : (k + 1) * C] for k in range(4) for dw in range(3)], axis=-1
            ).reshape(16 * 16, 12 * C)
            part = jnp.dot(lhs, w3[f].reshape(12 * C, 2 * C1), preferred_element_type=F32)
            acc3[f] += part.reshape(8, 2, 16, 2 * C1)
        else:
            for a in range(2):
                lhs = jnp.concatenate(
                    [lf[g, dw : dw + 16, :, (a + k) * C : (a + k + 1) * C] for k in range(3) for dw in range(3)], axis=-1
                ).reshape(16 * 16, 9 * C)
                part = jnp.dot(lhs, wp[g - 1].reshape(9 * C, 2 * C1), preferred_element_type=F32)
                part = part.reshape(8, 2, 16, 2 * C1)
                for f in range(2):
                    acc3[f, :, :, :, a * C1 : (a + 1) * C1] += part[..., f * C1 : (f + 1) * C1]

    def finish_fine(f):
        for c in range(16):
            for a in range(2):
                back[pl.ds(f * 512 + a * 16 + c, 16, stride=32), :] = acc3[f, c // 2, c % 2, :, a * C1 : (a + 1) * C1]
        outb[f * 512 : (f + 1) * 512] = back[f * 512 : (f + 1) * 512].astype(BF16)
        leave[f].start()

    leave = [
        pltpu.make_async_copy(outb.at[f * 512 : (f + 1) * 512], out_ref.at[f * 512 : (f + 1) * 512], local_sem.at[57 + f])
        for f in range(2)
    ]

    spread_fine(0, fine_act_or_cached)
    spread_fine(1, fine_act_or_cached)
    conv_fine(0)
    spread_fine(2, fine_act)
    conv_fine(1)
    spread_fine(3, fine_act)
    conv_fine(2)
    finish_fine(0)
    conv_fine(3)
    finish_fine(1)

    for copy in leave:
        copy.wait()
    for which in range(2):
        for stage in range(2):
            for copy in ar_copies(which, stage):
                copy.wait_send()
    for copy in cols_own + rows_own:
        copy.wait_send()

    @pl.when(ta < 2)
    def _():
        for copy in cm_first + cm_second:
            copy.wait_send()

    @pl.when(ta == 0)
    def _():
        for copy in cols_cached + rows_cached + cf_first + cf_second:
            copy.wait_send()

    @pl.when(ta < nt - 1)
    def _():
        for copy in [center] + cols_next + rows_next + to_next:
            copy.wait_send()

    @pl.when(jnp.logical_or(ta == 0, ta == 2))
    def _():
        to_second.wait_send()


def local(
    sizes, coarse, cache_coarse, cache_middle, cache_fine, coarse_gain, coarse_shift, fine_gain, fine_shift,
    coarse_kernel, lift_kernel, fine_kernel, skip_kernel,
):
    nt, nh, nw, C, C1 = sizes
    frames, rows, cols, _ = coarse.shape
    assert (frames, rows, cols) == (2, 16, 8)
    peers = 2 * nh + 2 * nw - 2
    hbm = pl.BlockSpec(memory_space=pltpu.HBM)
    V = pltpu.VMEM
    W = min(128, C)
    L = C // W
    scratch = [
        V((4, 1, C), F32),
        V((256, C), BF16), V((256, C), BF16), V((256, C), BF16), V((1024, C), BF16),
        V((L, 256, W), F32), V((L, 1024, W), F32),
        V((4, 12, 16, C), BF16), V((L, 4 * 12 * 16 + 64, W), F32),
        V((2, 4, 2, 16, C), BF16), V((2, 4, 2, 16, C), BF16), V((4, 2, 2, 16, C), F32),
        V((4, 18, 16, 3 * C), BF16), V((2, 12, 16, C), F32),
        V((3, 3, 3, C, C), BF16), V((3, 3, 3, C, C), BF16), V((2, 3, 4 * C, 2 * C), BF16),
        V((2, 4, 3, C, 2 * C1), BF16), V((2, 3, 3, C, 2 * C1), BF16), V((2 * C, 2 * C1), BF16),
        V((2, 12, 16, C), BF16), V((2, 2, 16, C), BF16), V((2, 2, 1, 16, 2 * C), BF16),
        V((6, 12, 16, C), BF16), V((6, 14, 16, 3 * C), BF16), V((2 * L, 256, W), F32),
        V((2, 2, 10, 16, 2 * C), F32), V((2, 4, 10, 16, 2 * C), BF16),
        V((4, 18, 16, 4 * C), BF16), V((2, 8, 2, 16, 2 * C1), F32), V((1024, C1), F32), V((1024, C1), BF16),
        V((2, 2, 8, C), F32), V((2, peers, 8, C), F32),
        pltpu.SemaphoreType.DMA((60,)),
        pltpu.SemaphoreType.DMA((2, peers)), pltpu.SemaphoreType.DMA((2, peers)),
        pltpu.SemaphoreType.DMA((24,)), pltpu.SemaphoreType.DMA((24,)),
    ]
    decoded = pl.pallas_call(
        functools.partial(body, sizes),
        out_shape=jax.ShapeDtypeStruct((1024, C1), BF16),
        in_specs=[hbm] * 12,
        out_specs=hbm,
        scratch_shapes=scratch,
        compiler_params=pltpu.CompilerParams(
            collective_id=0, has_side_effects=True, vmem_limit_bytes=63 * 1024 * 1024
        ),
    )(
        coarse.reshape(256, C), cache_coarse.reshape(256, C), cache_middle.reshape(256, C), cache_fine.reshape(1024, C),
        coarse_gain.reshape(1, C), coarse_shift.reshape(1, C), fine_gain.reshape(1, C), fine_shift.reshape(1, C),
        coarse_kernel, lift_kernel, fine_kernel, skip_kernel,
    )
    return decoded.reshape(2, 32, 16, C1)


def solution(mesh):
    def run(*args):
        channels, outer = args[-1].shape
        sizes = (mesh.shape["ta"], mesh.shape["ha"], mesh.shape["wa"], channels, outer)
        return jax.shard_map(
            functools.partial(local, sizes),
            mesh=mesh,
            in_specs=(P("ta", "ha", "wa", None),) + (P(None, "ha", "wa", None),) * 3 + (P(),) * 8,
            out_specs=P("ta", "ha", "wa", None),
            check_vma=False,
        )(*args)

    return run
```

```python
import functools

import jax
import jax.numpy as jnp
from jax import lax
from jax.experimental import pallas as pl
from jax.experimental.pallas import tpu as pltpu
from jax.sharding import PartitionSpec as P

GROUPS = 32
EPS = 1e-06
MESH = pl.DeviceIdType.MESH
F32 = jnp.float32
BF16 = jnp.bfloat16


def rolled(value, shift):
    size = value.shape[0]
    shift = shift % size
    return value if shift == 0 else pltpu.roll(value, shift, 0)


def put(ref, start, value):
    width = ref.shape[-1]
    for part in range(value.shape[1] // width):
        ref[part, pl.ds(start, value.shape[0]), :] = value[:, part * width : (part + 1) * width]


def take(ref, start, stride=1, parts=None):
    at = pl.ds(start, 16) if stride == 1 else pl.ds(start, 16, stride=stride)
    return jnp.concatenate([ref[part, at, :] for part in range(parts or ref.shape[0])], axis=1)


def body(
    sizes,
    coarse_hbm, cache_coarse_hbm, cache_middle_hbm, cache_fine_hbm,
    coarse_gain, coarse_shift, fine_gain, fine_shift,
    coarse_kernel, lift_kernel, fine_kernel, skip_kernel,
    out_ref, affine,
    cb, cbp, cmb, cfb, xf, cff, xt, xtf, ss, sr, saf, act_a, acc1, w1, lk, w2, w3, skw,
    cm, cs, cfs, mt, mid_g, gf, acc2, lt, lf, acc3, back, outb, ar_src, ar_recv,
    local_sem, ar_send, ar_got, send_sem, recv_sem,
):
    nt, nh, nw, C, C1 = sizes
    half = gf.shape[0] // 2
    ta, ha, wa = lax.axis_index("ta"), lax.axis_index("ha"), lax.axis_index("wa")
    row16 = lax.broadcasted_iota(jnp.int32, (16, C), 0)
    row16w = lax.broadcasted_iota(jnp.int32, (16, 2 * C), 0)
    first_w, last_w, first_h, last_h = wa == 0, wa == nw - 1, ha == 0, ha == nh - 1

    def near(t=0, h=0, w=0):
        where = {}
        if t:
            where["ta"] = lax.rem(ta + (t + nt), nt)
        if h:
            where["ha"] = lax.rem(ha + (h + nh), nh)
        if w:
            where["wa"] = lax.rem(wa + (w + nw), nw)
        return where

    loads = []

    def load(src, dst):
        copy = pltpu.make_async_copy(src, dst, local_sem.at[len(loads)])
        copy.start()
        loads.append(copy)
        return copy

    get_coarse = load(coarse_hbm, cb)
    barrier = pltpu.get_barrier_semaphore()
    y_hi, core = ta // 2, lax.rem(ta, 2)
    by_z = [
        {"ta": 2 * y_hi + lax.rem(core + dc, 2), "ha": lax.rem(ha + dh, nh)}
        for dc in range(2) for dh in range(nh) if dc or dh
    ]
    by_xy = [
        {"ta": 2 * lax.rem(y_hi + dy, 2) + core, "wa": lax.rem(wa + dw, nw)}
        for dy in range(2) for dw in range(nw) if dy or dw
    ]
    stages = ((by_z, 0), (by_xy, len(by_z)))
    friends = by_z + by_xy + [near(t=-1), near(t=-1, w=1), near(t=-1, w=-1), near(t=-1, h=1), near(t=-1, h=-1)]
    for friend in friends:
        pl.semaphore_signal(barrier, inc=1, device_id=friend, device_id_type=MESH)
    get_cc = pltpu.make_async_copy(cache_coarse_hbm, cbp, local_sem.at[59])

    @pl.when(ta == 0)
    def _():
        get_cc.start()

    get_lk = load(lift_kernel, lk)

    def message(index, src, dst, where, leaves=None):
        return pltpu.make_async_remote_copy(
            src_ref=src, dst_ref=dst, send_sem=send_sem.at[index if leaves is None else leaves], recv_sem=recv_sem.at[index],
            device_id=where, device_id_type=MESH,
        )

    center = message(0, coarse_hbm, cbp, near(t=1))
    cols_own = [
        message(1, xt.at[2:4, 8:10], xt.at[2:4, 0:2], near(w=1)),
        message(2, xt.at[2:4, 2:4], xt.at[2:4, 10:12], near(w=-1)),
    ]
    cols_next = [
        message(3, xt.at[2:4, 8:10], xt.at[0:2, 0:2], near(t=1, w=1)),
        message(4, xt.at[2:4, 2:4], xt.at[0:2, 10:12], near(t=1, w=-1)),
    ]
    cols_cached = [
        message(3, xt.at[0:2, 8:10], xt.at[0:2, 0:2], near(w=1), 18),
        message(4, xt.at[0:2, 2:4], xt.at[0:2, 10:12], near(w=-1), 19),
    ]
    rows_own = [
        message(9, ss.at[0, 2:4], sr.at[1, 2:4], near(h=-1)),
        message(10, ss.at[1, 2:4], sr.at[0, 2:4], near(h=1)),
    ]
    rows_next = [
        message(20, ss.at[0, 2:4], sr.at[1, 0:2], near(t=1, h=-1)),
        message(21, ss.at[1, 2:4], sr.at[0, 0:2], near(t=1, h=1)),
    ]
    rows_cached = [
        message(20, ss.at[0, 0:2], sr.at[1, 0:2], near(h=-1), 22),
        message(21, ss.at[1, 0:2], sr.at[0, 0:2], near(h=1), 23),
    ]

    pl.semaphore_wait(barrier, len(friends))

    @pl.when(ta < nt - 1)
    def _():
        center.start()

    def transpose_into(first_frame):
        for f in range(2):
            for c in range(8):
                cells = take(xf, f * 128 + c, 8)
                put(xtf, (first_frame + f) * 192 + (2 + c) * 16, cells)
                xt[first_frame + f, 2 + c] = cells.astype(BF16)

    get_coarse.wait()
    flat = cb[...].astype(F32)
    put(xf, 0, flat)
    transpose_into(2)
    for copy in cols_own:
        copy.start()

    @pl.when(ta < nt - 1)
    def _():
        for copy in cols_next:
            copy.start()

    count = flat.shape[0]
    mean = jnp.sum(flat, axis=0, keepdims=True) / count
    centred = flat - mean
    ar_src[0, 0] = jnp.zeros((8, C), F32)
    ar_src[0, 0, 0:1, :] = mean
    ar_src[0, 0, 1:2, :] = jnp.sum(centred * centred, axis=0, keepdims=True) / count

    def ar_copies(which, stage):
        peers, base = stages[stage]
        return [
            pltpu.make_async_remote_copy(
                src_ref=ar_src.at[which, stage], dst_ref=ar_recv.at[which, base + i],
                send_sem=ar_send.at[which, stage], recv_sem=ar_got.at[which, stage],
                device_id=peer, device_id_type=MESH,
            )
            for i, peer in enumerate(peers)
        ]

    def ar_start(which, stage):
        for copy in ar_copies(which, stage):
            copy.start()

    def ar_all(which, stage, sem):
        peers, base = stages[stage]
        slots = ar_recv.at[which, base : base + len(peers)]
        return pltpu.make_async_copy(slots, slots, sem.at[which, stage])

    def ar_finish(which, stage):
        peers, base = stages[stage]
        n = len(peers) + 1
        ar_all(which, stage, ar_got).wait()
        tiles = [ar_src[which, stage]] + [ar_recv[which, base + i] for i in range(n - 1)]
        average = functools.reduce(jnp.add, tiles) / n
        spread = functools.reduce(jnp.add, [(tile - average) * (tile - average) for tile in tiles]) / n
        rows = lax.broadcasted_iota(jnp.int32, (8, C), 0)
        return average + jnp.where(rows == 1, pltpu.roll(spread, 1, 0), 0.0)

    def ar_next(which, stage):
        ar_src[which, stage + 1] = ar_finish(which, stage)
        ar_start(which, stage + 1)

    size = C // GROUPS
    width = xf.shape[-1]

    def group_mean(value):
        lane_of = lax.broadcasted_iota(jnp.int32, (8, width), 1)
        parts = []
        for part in range(C // width):
            x = jnp.broadcast_to(value[:, part * width : (part + 1) * width], (8, width))
            step = 1
            while step < size:
                x = x + jnp.where((lane_of & step) == 0, pltpu.roll(x, width - step, 1), pltpu.roll(x, step, 1))
                step *= 2
            parts.append(x[0:1])
        return jnp.concatenate(parts, axis=1) / size

    def normaliser(which, gain, shift):
        tile = ar_finish(which, 1)
        mean, variance = tile[0:1], tile[1:2]
        grouped = group_mean(mean)
        away = mean - grouped
        mean, variance = grouped, group_mean(variance + away * away)
        half_scale = 0.5 * (gain * lax.rsqrt(variance + EPS))
        half_shift = 0.5 * shift

        def act(x, mean=mean, half_scale=half_scale, half_shift=half_shift):
            half = (x - mean) * half_scale + half_shift
            return half + half * jnp.tanh(half)

        return act, mean, half_scale, half_shift

    ar_start(0, 0)
    get_cm = load(cache_middle_hbm, cmb)
    get_w1 = load(coarse_kernel, w1)
    get_affine = [load(ref, affine.at[i]) for i, ref in enumerate((coarse_gain, coarse_shift, fine_gain, fine_shift))]
    get_w3 = [load(fine_kernel, w3.at[:, a : a + 3, :, :, a * C1 : (a + 1) * C1]) for a in range(2)]
    get_skip = [load(skip_kernel, skw.at[a * C : (a + 1) * C, a * C1 : (a + 1) * C1]) for a in range(2)]
    get_cf = load(cache_fine_hbm, cfb)

    @pl.when(ta == 0)
    def _():
        get_cc.wait()
        put(xf, 0, cbp[...].astype(F32))
        transpose_into(0)
        for copy in cols_cached:
            copy.start()

    cm_first = [
        message(5, cm.at[:, 8:9], cm.at[:, 0:1], near(w=1)),
        message(6, cm.at[:, 1:2], cm.at[:, 9:10], near(w=-1)),
    ]
    cf_first = [
        message(7, lt.at[:, 0:2, 8:9, :, 0:C], lt.at[:, 0:2, 0:1, :, 0:C], near(w=1)),
        message(8, lt.at[:, 0:2, 0:1, :, C : 2 * C], lt.at[:, 0:2, 8:9, :, C : 2 * C], near(w=-1)),
    ]
    cm_second = [
        message(11, cs.at[:, 0:1], cm.at[:, 11:12], near(h=-1)),
        message(12, cs.at[:, 1:2], cm.at[:, 10:11], near(h=1)),
    ]
    cf_second = [
        message(13, cfs.at[0], lt.at[0, 0:2, 9:10], near(h=-1)),
        message(14, cfs.at[1], lt.at[1, 0:2, 9:10], near(h=1)),
    ]

    get_cm.wait()

    @pl.when(ta < 2)
    def _():
        put(xf, 0, cmb[...].astype(F32))
        for f in range(2):
            for c in range(8):
                cm[f, 1 + c] = take(xf, f * 128 + c, 8).astype(BF16)
        for copy in cm_first:
            copy.start()

    def widen(f, slots):
        for c in slots:
            put(xtf, f * 192 + c * 16, xt[f, c].astype(F32))

    def pick_rows(f):
        for side, rows in enumerate(((0, 1), (14, 15))):
            for k, row in enumerate(rows):
                ss[side, f, k] = take(xtf, f * 192 + row, 16).astype(BF16)

    for copy in cols_own:
        copy.wait_recv()
    for f in (2, 3):
        widen(f, (0, 1, 10, 11))
        pick_rows(f)
    for copy in rows_own:
        copy.start()

    @pl.when(ta < nt - 1)
    def _():
        for copy in rows_next:
            copy.start()

    @pl.when(ta == 0)
    def _():
        for copy in cols_cached:
            copy.wait_recv()
        for f in (0, 1):
            widen(f, (0, 1, 10, 11))
            pick_rows(f)
        for copy in rows_cached:
            copy.start()

    def fold(i, carry):
        dt, r = i // (C // 16), pl.multiple_of(lax.rem(i, C // 16) * 16, 16)
        taps = [[lk[dt, dh, dw, pl.ds(r, 16), :].astype(F32) for dw in range(3)] for dh in range(3)]
        for a in range(2):
            for k in range(2):
                if a == 0:
                    line = taps[0] if k == 0 else [taps[1][d] + taps[2][d] for d in range(3)]
                else:
                    line = [taps[0][d] + taps[1][d] for d in range(3)] if k == 0 else taps[2]
                wide = ((line[0] + line[1], line[2]), (line[0], line[1] + line[2]))
                for b in range(2):
                    for j in range(2):
                        w2[a, dt, pl.ds((2 * j + k) * C + r, 16), b * C : (b + 1) * C] = wide[b][j].astype(BF16)
        return carry

    get_lk.wait()
    ar_next(0, 0)
    lax.fori_loop(2 * (C // 16), 3 * (C // 16), fold, 0)

    @pl.when(ta < 2)
    def _():
        for copy in cm_first:
            copy.wait_recv()
        for f in range(2):
            for c in range(10):
                put(gf, 16 * c, cm[f, c].astype(F32))
            cs[f, 0] = take(gf, 0, 16, half).astype(BF16)
            cs[f, 1] = take(gf, 15, 16, half).astype(BF16)
        for copy in cm_second:
            copy.start()

    @pl.when(ta > 0)
    def _():
        center.wait_recv()
        put(xf, 0, cbp[...].astype(F32))
        for f in range(2):
            for c in range(8):
                put(xtf, f * 192 + (2 + c) * 16, take(xf, f * 128 + c, 8))
        for copy in cols_next:
            copy.wait_recv()
        for f in (0, 1):
            widen(f, (0, 1, 10, 11))

    lax.fori_loop(C // 16, 2 * (C // 16), fold, 0)
    for copy in [get_w1] + get_affine:
        copy.wait()

    for copy in rows_own + rows_next:
        copy.wait_recv()
    act, *_ = normaliser(0, affine[0], affine[1])

    cols = lax.broadcasted_iota(jnp.int32, (16, C), 0)

    def strips_of(f):
        raw = jnp.logical_and(ta == 0, f < 2)
        for side in range(2):
            outside = first_h if side == 0 else last_h
            for k in range(2):
                x = sr[side, f, k].astype(F32)
                y = jnp.where(raw, x, act(x))
                gone = jnp.logical_or(jnp.logical_and(first_w, cols < 2), jnp.logical_and(last_w, cols >= 10))
                saf[f, side, k] = jnp.where(jnp.logical_or(outside, gone), 0.0, y)

    def act_coarse(f, carry):
        strips_of(f)
        raw = jnp.logical_and(ta == 0, f < 2)
        for c in range(12):
            at = pl.multiple_of(f * 192 + c * 16, 16)
            x = take(xtf, at)
            x = jnp.where(raw, x, act(x))
            if c < 2:
                x = jnp.where(first_w, 0.0, x)
            if c >= 10:
                x = jnp.where(last_w, 0.0, x)
            put(xtf, at, x)
            above = jnp.where(row16 == 0, saf[f, 0, 1, c : c + 1, :], rolled(x, 1))
            below = jnp.where(row16 == 15, saf[f, 1, 0, c : c + 1, :], rolled(x, -1))
            act_a[f, c, :, 0:C] = above.astype(BF16)
            act_a[f, c, :, C : 2 * C] = x.astype(BF16)
            act_a[f, c, :, 2 * C : 3 * C] = below.astype(BF16)
        top = take(xtf, f * 192, 16)
        bottom = take(xtf, f * 192 + 15, 16)
        for side, lines in enumerate(((saf[f, 0, 0], saf[f, 0, 1], top), (bottom, saf[f, 1, 0], saf[f, 1, 1]))):
            for dw in range(3):
                for dh in range(3):
                    act_a[f, 12 + 2 * dw + side, :, dh * C : (dh + 1) * C] = rolled(lines[dh], -dw).astype(BF16)
        return carry

    def conv_coarse(f, g):
        lhs = jnp.concatenate(
            [
                jnp.concatenate([act_a[g, dw : dw + 10, :, lanes], act_a[g, 12 + 2 * dw : 14 + 2 * dw, :, lanes]], axis=0)
                for lanes in (slice(0, C), slice(C, 2 * C), slice(2 * C, 3 * C))
                for dw in range(3)
            ],
            axis=-1,
        ).reshape(12 * 16, 9 * C)
        part = jnp.dot(lhs, w1[g - f].reshape(9 * C, C), preferred_element_type=F32).reshape(12, 16, C)
        acc1[f] += part

    def finish_middle(f):
        for c in range(10):
            y = xt[2 + f, 1 + c].astype(F32) + acc1[f, c]
            if c == 0:
                y = jnp.where(first_w, 0.0, y)
            if c == 9:
                y = jnp.where(last_w, 0.0, y)
            mt[4 + f, c] = y.astype(BF16)
        gone = (cols > 9) | (first_w & (cols == 0)) | (last_w & (cols == 9))
        for side in range(2):
            y = rolled(sr[side, 2 + f, 1 - side].astype(F32), -1) + acc1[f, 10 + side]
            y = jnp.where(jnp.logical_or(gone, first_h if side == 0 else last_h), 0.0, y)
            mt[4 + f, 10 + side] = y.astype(BF16)

    to_next = [message(15 + f, mt.at[4 + f : 5 + f], mt.at[2 + f : 3 + f], near(t=1)) for f in range(2)]

    def send_middle(f):
        finish_middle(f)

        @pl.when(ta < nt - 1)
        def _():
            to_next[f].start()

    lax.fori_loop(0, 4, act_coarse, 0)
    acc1[...] = jnp.zeros_like(acc1)
    for f in (1, 0):

        def conv_step(dt, carry, f=f):
            conv_coarse(f, dt + f)
            return carry

        lax.fori_loop(0, 3, conv_step, 0)
        send_middle(f)

    to_second = message(17, mt.at[4:6], mt.at[0:2], near(t=2))
    by_second = message(17, mt.at[2:4], mt.at[0:2], near(t=1))

    def prepare(g, carry=0):
        top = mt[g, 10].astype(F32)
        bottom = mt[g, 11].astype(F32)
        for c in range(10):
            x = mt[g, c].astype(F32)
            put(gf, 16 * c, x)
            mid_g[0, g, c, :, 0:C] = jnp.where(row16 == 0, top[c : c + 1], rolled(x, 1)).astype(BF16)
            mid_g[0, g, c, :, C : 2 * C] = mt[g, c]
            mid_g[1, g, c, :, 0:C] = mt[g, c]
            mid_g[1, g, c, :, C : 2 * C] = jnp.where(row16 == 15, bottom[c : c + 1], rolled(x, -1)).astype(BF16)
        row_top = take(gf, 0, 16, half)
        row_bottom = take(gf, 15, 16, half)
        for j in range(2):
            mid_g[0, g, 10 + j, :, 0:C] = rolled(row_bottom, -j).astype(BF16)
            mid_g[0, g, 10 + j, :, C : 2 * C] = rolled(bottom, -j).astype(BF16)
            mid_g[1, g, 10 + j, :, 0:C] = rolled(top, -j).astype(BF16)
            mid_g[1, g, 10 + j, :, C : 2 * C] = rolled(row_top, -j).astype(BF16)
        return carry

    def lift_part(a, dt, g, frames):
        at = pl.ds(g, frames)
        lhs = jnp.concatenate(
            [jnp.concatenate([mid_g[a, at, j : j + 9], mid_g[a, at, 10 + j : 11 + j]], axis=1) for j in range(2)], axis=-1
        ).reshape(frames * 10 * 16, 4 * C)
        part = jnp.dot(lhs, w2[a, dt], preferred_element_type=F32)
        return part.reshape(frames, 10, 16, 2 * C)

    def cached_middle(at):
        gone = (cols > 9) | (first_w & (cols == 0)) | (last_w & (cols == 9))
        for f in range(2):
            mt[at + f, 1:9] = cm[f, 1:9]
            mt[at + f, 0] = jnp.where(first_w, 0.0, cm[f, 0].astype(F32)).astype(BF16)
            mt[at + f, 9] = jnp.where(last_w, 0.0, cm[f, 9].astype(F32)).astype(BF16)
            for side in range(2):
                outside = jnp.logical_or(gone, first_h if side == 0 else last_h)
                mt[at + f, 10 + side] = jnp.where(outside, 0.0, cm[f, 10 + side].astype(F32)).astype(BF16)

    for copy in get_w3 + get_skip + [get_cf]:
        copy.wait()
    lax.fori_loop(4, 6, prepare, 0)

    @pl.loop(0, 2)
    def _(a):
        acc2[a] = lift_part(a, 2, 4, 2)
        acc2[a, 1:2] += lift_part(a, 1, 4, 1)

    lax.fori_loop(0, C // 16, fold, 0)
    for i in range(3):
        for dw in range(3):
            w3[i, 3, dw, :, 0:C1] = jnp.zeros((C, C1), BF16)
            w3[i, 0, dw, :, C1 : 2 * C1] = jnp.zeros((C, C1), BF16)
    skw[0:C, C1 : 2 * C1] = jnp.zeros((C, C1), BF16)
    skw[C : 2 * C, 0:C1] = jnp.zeros((C, C1), BF16)

    @pl.when(ta == 0)
    def _():
        for copy in cm_second:
            copy.wait_recv()
        cached_middle(2)

    @pl.when(ta > 0)
    def _():
        to_next[1].wait_recv()

    prepare(3)

    @pl.loop(0, 4)
    def _(i):
        a, out = i // 2, lax.rem(i, 2)
        acc2[a, pl.ds(out, 1)] += lift_part(a, 1 - out, 3, 1)

    @pl.when(ta > 0)
    def _():
        to_next[0].wait_recv()

    @pl.when(ta == 2)
    def _():
        by_second.start()

    prepare(2)

    @pl.loop(0, 2)
    def _(a):
        acc2[a, 0:1] += lift_part(a, 0, 2, 1)
        lt[a, 2:4] = acc2[a].astype(BF16)

    @pl.when(ta == 0)
    def _():
        to_second.start()
        put(cff, 0, cfb[...].astype(F32))
        for f in range(2):
            for c in range(16):
                p, b = (c + 1) // 2, (c + 1) % 2
                for a in range(2):
                    lt[a, f, p, :, b * C : (b + 1) * C] = take(cff, f * 512 + a * 16 + c, 32).astype(BF16)
        for copy in cf_first:
            copy.start()

    pivot = jnp.sum(lt[0, 2, 1, :, 0:C].astype(F32), axis=0, keepdims=True) / 16
    sums = jnp.zeros((16, C), F32)
    squares = jnp.zeros((16, C), F32)
    for a in range(2):
        for f in range(2):
            for p in range(9):
                for b in range(2):
                    if (p, b) not in ((0, 0), (8, 1)):
                        x = lt[a, 2 + f, p, :, b * C : (b + 1) * C].astype(F32) - pivot
                        sums = sums + x
                        squares = squares + x * x
    count = 2 * 2 * 16 * 16
    off = jnp.sum(sums, axis=0, keepdims=True) / count
    ar_src[1, 0] = jnp.zeros((8, C), F32)
    ar_src[1, 0, 0:1, :] = pivot + off
    ar_src[1, 0, 1:2, :] = jnp.maximum(jnp.sum(squares, axis=0, keepdims=True) / count - off * off, 0.0)
    ar_start(1, 0)

    @pl.when(ta > 0)
    def _():
        @pl.loop(0, 2)
        def _(a):
            acc2[a] = lift_part(a, 2, 2, 2)

    @pl.when(ta == 0)
    def _():
        for copy in cf_first:
            copy.wait_recv()
        for f in range(2):
            for a, row in ((0, 0), (1, 15)):
                for p in range(9):
                    put(gf, 16 * p, lt[a, f, p].astype(F32))
                cfs[a, f, 0] = take(gf, row, 16).astype(BF16)
        for copy in cf_second:
            copy.start()

    ar_next(1, 0)

    for b in range(2):
        lhs = jnp.concatenate([lt[a, 2:4, 1 - b : 9 - b, :, b * C : (b + 1) * C] for a in range(2)], axis=-1)
        part = jnp.dot(lhs.reshape(2 * 8 * 16, 2 * C), skw[...], preferred_element_type=F32)
        acc3[:, :, 1 - b] = part.reshape(2, 8, 16, 2 * C1)

    @pl.when(ta == 1)
    def _():
        for copy in cm_second:
            copy.wait_recv()
        cached_middle(0)

    @pl.when(ta > 1)
    def _():
        to_second.wait_recv()

    @pl.when(ta > 0)
    def _():
        lax.fori_loop(0, 2, prepare, 0)

        @pl.loop(0, 4)
        def _(i):
            a, dt = i // 2, lax.rem(i, 2)
            acc2[a] += lift_part(a, dt, dt, 2)

        for a in range(2):
            lt[a, 0:2] = acc2[a].astype(BF16)

    for stage in range(2):
        ar_all(0, stage, ar_send).wait()
    for copy in cols_own + rows_own:
        copy.wait_send()

    @pl.when(ta < 2)
    def _():
        for copy in cm_first + cm_second:
            copy.wait_send()

    @pl.when(ta == 0)
    def _():
        for copy in cols_cached + rows_cached + cf_first + cf_second:
            copy.wait_send()

    @pl.when(ta < nt - 1)
    def _():
        for copy in [center] + cols_next + rows_next + to_next:
            copy.wait_send()

    @pl.when(jnp.logical_or(ta == 0, ta == 2))
    def _():
        to_second.wait_send()

    lane = lax.broadcasted_iota(jnp.int32, (16, 2 * C), 1)

    def spread_fine(f, carry):
        raw = jnp.logical_and(ta == 0, f < 2)

        def fn(x):
            return jnp.where(raw, x, fine_act(x))

        top = jnp.where(first_h, 0.0, fn(lt[1, f, 9].astype(F32)))
        bottom = jnp.where(last_h, 0.0, fn(lt[0, f, 9].astype(F32)))
        for p in range(9):
            even = fn(lt[0, f, p].astype(F32))
            odd = fn(lt[1, f, p].astype(F32))
            before = jnp.where(row16w == 0, top[p : p + 1], rolled(odd, 1))
            after = jnp.where(row16w == 15, bottom[p : p + 1], rolled(even, -1))
            for k, part in enumerate((before, even, odd, after)):
                if p == 0:
                    part = jnp.where(first_w & (lane < C), 0.0, part)
                if p == 8:
                    part = jnp.where(last_w & (lane >= C), 0.0, part)
                part = part.astype(BF16)
                for b in range(2):
                    lf[f, 2 * p + b, :, k * C : (k + 1) * C] = part[:, b * C : (b + 1) * C]
        return carry

    @pl.when(ta == 0)
    def _():
        for copy in cf_second:
            copy.wait_recv()

    _, mean, half_scale, half_shift = normaliser(1, affine[2], affine[3])
    mean2 = jnp.concatenate([mean, mean], axis=1)
    scale2 = jnp.concatenate([half_scale, half_scale], axis=1)
    shift2 = jnp.concatenate([half_shift, half_shift], axis=1)

    def fine_act(x):
        half = (x - mean2) * scale2 + shift2
        return half + half * jnp.tanh(half)

    def conv_fine(dt, carry):
        at = pl.ds(dt, 2)
        lhs = jnp.concatenate(
            [lf[at, dw : dw + 16, :, k * C : (k + 1) * C] for k in range(4) for dw in range(3)], axis=-1
        ).reshape(2 * 16 * 16, 12 * C)
        part = jnp.dot(lhs, w3[dt].reshape(12 * C, 2 * C1), preferred_element_type=F32)
        acc3[...] += part.reshape(2, 8, 2, 16, 2 * C1)
        return carry

    def finish_fine(f):
        for c in range(16):
            for a in range(2):
                back[pl.ds(f * 512 + a * 16 + c, 16, stride=32), :] = acc3[f, c // 2, c % 2, :, a * C1 : (a + 1) * C1]
        outb[f * 512 : (f + 1) * 512] = back[f * 512 : (f + 1) * 512].astype(BF16)
        leave[f].start()

    leave = [
        pltpu.make_async_copy(outb.at[f * 512 : (f + 1) * 512], out_ref.at[f * 512 : (f + 1) * 512], local_sem.at[57 + f])
        for f in range(2)
    ]

    lax.fori_loop(0, 4, spread_fine, 0)
    lax.fori_loop(0, 3, conv_fine, 0)
    finish_fine(0)
    finish_fine(1)

    for copy in leave:
        copy.wait()
    for stage in range(2):
        ar_all(1, stage, ar_send).wait()


def local(
    sizes, coarse, cache_coarse, cache_middle, cache_fine, coarse_gain, coarse_shift, fine_gain, fine_shift,
    coarse_kernel, lift_kernel, fine_kernel, skip_kernel,
):
    nt, nh, nw, C, C1 = sizes
    frames, rows, cols, _ = coarse.shape
    assert (frames, rows, cols) == (2, 16, 8)
    peers = 2 * nh + 2 * nw - 2
    hbm = pl.BlockSpec(memory_space=pltpu.HBM)
    V = pltpu.VMEM
    W = min(128, C)
    L = C // W
    scratch = [
        V((4, 1, C), F32),
        V((256, C), BF16), V((256, C), BF16), V((256, C), BF16), V((1024, C), BF16),
        V((L, 256, W), F32), V((L, 1024, W), F32),
        V((4, 12, 16, C), BF16), V((L, 4 * 12 * 16 + 64, W), F32),
        V((2, 4, 2, 16, C), BF16), V((2, 4, 2, 16, C), BF16), V((4, 2, 2, 16, C), F32),
        V((4, 18, 16, 3 * C), BF16), V((2, 12, 16, C), F32),
        V((3, 3, 3, C, C), BF16), V((3, 3, 3, C, C), BF16), V((2, 3, 4 * C, 2 * C), BF16),
        V((3, 4, 3, C, 2 * C1), BF16), V((2 * C, 2 * C1), BF16),
        V((2, 12, 16, C), BF16), V((2, 2, 16, C), BF16), V((2, 2, 1, 16, 2 * C), BF16),
        V((6, 12, 16, C), BF16), V((2, 6, 12, 16, 2 * C), BF16), V((2 * L, 256, W), F32),
        V((2, 2, 10, 16, 2 * C), F32), V((2, 4, 10, 16, 2 * C), BF16),
        V((4, 18, 16, 4 * C), BF16), V((2, 8, 2, 16, 2 * C1), F32), V((1024, C1), F32), V((1024, C1), BF16),
        V((2, 2, 8, C), F32), V((2, peers, 8, C), F32),
        pltpu.SemaphoreType.DMA((60,)),
        pltpu.SemaphoreType.DMA((2, 2)), pltpu.SemaphoreType.DMA((2, 2)),
        pltpu.SemaphoreType.DMA((24,)), pltpu.SemaphoreType.DMA((24,)),
    ]
    decoded = pl.pallas_call(
        functools.partial(body, sizes),
        out_shape=jax.ShapeDtypeStruct((1024, C1), BF16),
        in_specs=[hbm] * 12,
        out_specs=hbm,
        scratch_shapes=scratch,
        compiler_params=pltpu.CompilerParams(
            collective_id=0, has_side_effects=True, vmem_limit_bytes=63 * 1024 * 1024
        ),
    )(
        coarse.reshape(256, C), cache_coarse.reshape(256, C), cache_middle.reshape(256, C), cache_fine.reshape(1024, C),
        coarse_gain.reshape(1, C), coarse_shift.reshape(1, C), fine_gain.reshape(1, C), fine_shift.reshape(1, C),
        coarse_kernel, lift_kernel, fine_kernel, skip_kernel,
    )
    return decoded.reshape(2, 32, 16, C1)


def solution(mesh):
    def run(*args):
        channels, outer = args[-1].shape
        sizes = (mesh.shape["ta"], mesh.shape["ha"], mesh.shape["wa"], channels, outer)
        return jax.shard_map(
            functools.partial(local, sizes),
            mesh=mesh,
            in_specs=(P("ta", "ha", "wa", None),) + (P(None, "ha", "wa", None),) * 3 + (P(),) * 8,
            out_specs=P("ta", "ha", "wa", None),
            check_vma=False,
        )(*args)

    return run
```

```python
import functools

import jax
import jax.numpy as jnp
from jax import lax
from jax.experimental import pallas as pl
from jax.experimental.pallas import tpu as pltpu
from jax.sharding import PartitionSpec as P

GROUPS = 32
EPS = 1e-06
MESH = pl.DeviceIdType.MESH
F32 = jnp.float32
BF16 = jnp.bfloat16


def rolled(value, shift):
    size = value.shape[0]
    shift = shift % size
    return value if shift == 0 else pltpu.roll(value, shift, 0)


def put(ref, start, value):
    width = ref.shape[-1]
    for part in range(value.shape[1] // width):
        ref[part, pl.ds(start, value.shape[0]), :] = value[:, part * width : (part + 1) * width]


def take(ref, start, stride=1, parts=None):
    at = pl.ds(start, 16) if stride == 1 else pl.ds(start, 16, stride=stride)
    return jnp.concatenate([ref[part, at, :] for part in range(parts or ref.shape[0])], axis=1)


def body(
    sizes,
    coarse_hbm, cache_coarse_hbm, cache_middle_hbm, cache_fine_hbm,
    coarse_gain, coarse_shift, fine_gain, fine_shift,
    coarse_kernel, lift_kernel, fine_kernel, skip_kernel,
    out_ref, affine,
    cb, cbp, cmb, cfb, xf, cff, xt, xtf, ss, sr, saf, act_a, acc1, w1, lk, w2, w3, wp, skw,
    cm, cs, cfs, mt, mid_g, gf, acc2, lt, ltp, lf, acc3, back, outb, ar_src, ar_recv,
    local_sem, ar_send, ar_got, send_sem, recv_sem,
):
    nt, nh, nw, C, C1 = sizes
    half = gf.shape[0] // 2
    ta, ha, wa = lax.axis_index("ta"), lax.axis_index("ha"), lax.axis_index("wa")
    row16 = lax.broadcasted_iota(jnp.int32, (16, C), 0)
    row16w = lax.broadcasted_iota(jnp.int32, (16, 2 * C), 0)
    first_w, last_w, first_h, last_h = wa == 0, wa == nw - 1, ha == 0, ha == nh - 1

    def near(t=0, h=0, w=0):
        where = {}
        if t:
            where["ta"] = lax.rem(ta + (t + nt), nt)
        if h:
            where["ha"] = lax.rem(ha + (h + nh), nh)
        if w:
            where["wa"] = lax.rem(wa + (w + nw), nw)
        return where

    loads = []

    def load(src, dst):
        copy = pltpu.make_async_copy(src, dst, local_sem.at[len(loads)])
        copy.start()
        loads.append(copy)
        return copy

    get_coarse = load(coarse_hbm, cb)
    barrier = pltpu.get_barrier_semaphore()
    y_hi, core = ta // 2, lax.rem(ta, 2)
    by_z = [
        {"ta": 2 * y_hi + lax.rem(core + dc, 2), "ha": lax.rem(ha + dh, nh)}
        for dc in range(2) for dh in range(nh) if dc or dh
    ]
    by_xy = [
        {"ta": 2 * lax.rem(y_hi + dy, 2) + core, "wa": lax.rem(wa + dw, nw)}
        for dy in range(2) for dw in range(nw) if dy or dw
    ]
    stages = ((by_z, 0), (by_xy, len(by_z)))
    friends = by_z + by_xy + [near(t=-1), near(t=-1, w=1), near(t=-1, w=-1), near(t=-1, h=1), near(t=-1, h=-1)]
    for friend in friends:
        pl.semaphore_signal(barrier, inc=1, device_id=friend, device_id_type=MESH)
    get_cc = pltpu.make_async_copy(cache_coarse_hbm, cbp, local_sem.at[59])

    @pl.when(ta == 0)
    def _():
        get_cc.start()

    get_lk = load(lift_kernel, lk)

    def message(index, src, dst, where, leaves=None):
        return pltpu.make_async_remote_copy(
            src_ref=src, dst_ref=dst, send_sem=send_sem.at[index if leaves is None else leaves], recv_sem=recv_sem.at[index],
            device_id=where, device_id_type=MESH,
        )

    center = message(0, coarse_hbm, cbp, near(t=1))
    cols_own = [
        message(1, xt.at[2:4, 8:10], xt.at[2:4, 0:2], near(w=1)),
        message(2, xt.at[2:4, 2:4], xt.at[2:4, 10:12], near(w=-1)),
    ]
    cols_next = [
        message(3, xt.at[2:4, 8:10], xt.at[0:2, 0:2], near(t=1, w=1)),
        message(4, xt.at[2:4, 2:4], xt.at[0:2, 10:12], near(t=1, w=-1)),
    ]
    cols_cached = [
        message(3, xt.at[0:2, 8:10], xt.at[0:2, 0:2], near(w=1), 18),
        message(4, xt.at[0:2, 2:4], xt.at[0:2, 10:12], near(w=-1), 19),
    ]
    rows_own = [
        message(9, ss.at[0, 2:4], sr.at[1, 2:4], near(h=-1)),
        message(10, ss.at[1, 2:4], sr.at[0, 2:4], near(h=1)),
    ]
    rows_next = [
        message(20, ss.at[0, 2:4], sr.at[1, 0:2], near(t=1, h=-1)),
        message(21, ss.at[1, 2:4], sr.at[0, 0:2], near(t=1, h=1)),
    ]
    rows_cached = [
        message(20, ss.at[0, 0:2], sr.at[1, 0:2], near(h=-1), 22),
        message(21, ss.at[1, 0:2], sr.at[0, 0:2], near(h=1), 23),
    ]

    pl.semaphore_wait(barrier, len(friends))

    @pl.when(ta < nt - 1)
    def _():
        center.start()

    def transpose_into(first_frame):
        for f in range(2):
            for c in range(8):
                cells = take(xf, f * 128 + c, 8)
                put(xtf, (first_frame + f) * 192 + (2 + c) * 16, cells)
                xt[first_frame + f, 2 + c] = cells.astype(BF16)

    get_coarse.wait()
    flat = cb[...].astype(F32)
    put(xf, 0, flat)
    transpose_into(2)
    for copy in cols_own:
        copy.start()

    @pl.when(ta < nt - 1)
    def _():
        for copy in cols_next:
            copy.start()

    count = flat.shape[0]
    mean = jnp.sum(flat, axis=0, keepdims=True) / count
    centred = flat - mean
    ar_src[0, 0] = jnp.zeros((8, C), F32)
    ar_src[0, 0, 0:1, :] = mean
    ar_src[0, 0, 1:2, :] = jnp.sum(centred * centred, axis=0, keepdims=True) / count

    def ar_copies(which, stage):
        peers, base = stages[stage]
        return [
            pltpu.make_async_remote_copy(
                src_ref=ar_src.at[which, stage], dst_ref=ar_recv.at[which, base + i],
                send_sem=ar_send.at[which, stage], recv_sem=ar_got.at[which, stage],
                device_id=peer, device_id_type=MESH,
            )
            for i, peer in enumerate(peers)
        ]

    def ar_start(which, stage):
        for copy in ar_copies(which, stage):
            copy.start()

    def ar_all(which, stage, sem):
        peers, base = stages[stage]
        slots = ar_recv.at[which, base : base + len(peers)]
        return pltpu.make_async_copy(slots, slots, sem.at[which, stage])

    def ar_finish(which, stage):
        peers, base = stages[stage]
        n = len(peers) + 1
        ar_all(which, stage, ar_got).wait()
        tiles = [ar_src[which, stage]] + [ar_recv[which, base + i] for i in range(n - 1)]
        average = functools.reduce(jnp.add, tiles) / n
        spread = functools.reduce(jnp.add, [(tile - average) * (tile - average) for tile in tiles]) / n
        rows = lax.broadcasted_iota(jnp.int32, (8, C), 0)
        return average + jnp.where(rows == 1, pltpu.roll(spread, 1, 0), 0.0)

    def ar_next(which, stage):
        ar_src[which, stage + 1] = ar_finish(which, stage)
        ar_start(which, stage + 1)

    size = C // GROUPS
    width = xf.shape[-1]

    def group_mean(value):
        lane_of = lax.broadcasted_iota(jnp.int32, (8, width), 1)
        parts = []
        for part in range(C // width):
            x = jnp.broadcast_to(value[:, part * width : (part + 1) * width], (8, width))
            step = 1
            while step < size:
                x = x + jnp.where((lane_of & step) == 0, pltpu.roll(x, width - step, 1), pltpu.roll(x, step, 1))
                step *= 2
            parts.append(x[0:1])
        return jnp.concatenate(parts, axis=1) / size

    def normaliser(which, gain, shift):
        tile = ar_finish(which, 1)
        mean, variance = tile[0:1], tile[1:2]
        grouped = group_mean(mean)
        away = mean - grouped
        mean, variance = grouped, group_mean(variance + away * away)
        half_scale = 0.5 * (gain * lax.rsqrt(variance + EPS))
        half_shift = 0.5 * shift

        def act(x, mean=mean, half_scale=half_scale, half_shift=half_shift):
            half = (x - mean) * half_scale + half_shift
            return half + half * jnp.tanh(half)

        return act, mean, half_scale, half_shift

    ar_start(0, 0)
    get_cm = load(cache_middle_hbm, cmb)
    get_w1 = load(coarse_kernel, w1)
    get_affine = [load(ref, affine.at[i]) for i, ref in enumerate((coarse_gain, coarse_shift, fine_gain, fine_shift))]
    get_w3 = [
        load(fine_kernel.at[2 * i], w3.at[i, a : a + 3, :, :, a * C1 : (a + 1) * C1]) for i in range(2) for a in range(2)
    ] + [
        load(fine_kernel.at[1 + i - f], wp.at[i, :, :, :, f * C1 : (f + 1) * C1]) for i in range(2) for f in range(2)
    ]
    get_skip = [load(skip_kernel, skw.at[a * C : (a + 1) * C, a * C1 : (a + 1) * C1]) for a in range(2)]
    get_cf = load(cache_fine_hbm, cfb)

    @pl.when(ta == 0)
    def _():
        get_cc.wait()
        put(xf, 0, cbp[...].astype(F32))
        transpose_into(0)
        for copy in cols_cached:
            copy.start()

    cm_first = [
        message(5, cm.at[:, 8:9], cm.at[:, 0:1], near(w=1)),
        message(6, cm.at[:, 1:2], cm.at[:, 9:10], near(w=-1)),
    ]
    cf_first = [
        message(7, lt.at[:, 0:2, 8:9, :, 0:C], lt.at[:, 0:2, 0:1, :, 0:C], near(w=1)),
        message(8, lt.at[:, 0:2, 0:1, :, C : 2 * C], lt.at[:, 0:2, 8:9, :, C : 2 * C], near(w=-1)),
    ]
    cm_second = [
        message(11, cs.at[:, 0:1], cm.at[:, 11:12], near(h=-1)),
        message(12, cs.at[:, 1:2], cm.at[:, 10:11], near(h=1)),
    ]
    cf_second = [
        message(13, cfs.at[0], lt.at[0, 0:2, 9:10], near(h=-1)),
        message(14, cfs.at[1], lt.at[1, 0:2, 9:10], near(h=1)),
    ]

    get_cm.wait()

    @pl.when(ta < 2)
    def _():
        put(xf, 0, cmb[...].astype(F32))
        for f in range(2):
            for c in range(8):
                cm[f, 1 + c] = take(xf, f * 128 + c, 8).astype(BF16)
        for copy in cm_first:
            copy.start()

    def widen(f, slots):
        for c in slots:
            put(xtf, f * 192 + c * 16, xt[f, c].astype(F32))

    def pick_rows(f):
        for side, rows in enumerate(((0, 1), (14, 15))):
            for k, row in enumerate(rows):
                ss[side, f, k] = take(xtf, f * 192 + row, 16).astype(BF16)

    for copy in cols_own:
        copy.wait_recv()
    for f in (2, 3):
        widen(f, (0, 1, 10, 11))
        pick_rows(f)
    for copy in rows_own:
        copy.start()

    @pl.when(ta < nt - 1)
    def _():
        for copy in rows_next:
            copy.start()

    @pl.when(ta == 0)
    def _():
        for copy in cols_cached:
            copy.wait_recv()
        for f in (0, 1):
            widen(f, (0, 1, 10, 11))
            pick_rows(f)
        for copy in rows_cached:
            copy.start()

    def fold(i, carry):
        dt, r = i // (C // 16), pl.multiple_of(lax.rem(i, C // 16) * 16, 16)
        taps = [[lk[dt, dh, dw, pl.ds(r, 16), :].astype(F32) for dw in range(3)] for dh in range(3)]
        for a in range(2):
            for k in range(2):
                if a == 0:
                    line = taps[0] if k == 0 else [taps[1][d] + taps[2][d] for d in range(3)]
                else:
                    line = [taps[0][d] + taps[1][d] for d in range(3)] if k == 0 else taps[2]
                wide = ((line[0] + line[1], line[2]), (line[0], line[1] + line[2]))
                for b in range(2):
                    for j in range(2):
                        w2[a, dt, pl.ds((2 * j + k) * C + r, 16), b * C : (b + 1) * C] = wide[b][j].astype(BF16)
        return carry

    get_lk.wait()
    ar_next(0, 0)
    lax.fori_loop(3 * (C // 32), 3 * (C // 16), fold, 0)

    @pl.when(ta < 2)
    def _():
        for copy in cm_first:
            copy.wait_recv()
        for f in range(2):
            for c in range(10):
                put(gf, 16 * c, cm[f, c].astype(F32))
            cs[f, 0] = take(gf, 0, 16, half).astype(BF16)
            cs[f, 1] = take(gf, 15, 16, half).astype(BF16)
        for copy in cm_second:
            copy.start()

    @pl.when(ta > 0)
    def _():
        center.wait_recv()
        put(xf, 0, cbp[...].astype(F32))
        for f in range(2):
            for c in range(8):
                put(xtf, f * 192 + (2 + c) * 16, take(xf, f * 128 + c, 8))
        for copy in cols_next:
            copy.wait_recv()
        for f in (0, 1):
            widen(f, (0, 1, 10, 11))

    lax.fori_loop(0, 3 * (C // 32), fold, 0)
    for copy in [get_w1] + get_affine:
        copy.wait()

    for copy in rows_own + rows_next:
        copy.wait_recv()
    act, *_ = normaliser(0, affine[0], affine[1])

    cols = lax.broadcasted_iota(jnp.int32, (16, C), 0)

    def strips_of(f):
        raw = jnp.logical_and(ta == 0, f < 2)
        for side in range(2):
            outside = first_h if side == 0 else last_h
            for k in range(2):
                x = sr[side, f, k].astype(F32)
                y = jnp.where(raw, x, act(x)) if f < 2 else act(x)
                gone = jnp.logical_or(jnp.logical_and(first_w, cols < 2), jnp.logical_and(last_w, cols >= 10))
                saf[f, side, k] = jnp.where(jnp.logical_or(outside, gone), 0.0, y)

    def act_coarse(f):
        strips_of(f)
        for c in range(12):
            at = f * 192 + c * 16
            x = take(xtf, at)
            x = jnp.where(ta == 0, x, act(x)) if f < 2 else act(x)
            if c < 2:
                x = jnp.where(first_w, 0.0, x)
            if c >= 10:
                x = jnp.where(last_w, 0.0, x)
            put(xtf, at, x)
            above = jnp.where(row16 == 0, saf[f, 0, 1, c : c + 1, :], rolled(x, 1))
            below = jnp.where(row16 == 15, saf[f, 1, 0, c : c + 1, :], rolled(x, -1))
            act_a[f, c, :, 0:C] = above.astype(BF16)
            act_a[f, c, :, C : 2 * C] = x.astype(BF16)
            act_a[f, c, :, 2 * C : 3 * C] = below.astype(BF16)
        top = take(xtf, f * 192, 16)
        bottom = take(xtf, f * 192 + 15, 16)
        for side, lines in enumerate(((saf[f, 0, 0], saf[f, 0, 1], top), (bottom, saf[f, 1, 0], saf[f, 1, 1]))):
            for dw in range(3):
                for dh in range(3):
                    act_a[f, 12 + 2 * dw + side, :, dh * C : (dh + 1) * C] = rolled(lines[dh], -dw).astype(BF16)

    def conv_coarse(f, g):
        lhs = jnp.concatenate(
            [
                jnp.concatenate([act_a[g, dw : dw + 10, :, lanes], act_a[g, 12 + 2 * dw : 14 + 2 * dw, :, lanes]], axis=0)
                for lanes in (slice(0, C), slice(C, 2 * C), slice(2 * C, 3 * C))
                for dw in range(3)
            ],
            axis=-1,
        ).reshape(12 * 16, 9 * C)
        part = jnp.dot(lhs, w1[g - f].reshape(9 * C, C), preferred_element_type=F32).reshape(12, 16, C)
        acc1[f] = part if g == f else acc1[f] + part

    def finish_middle(f):
        for c in range(10):
            y = xt[2 + f, 1 + c].astype(F32) + acc1[f, c]
            if c == 0:
                y = jnp.where(first_w, 0.0, y)
            if c == 9:
                y = jnp.where(last_w, 0.0, y)
            mt[4 + f, c] = y.astype(BF16)
        gone = (cols > 9) | (first_w & (cols == 0)) | (last_w & (cols == 9))
        for side in range(2):
            y = rolled(sr[side, 2 + f, 1 - side].astype(F32), -1) + acc1[f, 10 + side]
            y = jnp.where(jnp.logical_or(gone, first_h if side == 0 else last_h), 0.0, y)
            mt[4 + f, 10 + side] = y.astype(BF16)

    to_next = [message(15 + f, mt.at[4 + f : 5 + f], mt.at[2 + f : 3 + f], near(t=1)) for f in range(2)]

    def send_middle(f):
        finish_middle(f)

        @pl.when(ta < nt - 1)
        def _():
            to_next[f].start()

    act_coarse(1)
    act_coarse(2)
    conv_coarse(1, 1)
    act_coarse(3)
    conv_coarse(1, 2)
    conv_coarse(1, 3)
    send_middle(1)
    act_coarse(0)
    for g in range(3):
        conv_coarse(0, g)
    send_middle(0)

    to_second = message(17, mt.at[4:6], mt.at[0:2], near(t=2))
    by_second = message(17, mt.at[2:4], mt.at[0:2], near(t=1))

    def prepare(g):
        top = mt[g, 10].astype(F32)
        bottom = mt[g, 11].astype(F32)
        for c in range(10):
            x = mt[g, c].astype(F32)
            put(gf, 16 * c, x)
            mid_g[g, c, :, 0:C] = jnp.where(row16 == 0, top[c : c + 1], rolled(x, 1)).astype(BF16)
            mid_g[g, c, :, C : 2 * C] = mt[g, c]
            mid_g[g, c, :, 2 * C : 3 * C] = jnp.where(row16 == 15, bottom[c : c + 1], rolled(x, -1)).astype(BF16)
        row_top = take(gf, 0, 16, half)
        row_bottom = take(gf, 15, 16, half)
        for j in range(2):
            mid_g[g, 10 + j, :, 0:C] = rolled(row_bottom, -j).astype(BF16)
            mid_g[g, 10 + j, :, C : 2 * C] = rolled(bottom, -j).astype(BF16)
            mid_g[g, 12 + j, :, C : 2 * C] = rolled(top, -j).astype(BF16)
            mid_g[g, 12 + j, :, 2 * C : 3 * C] = rolled(row_top, -j).astype(BF16)

    def lift_part(a, dt, g, frames):
        lanes = slice(a * C, (a + 2) * C)
        lhs = jnp.concatenate(
            [
                jnp.concatenate(
                    [mid_g[g : g + frames, j : j + 9, :, lanes], mid_g[g : g + frames, 10 + 2 * a + j : 11 + 2 * a + j, :, lanes]],
                    axis=1,
                )
                for j in range(2)
            ],
            axis=-1,
        ).reshape(frames * 10 * 16, 4 * C)
        part = jnp.dot(lhs, w2[a, dt], preferred_element_type=F32)
        return part.reshape(frames, 10, 16, 2 * C)

    def cached_middle(at):
        gone = (cols > 9) | (first_w & (cols == 0)) | (last_w & (cols == 9))
        for f in range(2):
            mt[at + f, 1:9] = cm[f, 1:9]
            mt[at + f, 0] = jnp.where(first_w, 0.0, cm[f, 0].astype(F32)).astype(BF16)
            mt[at + f, 9] = jnp.where(last_w, 0.0, cm[f, 9].astype(F32)).astype(BF16)
            for side in range(2):
                outside = jnp.logical_or(gone, first_h if side == 0 else last_h)
                mt[at + f, 10 + side] = jnp.where(outside, 0.0, cm[f, 10 + side].astype(F32)).astype(BF16)

    for copy in get_w3 + get_skip + [get_cf]:
        copy.wait()
    prepare(4)
    prepare(5)
    for a in range(2):
        acc2[a] = lift_part(a, 2, 4, 2)
        acc2[a, 1:2] += lift_part(a, 1, 4, 1)

    for i in range(2):
        for dw in range(3):
            w3[i, 3, dw, :, 0:C1] = jnp.zeros((C, C1), BF16)
            w3[i, 0, dw, :, C1 : 2 * C1] = jnp.zeros((C, C1), BF16)
    skw[0:C, C1 : 2 * C1] = jnp.zeros((C, C1), BF16)
    skw[C : 2 * C, 0:C1] = jnp.zeros((C, C1), BF16)

    @pl.when(ta == 0)
    def _():
        for copy in cm_second:
            copy.wait_recv()
        cached_middle(2)

    @pl.when(ta > 0)
    def _():
        to_next[1].wait_recv()

    prepare(3)
    for a in range(2):
        acc2[a, 0:1] += lift_part(a, 1, 3, 1)
        acc2[a, 1:2] += lift_part(a, 0, 3, 1)

    @pl.when(ta > 0)
    def _():
        to_next[0].wait_recv()

    @pl.when(ta == 2)
    def _():
        by_second.start()

    prepare(2)
    for a in range(2):
        acc2[a, 0:1] += lift_part(a, 0, 2, 1)
        lt[a, 2:4] = acc2[a].astype(BF16)

    @pl.when(ta == 0)
    def _():
        to_second.start()
        put(cff, 0, cfb[...].astype(F32))
        for f in range(2):
            for c in range(16):
                p, b = (c + 1) // 2, (c + 1) % 2
                for a in range(2):
                    lt[a, f, p, :, b * C : (b + 1) * C] = take(cff, f * 512 + a * 16 + c, 32).astype(BF16)
        for copy in cf_first:
            copy.start()

    pivot = jnp.sum(lt[0, 2, 1, :, 0:C].astype(F32), axis=0, keepdims=True) / 16
    sums = jnp.zeros((16, C), F32)
    squares = jnp.zeros((16, C), F32)
    for a in range(2):
        for f in range(2):
            for p in range(9):
                for b in range(2):
                    if (p, b) not in ((0, 0), (8, 1)):
                        x = lt[a, 2 + f, p, :, b * C : (b + 1) * C].astype(F32) - pivot
                        sums = sums + x
                        squares = squares + x * x
    count = 2 * 2 * 16 * 16
    off = jnp.sum(sums, axis=0, keepdims=True) / count
    ar_src[1, 0] = jnp.zeros((8, C), F32)
    ar_src[1, 0, 0:1, :] = pivot + off
    ar_src[1, 0, 1:2, :] = jnp.maximum(jnp.sum(squares, axis=0, keepdims=True) / count - off * off, 0.0)
    ar_start(1, 0)

    def lift_before_new(a):
        acc2[a] = lift_part(a, 2, 2, 2)

    def lift_before_old(a):
        acc2[a] += lift_part(a, 0, 0, 2)
        ltp[a] = (acc2[a] + lift_part(a, 1, 1, 2)).astype(BF16)

    @pl.when(ta > 0)
    def _():
        lift_before_new(0)
        lift_before_new(1)

    @pl.when(ta == 0)
    def _():
        for copy in cf_first:
            copy.wait_recv()
        for f in range(2):
            for a, row in ((0, 0), (1, 15)):
                for p in range(9):
                    put(gf, 16 * p, lt[a, f, p].astype(F32))
                cfs[a, f, 0] = take(gf, row, 16).astype(BF16)
        for copy in cf_second:
            copy.start()

    ar_next(1, 0)

    for b in range(2):
        lhs = jnp.concatenate([lt[a, 2:4, 1 - b : 9 - b, :, b * C : (b + 1) * C] for a in range(2)], axis=-1)
        part = jnp.dot(lhs.reshape(2 * 8 * 16, 2 * C), skw[...], preferred_element_type=F32)
        acc3[:, :, 1 - b] = part.reshape(2, 8, 16, 2 * C1)

    @pl.when(ta == 1)
    def _():
        for copy in cm_second:
            copy.wait_recv()
        cached_middle(0)

    @pl.when(ta > 1)
    def _():
        to_second.wait_recv()

    prepare(0)
    prepare(1)

    for stage in range(2):
        ar_all(0, stage, ar_send).wait()
    for copy in cols_own + rows_own:
        copy.wait_send()

    @pl.when(ta < 2)
    def _():
        for copy in cm_first + cm_second:
            copy.wait_send()

    @pl.when(ta == 0)
    def _():
        for copy in cols_cached + rows_cached + cf_first + cf_second:
            copy.wait_send()

    @pl.when(ta < nt - 1)
    def _():
        for copy in [center] + cols_next + rows_next + to_next:
            copy.wait_send()

    @pl.when(jnp.logical_or(ta == 0, ta == 2))
    def _():
        to_second.wait_send()

    lane = lax.broadcasted_iota(jnp.int32, (16, 2 * C), 1)

    def fine_cells(a, f, p):
        if f < 2:
            return jnp.where(ta == 0, lt[a, f, p].astype(F32), fine_act(ltp[a, f, p].astype(F32)))
        return fine_act(lt[a, f, p].astype(F32))

    def spread_fine(f):
        top = jnp.where(first_h, 0.0, fine_cells(1, f, 9))
        bottom = jnp.where(last_h, 0.0, fine_cells(0, f, 9))
        for p in range(9):
            even = fine_cells(0, f, p)
            odd = fine_cells(1, f, p)
            before = jnp.where(row16w == 0, top[p : p + 1], rolled(odd, 1))
            after = jnp.where(row16w == 15, bottom[p : p + 1], rolled(even, -1))
            for k, part in enumerate((before, even, odd, after)):
                if p == 0:
                    part = jnp.where(first_w & (lane < C), 0.0, part)
                if p == 8:
                    part = jnp.where(last_w & (lane >= C), 0.0, part)
                part = part.astype(BF16)
                for b in range(2):
                    lf[f, 2 * p + b, :, k * C : (k + 1) * C] = part[:, b * C : (b + 1) * C]

    @pl.when(ta == 0)
    def _():
        for copy in cf_second:
            copy.wait_recv()

    _, mean, half_scale, half_shift = normaliser(1, affine[2], affine[3])
    mean2 = jnp.concatenate([mean, mean], axis=1)
    scale2 = jnp.concatenate([half_scale, half_scale], axis=1)
    shift2 = jnp.concatenate([half_shift, half_shift], axis=1)

    def fine_act(x):
        half = (x - mean2) * scale2 + shift2
        return half + half * jnp.tanh(half)

    def conv_fine(g):
        if g in (0, 3):
            f = 0 if g == 0 else 1
            lhs = jnp.concatenate(
                [lf[g, dw : dw + 16, :, k * C : (k + 1) * C] for k in range(4) for dw in range(3)], axis=-1
            ).reshape(16 * 16, 12 * C)
            part = jnp.dot(lhs, w3[f].reshape(12 * C, 2 * C1), preferred_element_type=F32)
            acc3[f] += part.reshape(8, 2, 16, 2 * C1)
        else:
            for a in range(2):
                lhs = jnp.concatenate(
                    [lf[g, dw : dw + 16, :, (a + k) * C : (a + k + 1) * C] for k in range(3) for dw in range(3)], axis=-1
                ).reshape(16 * 16, 9 * C)
                part = jnp.dot(lhs, wp[g - 1].reshape(9 * C, 2 * C1), preferred_element_type=F32)
                part = part.reshape(8, 2, 16, 2 * C1)
                for f in range(2):
                    acc3[f, :, :, :, a * C1 : (a + 1) * C1] += part[..., f * C1 : (f + 1) * C1]

    def finish_fine(f):
        for c in range(16):
            for a in range(2):
                back[pl.ds(f * 512 + a * 16 + c, 16, stride=32), :] = acc3[f, c // 2, c % 2, :, a * C1 : (a + 1) * C1]
        outb[f * 512 : (f + 1) * 512] = back[f * 512 : (f + 1) * 512].astype(BF16)
        leave[f].start()

    leave = [
        pltpu.make_async_copy(outb.at[f * 512 : (f + 1) * 512], out_ref.at[f * 512 : (f + 1) * 512], local_sem.at[57 + f])
        for f in range(2)
    ]

    spread_fine(2)
    lift_before_old(0)
    spread_fine(3)
    lift_before_old(1)
    conv_fine(3)
    spread_fine(0)
    conv_fine(2)
    spread_fine(1)
    conv_fine(1)
    finish_fine(1)
    conv_fine(0)
    finish_fine(0)

    for copy in leave:
        copy.wait()
    for stage in range(2):
        ar_all(1, stage, ar_send).wait()


def local(
    sizes, coarse, cache_coarse, cache_middle, cache_fine, coarse_gain, coarse_shift, fine_gain, fine_shift,
    coarse_kernel, lift_kernel, fine_kernel, skip_kernel,
):
    nt, nh, nw, C, C1 = sizes
    frames, rows, cols, _ = coarse.shape
    assert (frames, rows, cols) == (2, 16, 8)
    peers = 2 * nh + 2 * nw - 2
    hbm = pl.BlockSpec(memory_space=pltpu.HBM)
    V = pltpu.VMEM
    W = min(128, C)
    L = C // W
    scratch = [
        V((4, 1, C), F32),
        V((256, C), BF16), V((256, C), BF16), V((256, C), BF16), V((1024, C), BF16),
        V((L, 256, W), F32), V((L, 1024, W), F32),
        V((4, 12, 16, C), BF16), V((L, 4 * 12 * 16 + 64, W), F32),
        V((2, 4, 2, 16, C), BF16), V((2, 4, 2, 16, C), BF16), V((4, 2, 2, 16, C), F32),
        V((4, 18, 16, 3 * C), BF16), V((2, 12, 16, C), F32),
        V((3, 3, 3, C, C), BF16), V((3, 3, 3, C, C), BF16), V((2, 3, 4 * C, 2 * C), BF16),
        V((2, 4, 3, C, 2 * C1), BF16), V((2, 3, 3, C, 2 * C1), BF16), V((2 * C, 2 * C1), BF16),
        V((2, 12, 16, C), BF16), V((2, 2, 16, C), BF16), V((2, 2, 1, 16, 2 * C), BF16),
        V((6, 12, 16, C), BF16), V((6, 14, 16, 3 * C), BF16), V((2 * L, 256, W), F32),
        V((2, 2, 10, 16, 2 * C), F32), V((2, 4, 10, 16, 2 * C), BF16), V((2, 2, 10, 16, 2 * C), BF16),
        V((4, 18, 16, 4 * C), BF16), V((2, 8, 2, 16, 2 * C1), F32), V((1024, C1), F32), V((1024, C1), BF16),
        V((2, 2, 8, C), F32), V((2, peers, 8, C), F32),
        pltpu.SemaphoreType.DMA((60,)),
        pltpu.SemaphoreType.DMA((2, 2)), pltpu.SemaphoreType.DMA((2, 2)),
        pltpu.SemaphoreType.DMA((24,)), pltpu.SemaphoreType.DMA((24,)),
    ]
    decoded = pl.pallas_call(
        functools.partial(body, sizes),
        out_shape=jax.ShapeDtypeStruct((1024, C1), BF16),
        in_specs=[hbm] * 12,
        out_specs=hbm,
        scratch_shapes=scratch,
        compiler_params=pltpu.CompilerParams(
            collective_id=0, has_side_effects=True, vmem_limit_bytes=63 * 1024 * 1024
        ),
    )(
        coarse.reshape(256, C), cache_coarse.reshape(256, C), cache_middle.reshape(256, C), cache_fine.reshape(1024, C),
        coarse_gain.reshape(1, C), coarse_shift.reshape(1, C), fine_gain.reshape(1, C), fine_shift.reshape(1, C),
        coarse_kernel, lift_kernel, fine_kernel, skip_kernel,
    )
    return decoded.reshape(2, 32, 16, C1)


def solution(mesh):
    def run(*args):
        channels, outer = args[-1].shape
        sizes = (mesh.shape["ta"], mesh.shape["ha"], mesh.shape["wa"], channels, outer)
        return jax.shard_map(
            functools.partial(local, sizes),
            mesh=mesh,
            in_specs=(P("ta", "ha", "wa", None),) + (P(None, "ha", "wa", None),) * 3 + (P(),) * 8,
            out_specs=P("ta", "ha", "wa", None),
            check_vma=False,
        )(*args)

    return run
```

```python
import functools

import jax
import jax.numpy as jnp
from jax import lax
from jax.experimental import pallas as pl
from jax.experimental.pallas import tpu as pltpu
from jax.sharding import PartitionSpec as P

GROUPS = 32
EPS = 1e-06
MESH = pl.DeviceIdType.MESH
F32 = jnp.float32
BF16 = jnp.bfloat16


def rolled(value, shift):
    size = value.shape[0]
    shift = shift % size
    return value if shift == 0 else pltpu.roll(value, shift, 0)


def put(ref, start, value):
    width = ref.shape[-1]
    for part in range(value.shape[1] // width):
        ref[part, pl.ds(start, value.shape[0]), :] = value[:, part * width : (part + 1) * width]


def take(ref, start, stride=1, parts=None):
    at = pl.ds(start, 16) if stride == 1 else pl.ds(start, 16, stride=stride)
    return jnp.concatenate([ref[part, at, :] for part in range(parts or ref.shape[0])], axis=1)


def body(
    sizes,
    coarse_hbm, cache_coarse_hbm, cache_middle_hbm, cache_fine_hbm,
    coarse_gain, coarse_shift, fine_gain, fine_shift,
    coarse_kernel, lift_kernel, fine_kernel, skip_kernel,
    out_ref, affine,
    cb, cbp, cmb, cfb, xf, cff, xt, xtf, ss, sr, saf, act_a, acc1, w1, lk, w2, w3, wp, skw,
    cm, cs, cfs, mt, mid_g, gf, acc2, lt, ltp, lf, acc3, back, outb, ar_src, ar_recv,
    local_sem, ar_send, ar_got, send_sem, recv_sem,
):
    nt, nh, nw, C, C1 = sizes
    half = gf.shape[0] // 2
    ta, ha, wa = lax.axis_index("ta"), lax.axis_index("ha"), lax.axis_index("wa")
    row16 = lax.broadcasted_iota(jnp.int32, (16, C), 0)
    row16w = lax.broadcasted_iota(jnp.int32, (16, 2 * C), 0)
    first_w, last_w, first_h, last_h = wa == 0, wa == nw - 1, ha == 0, ha == nh - 1

    def near(t=0, h=0, w=0):
        where = {}
        if t:
            where["ta"] = lax.rem(ta + (t + nt), nt)
        if h:
            where["ha"] = lax.rem(ha + (h + nh), nh)
        if w:
            where["wa"] = lax.rem(wa + (w + nw), nw)
        return where

    loads = []

    def load(src, dst):
        copy = pltpu.make_async_copy(src, dst, local_sem.at[len(loads)])
        copy.start()
        loads.append(copy)
        return copy

    get_coarse = load(coarse_hbm, cb)
    barrier = pltpu.get_barrier_semaphore()
    y_hi, core = ta // 2, lax.rem(ta, 2)
    by_z = [
        {"ta": 2 * y_hi + lax.rem(core + dc, 2), "ha": lax.rem(ha + dh, nh)}
        for dc in range(2) for dh in range(nh) if dc or dh
    ]
    by_xy = [
        {"ta": 2 * lax.rem(y_hi + dy, 2) + core, "wa": lax.rem(wa + dw, nw)}
        for dy in range(2) for dw in range(nw) if dy or dw
    ]
    stages = ((by_z, 0), (by_xy, len(by_z)))
    friends = by_z + by_xy + [near(t=-1), near(t=-1, w=1), near(t=-1, w=-1), near(t=-1, h=1), near(t=-1, h=-1)]
    for friend in friends:
        pl.semaphore_signal(barrier, inc=1, device_id=friend, device_id_type=MESH)
    get_cc = pltpu.make_async_copy(cache_coarse_hbm, cbp, local_sem.at[59])

    @pl.when(ta == 0)
    def _():
        get_cc.start()

    get_lk = load(lift_kernel, lk)

    def message(index, src, dst, where, leaves=None):
        return pltpu.make_async_remote_copy(
            src_ref=src, dst_ref=dst, send_sem=send_sem.at[index if leaves is None else leaves], recv_sem=recv_sem.at[index],
            device_id=where, device_id_type=MESH,
        )

    center = message(0, coarse_hbm, cbp, near(t=1))
    cols_own = [
        message(1, xt.at[2:4, 8:10], xt.at[2:4, 0:2], near(w=1)),
        message(2, xt.at[2:4, 2:4], xt.at[2:4, 10:12], near(w=-1)),
    ]
    cols_next = [
        message(3, xt.at[2:4, 8:10], xt.at[0:2, 0:2], near(t=1, w=1)),
        message(4, xt.at[2:4, 2:4], xt.at[0:2, 10:12], near(t=1, w=-1)),
    ]
    cols_cached = [
        message(3, xt.at[0:2, 8:10], xt.at[0:2, 0:2], near(w=1), 18),
        message(4, xt.at[0:2, 2:4], xt.at[0:2, 10:12], near(w=-1), 19),
    ]
    rows_own = [
        message(9, ss.at[0, 2:4], sr.at[1, 2:4], near(h=-1)),
        message(10, ss.at[1, 2:4], sr.at[0, 2:4], near(h=1)),
    ]
    rows_next = [
        message(20, ss.at[0, 2:4], sr.at[1, 0:2], near(t=1, h=-1)),
        message(21, ss.at[1, 2:4], sr.at[0, 0:2], near(t=1, h=1)),
    ]
    rows_cached = [
        message(20, ss.at[0, 0:2], sr.at[1, 0:2], near(h=-1), 22),
        message(21, ss.at[1, 0:2], sr.at[0, 0:2], near(h=1), 23),
    ]

    pl.semaphore_wait(barrier, len(friends))

    @pl.when(ta < nt - 1)
    def _():
        center.start()

    def transpose_into(first_frame):
        for f in range(2):
            for c in range(8):
                cells = take(xf, f * 128 + c, 8)
                put(xtf, (first_frame + f) * 192 + (2 + c) * 16, cells)
                xt[first_frame + f, 2 + c] = cells.astype(BF16)

    get_coarse.wait()
    flat = cb[...].astype(F32)
    put(xf, 0, flat)
    transpose_into(2)
    for copy in cols_own:
        copy.start()

    @pl.when(ta < nt - 1)
    def _():
        for copy in cols_next:
            copy.start()

    count = flat.shape[0]
    mean = jnp.sum(flat, axis=0, keepdims=True) / count
    centred = flat - mean
    ar_src[0, 0] = jnp.zeros((8, C), F32)
    ar_src[0, 0, 0:1, :] = mean
    ar_src[0, 0, 1:2, :] = jnp.sum(centred * centred, axis=0, keepdims=True) / count

    def ar_copies(which, stage):
        peers, base = stages[stage]
        return [
            pltpu.make_async_remote_copy(
                src_ref=ar_src.at[which, stage], dst_ref=ar_recv.at[which, base + i],
                send_sem=ar_send.at[which, stage], recv_sem=ar_got.at[which, stage],
                device_id=peer, device_id_type=MESH,
            )
            for i, peer in enumerate(peers)
        ]

    def ar_start(which, stage):
        for copy in ar_copies(which, stage):
            copy.start()

    def ar_all(which, stage, sem):
        peers, base = stages[stage]
        slots = ar_recv.at[which, base : base + len(peers)]
        return pltpu.make_async_copy(slots, slots, sem.at[which, stage])

    def ar_finish(which, stage):
        peers, base = stages[stage]
        n = len(peers) + 1
        ar_all(which, stage, ar_got).wait()
        tiles = [ar_src[which, stage]] + [ar_recv[which, base + i] for i in range(n - 1)]
        average = functools.reduce(jnp.add, tiles) / n
        spread = functools.reduce(jnp.add, [(tile - average) * (tile - average) for tile in tiles]) / n
        rows = lax.broadcasted_iota(jnp.int32, (8, C), 0)
        return average + jnp.where(rows == 1, pltpu.roll(spread, 1, 0), 0.0)

    def ar_next(which, stage):
        ar_src[which, stage + 1] = ar_finish(which, stage)
        ar_start(which, stage + 1)

    size = C // GROUPS
    width = xf.shape[-1]

    def group_mean(value):
        lane_of = lax.broadcasted_iota(jnp.int32, (8, width), 1)
        parts = []
        for part in range(C // width):
            x = jnp.broadcast_to(value[:, part * width : (part + 1) * width], (8, width))
            step = 1
            while step < size:
                x = x + jnp.where((lane_of & step) == 0, pltpu.roll(x, width - step, 1), pltpu.roll(x, step, 1))
                step *= 2
            parts.append(x[0:1])
        return jnp.concatenate(parts, axis=1) / size

    def normaliser(which, gain, shift):
        tile = ar_finish(which, 1)
        mean, variance = tile[0:1], tile[1:2]
        grouped = group_mean(mean)
        away = mean - grouped
        mean, variance = grouped, group_mean(variance + away * away)
        half_scale = 0.5 * (gain * lax.rsqrt(variance + EPS))
        half_shift = 0.5 * shift

        def act(x, mean=mean, half_scale=half_scale, half_shift=half_shift):
            half = (x - mean) * half_scale + half_shift
            return half + half * jnp.tanh(half)

        return act, mean, half_scale, half_shift

    ar_start(0, 0)
    get_cm = load(cache_middle_hbm, cmb)
    get_w1 = load(coarse_kernel, w1)
    get_affine = [load(ref, affine.at[i]) for i, ref in enumerate((coarse_gain, coarse_shift, fine_gain, fine_shift))]
    get_w3 = [
        load(fine_kernel.at[2 * i], w3.at[i, a : a + 3, :, :, a * C1 : (a + 1) * C1]) for i in range(2) for a in range(2)
    ] + [
        load(fine_kernel.at[1 + i - f], wp.at[i, :, :, :, f * C1 : (f + 1) * C1]) for i in range(2) for f in range(2)
    ]
    get_skip = [load(skip_kernel, skw.at[a * C : (a + 1) * C, a * C1 : (a + 1) * C1]) for a in range(2)]
    get_cf = load(cache_fine_hbm, cfb)

    @pl.when(ta == 0)
    def _():
        get_cc.wait()
        put(xf, 0, cbp[...].astype(F32))
        transpose_into(0)
        for copy in cols_cached:
            copy.start()

    cm_first = [
        message(5, cm.at[:, 8:9], cm.at[:, 0:1], near(w=1)),
        message(6, cm.at[:, 1:2], cm.at[:, 9:10], near(w=-1)),
    ]
    cf_first = [
        message(7, lt.at[:, 0:2, 8:9, :, 0:C], lt.at[:, 0:2, 0:1, :, 0:C], near(w=1)),
        message(8, lt.at[:, 0:2, 0:1, :, C : 2 * C], lt.at[:, 0:2, 8:9, :, C : 2 * C], near(w=-1)),
    ]
    cm_second = [
        message(11, cs.at[:, 0:1], cm.at[:, 11:12], near(h=-1)),
        message(12, cs.at[:, 1:2], cm.at[:, 10:11], near(h=1)),
    ]
    cf_second = [
        message(13, cfs.at[0], lt.at[0, 0:2, 9:10], near(h=-1)),
        message(14, cfs.at[1], lt.at[1, 0:2, 9:10], near(h=1)),
    ]

    get_cm.wait()

    @pl.when(ta < 2)
    def _():
        put(xf, 0, cmb[...].astype(F32))
        for f in range(2):
            for c in range(8):
                cm[f, 1 + c] = take(xf, f * 128 + c, 8).astype(BF16)
        for copy in cm_first:
            copy.start()

    def widen(f, slots):
        for c in slots:
            put(xtf, f * 192 + c * 16, xt[f, c].astype(F32))

    def pick_rows(f):
        for side, rows in enumerate(((0, 1), (14, 15))):
            for k, row in enumerate(rows):
                ss[side, f, k] = take(xtf, f * 192 + row, 16).astype(BF16)

    for copy in cols_own:
        copy.wait_recv()
    for f in (2, 3):
        widen(f, (0, 1, 10, 11))
        pick_rows(f)
    for copy in rows_own:
        copy.start()

    @pl.when(ta < nt - 1)
    def _():
        for copy in rows_next:
            copy.start()

    @pl.when(ta == 0)
    def _():
        for copy in cols_cached:
            copy.wait_recv()
        for f in (0, 1):
            widen(f, (0, 1, 10, 11))
            pick_rows(f)
        for copy in rows_cached:
            copy.start()

    def fold(i, carry):
        dt, r = i // (C // 16), pl.multiple_of(lax.rem(i, C // 16) * 16, 16)
        taps = [[lk[dt, dh, dw, pl.ds(r, 16), :].astype(F32) for dw in range(3)] for dh in range(3)]
        for a in range(2):
            for k in range(2):
                if a == 0:
                    line = taps[0] if k == 0 else [taps[1][d] + taps[2][d] for d in range(3)]
                else:
                    line = [taps[0][d] + taps[1][d] for d in range(3)] if k == 0 else taps[2]
                wide = ((line[0] + line[1], line[2]), (line[0], line[1] + line[2]))
                for b in range(2):
                    for j in range(2):
                        w2[a, dt, pl.ds((2 * j + k) * C + r, 16), b * C : (b + 1) * C] = wide[b][j].astype(BF16)
        return carry

    get_lk.wait()
    ar_next(0, 0)
    lax.fori_loop(3 * (C // 32), 3 * (C // 16), fold, 0)

    @pl.when(ta < 2)
    def _():
        for copy in cm_first:
            copy.wait_recv()
        for f in range(2):
            for c in range(10):
                put(gf, 16 * c, cm[f, c].astype(F32))
            cs[f, 0] = take(gf, 0, 16, half).astype(BF16)
            cs[f, 1] = take(gf, 15, 16, half).astype(BF16)
        for copy in cm_second:
            copy.start()

    lax.fori_loop(0, 3 * (C // 32), fold, 0)
    for copy in [get_w1] + get_affine:
        copy.wait()

    for copy in rows_own:
        copy.wait_recv()
    act, *_ = normaliser(0, affine[0], affine[1])

    cols = lax.broadcasted_iota(jnp.int32, (16, C), 0)

    def strips_of(f):
        raw = jnp.logical_and(ta == 0, f < 2)
        for side in range(2):
            outside = first_h if side == 0 else last_h
            for k in range(2):
                x = sr[side, f, k].astype(F32)
                y = jnp.where(raw, x, act(x)) if f < 2 else act(x)
                gone = jnp.logical_or(jnp.logical_and(first_w, cols < 2), jnp.logical_and(last_w, cols >= 10))
                saf[f, side, k] = jnp.where(jnp.logical_or(outside, gone), 0.0, y)

    def act_coarse(f):
        strips_of(f)
        for c in range(12):
            at = f * 192 + c * 16
            x = take(xtf, at)
            x = jnp.where(ta == 0, x, act(x)) if f < 2 else act(x)
            if c < 2:
                x = jnp.where(first_w, 0.0, x)
            if c >= 10:
                x = jnp.where(last_w, 0.0, x)
            put(xtf, at, x)
            above = jnp.where(row16 == 0, saf[f, 0, 1, c : c + 1, :], rolled(x, 1))
            below = jnp.where(row16 == 15, saf[f, 1, 0, c : c + 1, :], rolled(x, -1))
            act_a[f, c, :, 0:C] = above.astype(BF16)
            act_a[f, c, :, C : 2 * C] = x.astype(BF16)
            act_a[f, c, :, 2 * C : 3 * C] = below.astype(BF16)
        top = take(xtf, f * 192, 16)
        bottom = take(xtf, f * 192 + 15, 16)
        for side, lines in enumerate(((saf[f, 0, 0], saf[f, 0, 1], top), (bottom, saf[f, 1, 0], saf[f, 1, 1]))):
            for dw in range(3):
                for dh in range(3):
                    act_a[f, 12 + 2 * dw + side, :, dh * C : (dh + 1) * C] = rolled(lines[dh], -dw).astype(BF16)

    def conv_coarse(f, g):
        lhs = jnp.concatenate(
            [
                jnp.concatenate([act_a[g, dw : dw + 10, :, lanes], act_a[g, 12 + 2 * dw : 14 + 2 * dw, :, lanes]], axis=0)
                for lanes in (slice(0, C), slice(C, 2 * C), slice(2 * C, 3 * C))
                for dw in range(3)
            ],
            axis=-1,
        ).reshape(12 * 16, 9 * C)
        part = jnp.dot(lhs, w1[g - f].reshape(9 * C, C), preferred_element_type=F32).reshape(12, 16, C)
        acc1[f] = part if g == 2 else acc1[f] + part

    def finish_middle(f):
        for c in range(10):
            y = xt[2 + f, 1 + c].astype(F32) + acc1[f, c]
            if c == 0:
                y = jnp.where(first_w, 0.0, y)
            if c == 9:
                y = jnp.where(last_w, 0.0, y)
            mt[4 + f, c] = y.astype(BF16)
        gone = (cols > 9) | (first_w & (cols == 0)) | (last_w & (cols == 9))
        for side in range(2):
            y = rolled(sr[side, 2 + f, 1 - side].astype(F32), -1) + acc1[f, 10 + side]
            y = jnp.where(jnp.logical_or(gone, first_h if side == 0 else last_h), 0.0, y)
            mt[4 + f, 10 + side] = y.astype(BF16)

    to_next = [message(15 + f, mt.at[4 + f : 5 + f], mt.at[2 + f : 3 + f], near(t=1)) for f in range(2)]

    def send_middle(f):
        finish_middle(f)

        @pl.when(ta < nt - 1)
        def _():
            to_next[f].start()

    act_coarse(2)
    act_coarse(3)
    conv_coarse(1, 2)
    conv_coarse(0, 2)
    conv_coarse(1, 3)

    @pl.when(ta > 0)
    def _():
        center.wait_recv()
        put(xf, 0, cbp[...].astype(F32))
        for f in range(2):
            for c in range(8):
                put(xtf, f * 192 + (2 + c) * 16, take(xf, f * 128 + c, 8))
        for copy in cols_next:
            copy.wait_recv()
        for f in (0, 1):
            widen(f, (0, 1, 10, 11))

    for copy in rows_next:
        copy.wait_recv()

    act_coarse(1)
    conv_coarse(1, 1)
    send_middle(1)
    act_coarse(0)
    conv_coarse(0, 1)
    conv_coarse(0, 0)
    send_middle(0)

    to_second = message(17, mt.at[4:6], mt.at[0:2], near(t=2))
    by_second = message(17, mt.at[2:4], mt.at[0:2], near(t=1))

    def prepare(g):
        top = mt[g, 10].astype(F32)
        bottom = mt[g, 11].astype(F32)
        for c in range(10):
            x = mt[g, c].astype(F32)
            put(gf, 16 * c, x)
            mid_g[g, c, :, 0:C] = jnp.where(row16 == 0, top[c : c + 1], rolled(x, 1)).astype(BF16)
            mid_g[g, c, :, C : 2 * C] = mt[g, c]
            mid_g[g, c, :, 2 * C : 3 * C] = jnp.where(row16 == 15, bottom[c : c + 1], rolled(x, -1)).astype(BF16)
        row_top = take(gf, 0, 16, half)
        row_bottom = take(gf, 15, 16, half)
        for j in range(2):
            mid_g[g, 10 + j, :, 0:C] = rolled(row_bottom, -j).astype(BF16)
            mid_g[g, 10 + j, :, C : 2 * C] = rolled(bottom, -j).astype(BF16)
            mid_g[g, 12 + j, :, C : 2 * C] = rolled(top, -j).astype(BF16)
            mid_g[g, 12 + j, :, 2 * C : 3 * C] = rolled(row_top, -j).astype(BF16)

    def lift_part(a, dt, g, frames):
        lanes = slice(a * C, (a + 2) * C)
        lhs = jnp.concatenate(
            [
                jnp.concatenate(
                    [mid_g[g : g + frames, j : j + 9, :, lanes], mid_g[g : g + frames, 10 + 2 * a + j : 11 + 2 * a + j, :, lanes]],
                    axis=1,
                )
                for j in range(2)
            ],
            axis=-1,
        ).reshape(frames * 10 * 16, 4 * C)
        part = jnp.dot(lhs, w2[a, dt], preferred_element_type=F32)
        return part.reshape(frames, 10, 16, 2 * C)

    def cached_middle(at):
        gone = (cols > 9) | (first_w & (cols == 0)) | (last_w & (cols == 9))
        for f in range(2):
            mt[at + f, 1:9] = cm[f, 1:9]
            mt[at + f, 0] = jnp.where(first_w, 0.0, cm[f, 0].astype(F32)).astype(BF16)
            mt[at + f, 9] = jnp.where(last_w, 0.0, cm[f, 9].astype(F32)).astype(BF16)
            for side in range(2):
                outside = jnp.logical_or(gone, first_h if side == 0 else last_h)
                mt[at + f, 10 + side] = jnp.where(outside, 0.0, cm[f, 10 + side].astype(F32)).astype(BF16)

    for copy in get_w3 + get_skip + [get_cf]:
        copy.wait()
    prepare(4)
    prepare(5)
    for a in range(2):
        acc2[a] = lift_part(a, 2, 4, 2)
        acc2[a, 1:2] += lift_part(a, 1, 4, 1)

    for i in range(2):
        for dw in range(3):
            w3[i, 3, dw, :, 0:C1] = jnp.zeros((C, C1), BF16)
            w3[i, 0, dw, :, C1 : 2 * C1] = jnp.zeros((C, C1), BF16)
    skw[0:C, C1 : 2 * C1] = jnp.zeros((C, C1), BF16)
    skw[C : 2 * C, 0:C1] = jnp.zeros((C, C1), BF16)

    @pl.when(ta == 0)
    def _():
        for copy in cm_second:
            copy.wait_recv()
        cached_middle(2)

    @pl.when(ta > 0)
    def _():
        to_next[1].wait_recv()

    prepare(3)
    for a in range(2):
        acc2[a, 0:1] += lift_part(a, 1, 3, 1)
        acc2[a, 1:2] += lift_part(a, 0, 3, 1)

    @pl.when(ta > 0)
    def _():
        to_next[0].wait_recv()

    @pl.when(ta == 2)
    def _():
        by_second.start()

    prepare(2)
    for a in range(2):
        acc2[a, 0:1] += lift_part(a, 0, 2, 1)
        lt[a, 2:4] = acc2[a].astype(BF16)

    @pl.when(ta == 0)
    def _():
        to_second.start()
        put(cff, 0, cfb[...].astype(F32))
        for f in range(2):
            for c in range(16):
                p, b = (c + 1) // 2, (c + 1) % 2
                for a in range(2):
                    lt[a, f, p, :, b * C : (b + 1) * C] = take(cff, f * 512 + a * 16 + c, 32).astype(BF16)
        for copy in cf_first:
            copy.start()

    pivot = jnp.sum(lt[0, 2, 1, :, 0:C].astype(F32), axis=0, keepdims=True) / 16
    sums = jnp.zeros((16, C), F32)
    squares = jnp.zeros((16, C), F32)
    for a in range(2):
        for f in range(2):
            for p in range(9):
                for b in range(2):
                    if (p, b) not in ((0, 0), (8, 1)):
                        x = lt[a, 2 + f, p, :, b * C : (b + 1) * C].astype(F32) - pivot
                        sums = sums + x
                        squares = squares + x * x
    count = 2 * 2 * 16 * 16
    off = jnp.sum(sums, axis=0, keepdims=True) / count
    ar_src[1, 0] = jnp.zeros((8, C), F32)
    ar_src[1, 0, 0:1, :] = pivot + off
    ar_src[1, 0, 1:2, :] = jnp.maximum(jnp.sum(squares, axis=0, keepdims=True) / count - off * off, 0.0)
    ar_start(1, 0)

    def lift_before_new(a):
        acc2[a] = lift_part(a, 2, 2, 2)

    def lift_before_old(a):
        acc2[a] += lift_part(a, 0, 0, 2)
        ltp[a] = (acc2[a] + lift_part(a, 1, 1, 2)).astype(BF16)

    @pl.when(ta > 0)
    def _():
        lift_before_new(0)
        lift_before_new(1)

    @pl.when(ta == 0)
    def _():
        for copy in cf_first:
            copy.wait_recv()
        for f in range(2):
            for a, row in ((0, 0), (1, 15)):
                for p in range(9):
                    put(gf, 16 * p, lt[a, f, p].astype(F32))
                cfs[a, f, 0] = take(gf, row, 16).astype(BF16)
        for copy in cf_second:
            copy.start()

    ar_next(1, 0)

    for b in range(2):
        lhs = jnp.concatenate([lt[a, 2:4, 1 - b : 9 - b, :, b * C : (b + 1) * C] for a in range(2)], axis=-1)
        part = jnp.dot(lhs.reshape(2 * 8 * 16, 2 * C), skw[...], preferred_element_type=F32)
        acc3[:, :, 1 - b] = part.reshape(2, 8, 16, 2 * C1)

    @pl.when(ta == 1)
    def _():
        for copy in cm_second:
            copy.wait_recv()
        cached_middle(0)

    @pl.when(ta > 1)
    def _():
        to_second.wait_recv()

    prepare(0)
    prepare(1)

    for stage in range(2):
        ar_all(0, stage, ar_send).wait()
    for copy in cols_own + rows_own:
        copy.wait_send()

    @pl.when(ta < 2)
    def _():
        for copy in cm_first + cm_second:
            copy.wait_send()

    @pl.when(ta == 0)
    def _():
        for copy in cols_cached + rows_cached + cf_first + cf_second:
            copy.wait_send()

    @pl.when(ta < nt - 1)
    def _():
        for copy in [center] + cols_next + rows_next + to_next:
            copy.wait_send()

    @pl.when(jnp.logical_or(ta == 0, ta == 2))
    def _():
        to_second.wait_send()

    lane = lax.broadcasted_iota(jnp.int32, (16, 2 * C), 1)

    def fine_cells(a, f, p):
        if f < 2:
            return jnp.where(ta == 0, lt[a, f, p].astype(F32), fine_act(ltp[a, f, p].astype(F32)))
        return fine_act(lt[a, f, p].astype(F32))

    def spread_fine(f):
        top = jnp.where(first_h, 0.0, fine_cells(1, f, 9))
        bottom = jnp.where(last_h, 0.0, fine_cells(0, f, 9))
        for p in range(9):
            even = fine_cells(0, f, p)
            odd = fine_cells(1, f, p)
            before = jnp.where(row16w == 0, top[p : p + 1], rolled(odd, 1))
            after = jnp.where(row16w == 15, bottom[p : p + 1], rolled(even, -1))
            for k, part in enumerate((before, even, odd, after)):
                if p == 0:
                    part = jnp.where(first_w & (lane < C), 0.0, part)
                if p == 8:
                    part = jnp.where(last_w & (lane >= C), 0.0, part)
                part = part.astype(BF16)
                for b in range(2):
                    lf[f, 2 * p + b, :, k * C : (k + 1) * C] = part[:, b * C : (b + 1) * C]

    @pl.when(ta == 0)
    def _():
        for copy in cf_second:
            copy.wait_recv()

    _, mean, half_scale, half_shift = normaliser(1, affine[2], affine[3])
    mean2 = jnp.concatenate([mean, mean], axis=1)
    scale2 = jnp.concatenate([half_scale, half_scale], axis=1)
    shift2 = jnp.concatenate([half_shift, half_shift], axis=1)

    def fine_act(x):
        half = (x - mean2) * scale2 + shift2
        return half + half * jnp.tanh(half)

    def conv_fine(g):
        if g in (0, 3):
            f = 0 if g == 0 else 1
            lhs = jnp.concatenate(
                [lf[g, dw : dw + 16, :, k * C : (k + 1) * C] for k in range(4) for dw in range(3)], axis=-1
            ).reshape(16 * 16, 12 * C)
            part = jnp.dot(lhs, w3[f].reshape(12 * C, 2 * C1), preferred_element_type=F32)
            acc3[f] += part.reshape(8, 2, 16, 2 * C1)
        else:
            for a in range(2):
                lhs = jnp.concatenate(
                    [lf[g, dw : dw + 16, :, (a + k) * C : (a + k + 1) * C] for k in range(3) for dw in range(3)], axis=-1
                ).reshape(16 * 16, 9 * C)
                part = jnp.dot(lhs, wp[g - 1].reshape(9 * C, 2 * C1), preferred_element_type=F32)
                part = part.reshape(8, 2, 16, 2 * C1)
                for f in range(2):
                    acc3[f, :, :, :, a * C1 : (a + 1) * C1] += part[..., f * C1 : (f + 1) * C1]

    def finish_fine(f):
        for c in range(16):
            for a in range(2):
                back[pl.ds(f * 512 + a * 16 + c, 16, stride=32), :] = acc3[f, c // 2, c % 2, :, a * C1 : (a + 1) * C1]
        outb[f * 512 : (f + 1) * 512] = back[f * 512 : (f + 1) * 512].astype(BF16)
        leave[f].start()

    leave = [
        pltpu.make_async_copy(outb.at[f * 512 : (f + 1) * 512], out_ref.at[f * 512 : (f + 1) * 512], local_sem.at[57 + f])
        for f in range(2)
    ]

    spread_fine(2)
    lift_before_old(0)
    spread_fine(3)
    lift_before_old(1)
    conv_fine(3)
    spread_fine(0)
    conv_fine(2)
    spread_fine(1)
    conv_fine(1)
    finish_fine(1)
    conv_fine(0)
    finish_fine(0)

    for copy in leave:
        copy.wait()
    for stage in range(2):
        ar_all(1, stage, ar_send).wait()


def local(
    sizes, coarse, cache_coarse, cache_middle, cache_fine, coarse_gain, coarse_shift, fine_gain, fine_shift,
    coarse_kernel, lift_kernel, fine_kernel, skip_kernel,
):
    nt, nh, nw, C, C1 = sizes
    frames, rows, cols, _ = coarse.shape
    assert (frames, rows, cols) == (2, 16, 8)
    peers = 2 * nh + 2 * nw - 2
    hbm = pl.BlockSpec(memory_space=pltpu.HBM)
    V = pltpu.VMEM
    W = min(128, C)
    L = C // W
    scratch = [
        V((4, 1, C), F32),
        V((256, C), BF16), V((256, C), BF16), V((256, C), BF16), V((1024, C), BF16),
        V((L, 256, W), F32), V((L, 1024, W), F32),
        V((4, 12, 16, C), BF16), V((L, 4 * 12 * 16 + 64, W), F32),
        V((2, 4, 2, 16, C), BF16), V((2, 4, 2, 16, C), BF16), V((4, 2, 2, 16, C), F32),
        V((4, 18, 16, 3 * C), BF16), V((2, 12, 16, C), F32),
        V((3, 3, 3, C, C), BF16), V((3, 3, 3, C, C), BF16), V((2, 3, 4 * C, 2 * C), BF16),
        V((2, 4, 3, C, 2 * C1), BF16), V((2, 3, 3, C, 2 * C1), BF16), V((2 * C, 2 * C1), BF16),
        V((2, 12, 16, C), BF16), V((2, 2, 16, C), BF16), V((2, 2, 1, 16, 2 * C), BF16),
        V((6, 12, 16, C), BF16), V((6, 14, 16, 3 * C), BF16), V((2 * L, 256, W), F32),
        V((2, 2, 10, 16, 2 * C), F32), V((2, 4, 10, 16, 2 * C), BF16), V((2, 2, 10, 16, 2 * C), BF16),
        V((4, 18, 16, 4 * C), BF16), V((2, 8, 2, 16, 2 * C1), F32), V((1024, C1), F32), V((1024, C1), BF16),
        V((2, 2, 8, C), F32), V((2, peers, 8, C), F32),
        pltpu.SemaphoreType.DMA((60,)),
        pltpu.SemaphoreType.DMA((2, 2)), pltpu.SemaphoreType.DMA((2, 2)),
        pltpu.SemaphoreType.DMA((24,)), pltpu.SemaphoreType.DMA((24,)),
    ]
    decoded = pl.pallas_call(
        functools.partial(body, sizes),
        out_shape=jax.ShapeDtypeStruct((1024, C1), BF16),
        in_specs=[hbm] * 12,
        out_specs=hbm,
        scratch_shapes=scratch,
        compiler_params=pltpu.CompilerParams(
            collective_id=0, has_side_effects=True, vmem_limit_bytes=63 * 1024 * 1024
        ),
    )(
        coarse.reshape(256, C), cache_coarse.reshape(256, C), cache_middle.reshape(256, C), cache_fine.reshape(1024, C),
        coarse_gain.reshape(1, C), coarse_shift.reshape(1, C), fine_gain.reshape(1, C), fine_shift.reshape(1, C),
        coarse_kernel, lift_kernel, fine_kernel, skip_kernel,
    )
    return decoded.reshape(2, 32, 16, C1)


def solution(mesh):
    def run(*args):
        channels, outer = args[-1].shape
        sizes = (mesh.shape["ta"], mesh.shape["ha"], mesh.shape["wa"], channels, outer)
        return jax.shard_map(
            functools.partial(local, sizes),
            mesh=mesh,
            in_specs=(P("ta", "ha", "wa", None),) + (P(None, "ha", "wa", None),) * 3 + (P(),) * 8,
            out_specs=P("ta", "ha", "wa", None),
            check_vma=False,
        )(*args)

    return run
```
